32 devices in a mesh: dp: 16 (over z, y, x), section: 2 (over core).
Axes of the slice: x: 2, y: 2, z: 4, core: 2. Of those that a mesh axis runs over, the one named last changes fastest.
Arguments:
- patches: bfloat16 [8192, 768], P('dp'), may hold values from -4 to 4
- recon_cot: bfloat16 [8192, 768], P('dp'), may hold values from -6 to 6
- lengths: int32 [32, 4], P('dp'), may hold values from 1 to 128, 256 in all within a row
- codebook: bfloat16 [4096, 768], P(('dp', 'section')), may hold values from -4 to 4
- w_qkv: bfloat16 [2, 768, 2304], P('section'), may hold values from -0.21875 to 0.21875
- w_out: bfloat16 [2, 768, 768], P('section'), may hold values from -0.625 to 0.625
- w_up: bfloat16 [2, 768, 3072], P('section'), may hold values from -0.21875 to 0.21875
- w_down: bfloat16 [2, 3072, 768], P('section'), may hold values from -0.109375 to 0.109375
- norm_gain: float32 [2, 2, 768], P('section'), may hold values from 0.1 to 1.9
- norm_bias: float32 [2, 2, 768], P('section'), may hold values from -3 to 3
- bias_out: float32 [2, 2, 768], P('section'), may hold values from -3 to 3
- bias_up: float32 [2, 3072], P('section'), may hold values from -3 to 3
Outputs:
- ends: float32 [2, 8192, 768], P('section', 'dp')
- codes: float32 [8192], P('dp')
- grad_qkv: float32 [2, 768, 2304], P('section', 'dp')
- grad_out: float32 [2, 768, 768], P('section', 'dp')
- grad_up: float32 [2, 768, 3072], P('section', 'dp')
- grad_down: float32 [2, 3072, 768], P('section', 'dp')
- grad_gain: float32 [2, 2, 768], P('section', None, 'dp')
- grad_nbias: float32 [2, 2, 768], P('section', None, 'dp')
- grad_bout: float32 [2, 2, 768], P('section', None, 'dp')
- grad_bup: float32 [2, 3072], P('section', 'dp')
The draws below stay inside these ranges and needn't reach their ends.
Inputs may be any that keep to these rules, and one draw needn't show every extreme that they name: In each row the 4 image lengths sum to 256, and the largest is exactly half of 256.
All inputs are finite; a program needn't handle non-finite values.
Results may differ from the reference program's by a relative error of at most 0.025.
Values may be sent and summed in bfloat16 or wider, within the bound.
No kernel may reach another device: no remote copies, remote signals or barrier semaphores. Data moves between devices by JAX's collectives and lax.ppermute only.
A program may use at most 256 MiB of HBM per device.

```python
import math
import jax
import jax.numpy as jnp
import numpy as np
from jax import lax

D = 768
HEADS = 12
HD = 64
FF = 3072
ROWS = 256
SLOTS = 4
VOCAB = 4096
BLOCKS = 32
TOKENS = 8192


def draw_patches(key, part):
    key = jax.random.fold_in(key, 11)
    return jax.random.truncated_normal(key, -4.0, 4.0, (TOKENS, D), jnp.float32).astype(jnp.bfloat16)


def draw_codebook(key, part):
    key = jax.random.fold_in(key, 23)
    return jax.random.truncated_normal(key, -4.0, 4.0, (VOCAB, D), jnp.float32).astype(jnp.bfloat16)


def block_scale(stream_key, shape, pieces, smallest, top_value):
    def one(position, blocks):
        heights = jax.random.uniform(jax.random.fold_in(jax.random.fold_in(stream_key, 6), position), (blocks,), jnp.float32, smallest / len(pieces), top_value / len(pieces))
        return jnp.repeat(jnp.exp(heights), shape[position] // blocks).reshape((-1,) + (1,) * (len(shape) - position - 1))

    factor_of = one(*pieces[0])
    for cut in pieces[1:]:
        factor_of = factor_of * one(*cut)
    return factor_of


def split_up(number_of, total, most, skew):
    weights = [(1 << 20) // math.isqrt(standing ** skew) + 1 for standing in range(2, number_of + 1)]
    spare, holding = total - most - (number_of - 1), [1] * (number_of - 1)
    while spare > 0:
        movable = [i for i in range(number_of - 1) if holding[i] < most]
        pool, budget = sum([weights[i] for i in movable]), spare
        for i in movable:
            addition = min(most - holding[i], max(1, budget * weights[i] // pool), spare)
            holding[i] = holding[i] + addition
            spare = spare - addition
    return np.array([most] + holding)


def uneven(rng, count, total, bound, lean):
    if count == 2:
        one = jax.random.randint(rng, (), max(1, total - bound), min(bound, total - 1) + 1)
        return jnp.stack([one, total - one])
    sizes = jnp.asarray(split_up(count, total, bound, lean), jnp.int32)
    twos = (count - 1) // 2
    source_of, receiver = sizes[1:1 + 2 * twos:2], sizes[2:2 + 2 * twos:2]
    slack = jnp.minimum(source_of - 1, bound - receiver)
    moved = jax.random.randint(jax.random.fold_in(rng, 1), (twos,), 0, 1 << 20) % (slack + 1)
    sizes = sizes.at[1:1 + 2 * twos:2].set(source_of - moved).at[2:2 + 2 * twos:2].set(receiver + moved)
    return sizes[jax.random.permutation(jax.random.fold_in(rng, 2), count)]


def centred(rng, extent, width, reach, cuts=(), kind=jnp.bfloat16):
    values = jax.random.normal(rng, extent, jnp.float32) * width
    if len(cuts) > 0:
        values = block_scale(rng, extent, cuts, -0.22, 0.18) * values
    return jnp.clip(values, min=-reach, max=reach).astype(kind)


def setup_inputs(seed: int = 0) -> dict:
    keys = jax.random.split(jax.random.key(seed), 13)
    patches = draw_patches(jax.random.fold_in(keys[12], 71), 0)
    recon_cot = centred(keys[1], (TOKENS, D), 1.0, 6.0, ((0, 16),))
    lengths = jax.vmap(lambda own: uneven(own, SLOTS, ROWS, ROWS // 2, 2))(jax.random.split(keys[2], BLOCKS)).reshape((BLOCKS, SLOTS)).astype(jnp.int32)
    codebook = draw_codebook(jax.random.fold_in(keys[12], 71), 0)
    w_qkv = centred(keys[4], (2, D, 3 * D), D ** -0.5, 0.21875, ((0, 2),))
    w_out = centred(keys[5], (2, D, D), (D // 8) ** -0.5, 0.625, ((0, 2),))
    w_up = centred(keys[6], (2, D, FF), D ** -0.5, 0.21875, ((0, 2),))
    w_down = centred(keys[7], (2, FF, D), FF ** -0.5, 0.109375, ((0, 2),))
    norm_gain = jnp.clip(1.0 + 0.18 * jax.random.normal(keys[8], (2, 2, D), jnp.float32), 0.1, 1.9)
    norm_bias = centred(keys[9], (2, 2, D), 0.3, 3.0, ((0, 2),), jnp.float32)
    bias_out = centred(keys[10], (2, 2, D), 0.3, 3.0, ((0, 2),), jnp.float32)
    bias_up = centred(keys[11], (2, FF), 0.3, 3.0, ((0, 2),), jnp.float32)
    return {"patches": patches, "recon_cot": recon_cot, "lengths": lengths, "codebook": codebook, "w_qkv": w_qkv, "w_out": w_out, "w_up": w_up, "w_down": w_down, "norm_gain": norm_gain, "norm_bias": norm_bias, "bias_out": bias_out, "bias_up": bias_up}


EPS = 1e-06
MASKED = -1e+30
HIGH = lax.Precision.HIGHEST

@jax.custom_vjp
def low(v):
    return lax.optimization_barrier(v.astype(jnp.bfloat16)).astype(jnp.float32)

@jax.custom_vjp
def low_back(v):
    return v

def low_keep(v):
    return (low(v), None)

def low_pass(kept, grad):
    return (grad,)

def back_keep(v):
    return (v, None)

def back_low(kept, grad):
    return (low(grad),)
low.defvjp(low_keep, low_pass)
low_back.defvjp(back_keep, back_low)

def image_mask(image_lens, row_count):
    limits = jnp.cumsum(image_lens)
    positions = jnp.arange(row_count, dtype=jnp.int32)
    idents = lax.optimization_barrier(jnp.sum((positions[:, None] >= limits[None, :]).astype(jnp.int32), axis=1))
    return idents[:, None] == idents[None, :]

def layer_norm(values, gains, shifts):
    centre = values - lax.optimization_barrier(jnp.mean(values, axis=-1, keepdims=True))
    spread = lax.optimization_barrier(jnp.mean(centre * centre, axis=-1, keepdims=True))
    return centre * lax.rsqrt(spread + EPS) * gains + shifts

def vit_block(inputs, same, params):
    w_qkv, w_out, w_up, w_down, gains, shifts, bias_out, bias_up = params
    row_count = inputs.shape[0]
    normed = low(layer_norm(inputs, gains[0], shifts[0]))
    packed = low(low_back(jnp.dot(normed, w_qkv, precision=HIGH)))
    heads = packed.reshape(row_count, 3, HEADS, HD)
    scores = low_back(jnp.einsum('qhd,khd->hqk', heads[:, 0], heads[:, 1], precision=HIGH) * HD ** (-0.5))
    scores = jnp.where(same[None], scores, MASKED)
    highest = lax.optimization_barrier(jnp.max(scores, axis=-1, keepdims=True))
    powers = jnp.exp(scores - highest)
    att_probs = low(powers / lax.optimization_barrier(jnp.sum(powers, axis=-1, keepdims=True)))
    mixed_heads = jnp.einsum('hqk,khd->qhd', att_probs, heads[:, 2], precision=HIGH)
    mixed_heads = low(low_back(mixed_heads.reshape(row_count, HEADS * HD)))
    residual = inputs + low_back(jnp.dot(mixed_heads, w_out, precision=HIGH)) + bias_out[0]
    normed_two = low(layer_norm(residual, gains[1], shifts[1]))
    pre_act = low_back(jnp.dot(normed_two, w_up, precision=HIGH) + bias_up)
    active = low(jax.nn.gelu(pre_act, approximate=False))
    return residual + low_back(jnp.dot(active, w_down, precision=HIGH)) + bias_out[1]

def quantize(hidden, table):
    hidden_low = low(hidden)
    scores = low_back(jnp.dot(hidden_low, table.T, precision=HIGH) * D ** (-0.5))
    highest = lax.optimization_barrier(jnp.max(scores, axis=-1, keepdims=True))
    log_total = highest + jnp.log(lax.optimization_barrier(jnp.sum(jnp.exp(scores - highest), axis=-1, keepdims=True)))
    code_probs = jnp.exp(scores - log_total)
    mean_code = low_back(jnp.dot(code_probs, table, precision=HIGH))
    unit_code = mean_code * lax.rsqrt(lax.optimization_barrier(jnp.mean(mean_code * mean_code, axis=-1, keepdims=True)) + EPS)
    return (unit_code, log_total[:, 0])

def reference(patches, recon_cot, lengths, codebook, w_qkv, w_out, w_up, w_down, norm_gain, norm_bias, bias_out, bias_up):
    table = codebook.astype(jnp.float32)
    start_values = (patches.astype(jnp.float32), w_qkv.astype(jnp.float32), w_out.astype(jnp.float32), w_up.astype(jnp.float32), w_down.astype(jnp.float32), norm_gain, norm_bias, bias_out, bias_up)

    def whole(patch_rows, wqkv_all, wout_all, wup_all, wdown_all, gain_all, shift_all, bout_all, bup_all):
        encoder = (wqkv_all[0], wout_all[0], wup_all[0], wdown_all[0], gain_all[0], shift_all[0], bout_all[0], bup_all[0])
        decoder = (wqkv_all[1], wout_all[1], wup_all[1], wdown_all[1], gain_all[1], shift_all[1], bout_all[1], bup_all[1])

        def one_block(running, item):
            block_rows, image_lens = item
            same = image_mask(image_lens, ROWS)
            hidden = vit_block(block_rows, same, encoder)
            unit_code, log_total = quantize(hidden, table)
            return (running, (vit_block(unit_code, same, decoder), log_total))
        _, (recon, log_totals) = lax.scan(jax.checkpoint(one_block), None, (patch_rows.reshape(BLOCKS, ROWS, D), lengths))
        return (recon.reshape(TOKENS, D), log_totals.reshape(TOKENS))
    (recon, codes), pull_back = jax.vjp(whole, *start_values)
    grads = pull_back((recon_cot.astype(jnp.float32), jnp.zeros_like(codes)))
    ends = jnp.stack([grads[0], recon])
    return (ends, codes, grads[1], grads[2], grads[3], grads[4], grads[5], grads[6], grads[7], grads[8])
```

```python
from functools import partial

import jax
import jax.numpy as jnp
from jax import lax
from jax.sharding import PartitionSpec as P

D = 768
HEADS = 12
HD = 64


EPS = 1e-06
MASKED = -1e30


def image_mask(image_lens, row_count):
    limits = jnp.cumsum(image_lens)
    positions = jnp.arange(row_count, dtype=jnp.int32)
    idents = jnp.sum((positions[:, None] >= limits[None, :]).astype(jnp.int32), axis=1)
    return idents[:, None] == idents[None, :]


def norm_parts(values, gains, shifts):
    centre = values - jnp.mean(values, axis=-1, keepdims=True)
    inverse = lax.rsqrt(jnp.mean(centre * centre, axis=-1, keepdims=True) + EPS)
    unit_rows = centre * inverse
    return (unit_rows * gains + shifts, unit_rows, inverse)


def norm_back(grad_rows, unit_rows, inverse, gains):
    scaled = grad_rows * gains
    return inverse * (
        scaled
        - jnp.mean(scaled, axis=-1, keepdims=True)
        - unit_rows * jnp.mean(scaled * unit_rows, axis=-1, keepdims=True)
    )


def head_scores(query_heads, key_heads, same):
    scores = jnp.einsum(
        "bqhd,bkhd->bhqk", query_heads, key_heads, preferred_element_type=jnp.float32
    ) * HD ** (-0.5)
    return jnp.where(same[:, None], scores, MASKED)


def block_forward(inputs, same, weights):
    w_qkv, w_out, w_up, w_down, gains, shifts, bias_out, bias_up = weights
    row_count = inputs.shape[0]
    normed, unit_one, inv_one = norm_parts(inputs, gains[0], shifts[0])
    normed_low = normed.astype(jnp.bfloat16)
    packed = jnp.dot(normed_low, w_qkv, preferred_element_type=jnp.float32).astype(jnp.bfloat16)
    heads = packed.reshape(same.shape[0], -1, 3, HEADS, HD)
    scores = head_scores(heads[:, :, 0], heads[:, :, 1], same)
    highest = jnp.max(scores, axis=-1, keepdims=True)
    powers = jnp.exp(scores - highest)
    totals = jnp.sum(powers, axis=-1, keepdims=True)
    att_probs = powers / totals
    log_total = highest + jnp.log(totals)
    mixed_heads = jnp.einsum(
        "bhqk,bkhd->bqhd",
        att_probs.astype(jnp.bfloat16),
        heads[:, :, 2],
        preferred_element_type=jnp.float32,
    )
    mixed_heads = mixed_heads.reshape(row_count, HEADS * HD).astype(jnp.bfloat16)
    residual = (
        inputs + jnp.dot(mixed_heads, w_out, preferred_element_type=jnp.float32) + bias_out[0]
    )
    normed_two, unit_two, inv_two = norm_parts(residual, gains[1], shifts[1])
    normed_two_low = normed_two.astype(jnp.bfloat16)
    pre_act = jnp.dot(normed_two_low, w_up, preferred_element_type=jnp.float32) + bias_up
    active = jax.nn.gelu(pre_act, approximate=False).astype(jnp.bfloat16)
    output = residual + jnp.dot(active, w_down, preferred_element_type=jnp.float32) + bias_out[1]
    kept_state = (
        unit_one,
        inv_one,
        normed_low,
        packed,
        log_total,
        mixed_heads,
        unit_two,
        inv_two,
        normed_two_low,
        pre_act,
        active,
    )
    return (output, kept_state)


def block_backward(grad_rows, kept_state, same, weights):
    w_qkv, w_out, w_up, w_down, gains, shifts, bias_out, bias_up = weights
    (
        unit_one,
        inv_one,
        normed_low,
        packed,
        log_total,
        mixed_heads,
        unit_two,
        inv_two,
        normed_two_low,
        pre_act,
        active,
    ) = kept_state
    row_count = grad_rows.shape[0]
    grad_low = grad_rows.astype(jnp.bfloat16)
    grad_down = jnp.einsum("rf,rd->fd", active, grad_low, preferred_element_type=jnp.float32)
    d_active = jnp.einsum("rd,fd->rf", grad_low, w_down, preferred_element_type=jnp.float32)
    _, gelu_pull = jax.vjp(partial(jax.nn.gelu, approximate=False), pre_act)
    d_pre = gelu_pull(d_active)[0].astype(jnp.bfloat16)
    grad_up = jnp.einsum("rd,rf->df", normed_two_low, d_pre, preferred_element_type=jnp.float32)
    grad_bias_up = jnp.sum(d_pre.astype(jnp.float32), axis=0)
    d_normed_two = jnp.einsum("rf,df->rd", d_pre, w_up, preferred_element_type=jnp.float32)
    gain_two = jnp.sum(d_normed_two * unit_two, axis=0)
    shift_two = jnp.sum(d_normed_two, axis=0)
    grad_resid = grad_rows + norm_back(d_normed_two, unit_two, inv_two, gains[1])
    resid_low = grad_resid.astype(jnp.bfloat16)
    grad_outw = jnp.einsum("re,rd->ed", mixed_heads, resid_low, preferred_element_type=jnp.float32)
    d_mixed = jnp.einsum("rd,ed->re", resid_low, w_out, preferred_element_type=jnp.float32)
    d_mixed = d_mixed.astype(jnp.bfloat16).reshape(same.shape[0], -1, HEADS, HD)
    heads = packed.reshape(same.shape[0], -1, 3, HEADS, HD)
    query_heads = heads[:, :, 0]
    key_heads = heads[:, :, 1]
    value_heads = heads[:, :, 2]
    att_probs = jnp.exp(head_scores(query_heads, key_heads, same) - log_total)
    d_probs = jnp.einsum("bqhd,bkhd->bhqk", d_mixed, value_heads, preferred_element_type=jnp.float32)
    d_value = jnp.einsum(
        "bhqk,bqhd->bkhd", att_probs.astype(jnp.bfloat16), d_mixed, preferred_element_type=jnp.float32
    )
    d_scores = att_probs * (d_probs - jnp.sum(d_probs * att_probs, axis=-1, keepdims=True))
    d_scores = d_scores.astype(jnp.bfloat16)
    d_query = jnp.einsum(
        "bhqk,bkhd->bqhd", d_scores, key_heads, preferred_element_type=jnp.float32
    ) * HD ** (-0.5)
    d_key = jnp.einsum(
        "bhqk,bqhd->bkhd", d_scores, query_heads, preferred_element_type=jnp.float32
    ) * HD ** (-0.5)
    d_packed = jnp.stack((d_query, d_key, d_value), axis=2).reshape(row_count, 3 * HEADS * HD)
    d_packed = d_packed.astype(jnp.bfloat16)
    grad_qkvw = jnp.einsum("rd,re->de", normed_low, d_packed, preferred_element_type=jnp.float32)
    d_normed = jnp.einsum("re,de->rd", d_packed, w_qkv, preferred_element_type=jnp.float32)
    gain_one = jnp.sum(d_normed * unit_one, axis=0)
    shift_one = jnp.sum(d_normed, axis=0)
    grad_input = grad_resid + norm_back(d_normed, unit_one, inv_one, gains[0])
    grad_parts = (
        grad_qkvw,
        grad_outw,
        grad_up,
        grad_down,
        jnp.stack((gain_one, gain_two)),
        jnp.stack((shift_one, shift_two)),
        jnp.stack((jnp.sum(grad_resid, axis=0), jnp.sum(grad_rows, axis=0))),
        grad_bias_up,
    )
    return (grad_input, grad_parts)


def merge_soft(left_part, right_part):
    highest = jnp.maximum(left_part[0], right_part[0])
    left_factor = jnp.exp(left_part[0] - highest)
    right_factor = jnp.exp(right_part[0] - highest)
    return (
        highest,
        left_part[1] * left_factor + right_part[1] * right_factor,
        left_part[2] * left_factor + right_part[2] * right_factor,
    )


def swapped(value):
    return lax.ppermute(value, "section", [(0, 1), (1, 0)])


def bit_count(size):
    count = size.bit_length() - 1
    return count if size == 1 << count else None


def pick(value, which, axis):
    return lax.dynamic_index_in_dim(value, which, axis, keepdims=False)


def total(terms):
    summed = terms[0].astype(jnp.float32)
    for term in terms[1:]:
        summed = summed + term.astype(jnp.float32)
    return summed


def scatter_sum(rows, order, section):
    size = lax.axis_size("dp")
    count = bit_count(size)
    me = lax.axis_index("dp")
    live = list(range(count))[::-1]
    terms = [rows.reshape((2,) * count + (rows.shape[0] // size,) + rows.shape[1:])]
    for bit in order:
        axis = live.index(bit)
        mine = (me >> bit) & 1
        sent = total([pick(term, 1 - mine, axis) for term in terms]).astype(jnp.bfloat16)
        route = [(2 * i + section, 2 * (i ^ (1 << bit)) + section) for i in range(size)]
        got = lax.ppermute(sent, ("dp", "section"), route)
        terms = [pick(term, mine, axis) for term in terms] + [got]
        live.remove(bit)
    return total(terms)


def gathered(rows):
    size = lax.axis_size("dp")
    count = bit_count(size)
    far = list(range(2, count))
    near = list(range(min(count, 2)))
    half = rows.shape[0] // 2
    out = []
    for piece, order in ((rows[:half], far + near), (rows[half:], far + near[::-1])):
        for bit in order:
            got = lax.ppermute(piece, "dp", [(i, i ^ (1 << bit)) for i in range(size)])
            piece = jnp.concatenate([piece, got])
        out.append(piece)
    return jnp.concatenate(out)


def per_device(
    patches,
    recon_cot,
    lengths,
    codebook,
    w_qkv,
    w_out,
    w_up,
    w_down,
    norm_gain,
    norm_bias,
    bias_out,
    bias_up,
):
    on_first = lax.axis_index("section") == 0
    micro_count = lengths.shape[0]
    row_count = patches.shape[0] // micro_count
    score_scale = D ** (-0.5)
    weights = (
        w_qkv[0],
        w_out[0],
        w_up[0],
        w_down[0],
        norm_gain[0],
        norm_bias[0],
        bias_out[0],
        bias_up[0],
    )
    table = gathered(codebook)
    masks = jax.vmap(partial(image_mask, row_count=row_count))(lengths)
    output, enc_state = block_forward(patches.astype(jnp.float32), masks, weights)
    sent_rows = output.astype(jnp.bfloat16)
    received = lax.ppermute(sent_rows, "section", [(0, 1)])
    hidden_low = jnp.where(on_first, sent_rows, received)
    scores = (
        jnp.einsum("rd,vd->rv", hidden_low, table, preferred_element_type=jnp.float32) * score_scale
    )
    highest = jnp.max(scores, axis=-1, keepdims=True)
    powers = jnp.exp(scores - highest)
    totals = jnp.sum(powers, axis=-1, keepdims=True)
    high_part = powers.astype(jnp.bfloat16)
    low_part = (powers - high_part.astype(jnp.float32)).astype(jnp.bfloat16)
    summed = jnp.dot(high_part, table, preferred_element_type=jnp.float32) + jnp.dot(
        low_part, table, preferred_element_type=jnp.float32
    )
    parts = (highest, totals, summed)
    parts = merge_soft(parts, jax.tree.map(swapped, parts))
    highest, totals, summed = parts
    log_total = highest + jnp.log(totals)
    mean_code = summed / totals
    inverse = lax.rsqrt(jnp.mean(mean_code * mean_code, axis=-1, keepdims=True) + EPS)
    unit_code = mean_code * inverse
    recon, dec_state = block_forward(unit_code, masks, weights)
    grad_unit, dec_parts = block_backward(recon_cot.astype(jnp.float32), dec_state, masks, weights)
    orders = orders_of_bits()
    dec_sums = [
        scatter_sum(part.astype(jnp.bfloat16), order, 1) for part, order in zip(dec_parts[:4], orders)
    ]
    grad_code = inverse * (
        grad_unit - unit_code * jnp.mean(grad_unit * unit_code, axis=-1, keepdims=True)
    )
    own_low = grad_code.astype(jnp.bfloat16)
    got_low = lax.ppermute(own_low, "section", [(1, 0)])
    code_grad_low = jnp.where(on_first, got_low, own_low)
    inner_prod = jnp.sum(code_grad_low.astype(jnp.float32) * mean_code, axis=-1, keepdims=True)
    code_probs = jnp.exp(scores - log_total)
    d_probs = jnp.einsum("rd,vd->rv", code_grad_low, table, preferred_element_type=jnp.float32)
    d_scores = (code_probs * (d_probs - inner_prod)).astype(jnp.bfloat16)
    half_grad = jnp.dot(d_scores, table, preferred_element_type=jnp.float32) * score_scale
    other_half = lax.ppermute(half_grad, "section", [(1, 0)])
    grad_patches, enc_parts = block_backward(half_grad + other_half, enc_state, masks, weights)
    enc_sums = [
        scatter_sum(part.astype(jnp.bfloat16), order, 0) for part, order in zip(enc_parts[:4], orders)
    ]
    size = lax.axis_size("dp")
    small = [jnp.where(on_first, enc, dec) for enc, dec in zip(enc_parts[4:], dec_parts[4:])]
    rows = [part.reshape(2, size, -1).swapaxes(0, 1).reshape(size, -1) for part in small[:3]]
    rows = jnp.concatenate(rows + [small[3].reshape(size, -1)], axis=1)
    share = lax.psum_scatter(rows, "dp", scatter_dimension=0, tiled=True)[0]
    width = D // size
    sums = [jnp.where(on_first, enc, dec)[None] for enc, dec in zip(enc_sums, dec_sums)]
    small_sums = [share[2 * width * i : 2 * width * (i + 1)].reshape(1, 2, width) for i in range(3)]
    ends = jnp.where(on_first, grad_patches, recon)[None]
    return (ends, log_total[:, 0], *sums, *small_sums, share[None, 6 * width :])


def orders_of_bits():
    bits = list(range(bit_count(lax.axis_size("dp"))))
    other = bits[:2][::-1] + bits[2:]
    return [bits, other, other, bits]


def solution(mesh):
    placed = (
        P("dp", None),
        P("dp", None),
        P("dp", None),
        P(("dp", "section"), None),
        P("section", None, None),
        P("section", None, None),
        P("section", None, None),
        P("section", None, None),
        P("section", None, None),
        P("section", None, None),
        P("section", None, None),
        P("section", None),
    )
    return jax.shard_map(
        per_device,
        mesh=mesh,
        in_specs=placed,
        out_specs=(
            P("section", "dp", None),
            P("dp"),
            P("section", "dp", None),
            P("section", "dp", None),
            P("section", "dp", None),
            P("section", "dp", None),
            P("section", None, "dp"),
            P("section", None, "dp"),
            P("section", None, "dp"),
            P("section", "dp"),
        ),
        check_vma=False,
    )
```

```python
from functools import partial

import jax
import jax.numpy as jnp
from jax import lax
from jax.experimental import pallas as pl
from jax.experimental.pallas import tpu as pltpu
from jax.sharding import PartitionSpec as P

D = 768
HEADS = 12
HD = 64
FF = 3072
ROWS = 256
PAIR = 2 * HD
EPS = 1e-06
MASKED = -1e30
F32 = jnp.float32
BF16 = jnp.bfloat16
ACT, N2, N1, MIX, FACTS = 0, FF, FF + D, FF + 2 * D, FF + 3 * D
TAIL_P = 0.35
TAIL = (0.19620077326315646, 0.2185939781557991, 0.05480664657447366, 0.5651487076988272,
        -0.5574354264567037, 0.7060774515721405, -0.18339209581143395)
VMEM = pl.BlockSpec(memory_space=pltpu.VMEM)
SMEM = pl.BlockSpec(memory_space=pltpu.SMEM)
ANY = pl.BlockSpec(memory_space=pl.ANY)
ROOM = 60 * 1024 * 1024


def dot(a, b):
    return jnp.dot(a, b, preferred_element_type=F32)


def dot_rows(a, b):
    return lax.dot_general(a, b, (((1,), (1,)), ((), ())), preferred_element_type=F32)


def dot_cols(a, b):
    return lax.dot_general(a, b, (((0,), (0,)), ((), ())), preferred_element_type=F32)


def unit_rows(values):
    centre = values - jnp.mean(values, axis=-1, keepdims=True)
    inverse = lax.rsqrt(jnp.mean(centre * centre, axis=-1, keepdims=True) + EPS)
    return centre * inverse, inverse


def norm_back(scaled, unit, inverse):
    return inverse * (
        scaled
        - jnp.mean(scaled, axis=-1, keepdims=True)
        - unit * jnp.mean(scaled * unit, axis=-1, keepdims=True)
    )


def gelu_parts(z):
    bell = jnp.exp(-0.5 * z * z)
    t = 1.0 / (1.0 + (TAIL_P * 0.5**0.5) * jnp.abs(z))
    poly = TAIL[6] * t + TAIL[5]
    for c in TAIL[4::-1]:
        poly = poly * t + c
    tail = 0.5 * poly * t * bell
    cdf = jnp.where(z >= 0, 1.0 - tail, tail)
    return z * cdf, cdf + z * bell * 0.3989422804014327


def fetch(scal, block, own, other, dst, sem, action):
    for take, src in ((scal[0] == block, own), (scal[0] != block, other)):
        @pl.when(take)
        def _():
            copy = pltpu.make_async_copy(src, dst, sem)
            copy.start() if action == "start" else copy.wait()


def image_ids(scal, shape, axis):
    position = lax.broadcasted_iota(jnp.int32, shape, axis)
    limit = jnp.int32(0)
    ids = jnp.zeros(shape, jnp.int32)
    for i in range(4):
        limit = limit + scal[1 + i]
        ids = ids + (position >= limit).astype(jnp.int32)
    return ids


def forward_kernel(block, scal, x_ref, small, wq_a, wq_b, wo_a, wo_b, wu_a, wu_b, wd_a, wd_b,
                   y_ref, facts, qkv, probs, resid_ref, slope, wq, wo, wu, wd, sems):
    jobs = ((wq_a, wq_b, wq), (wo_a, wo_b, wo), (wu_a, wu_b, wu), (wd_a, wd_b, wd))

    def weight(i, action):
        own, other, dst = jobs[i]
        fetch(scal, block, own, other, dst, sems.at[i], action)

    for i in range(4):
        weight(i, "start")
    x = x_ref[...].astype(F32)
    unit, _ = unit_rows(x)
    n1 = (unit * small[0:1, :] + small[2:3, :]).astype(BF16)
    facts[:, N1 : N1 + D] = n1
    same = image_ids(scal, (ROWS, ROWS), 0) == image_ids(scal, (ROWS, ROWS), 1)
    bias = jnp.where(same, 0.0, MASKED)
    first = lax.broadcasted_iota(jnp.int32, (1, PAIR), 1) < HD
    weight(0, "wait")
    for j in range(3):
        qkv[:, D * j : D * (j + 1)] = dot(n1, wq[:, D * j : D * (j + 1)]).astype(BF16)
    for p in range(HEADS // 2):
        cols = slice(PAIR * p, PAIR * (p + 1))
        q = qkv[:, PAIR * p : PAIR * (p + 1)] * jnp.asarray(HD**-0.5, BF16)
        k = qkv[:, D + PAIR * p : D + PAIR * (p + 1)]
        v = qkv[:, 2 * D + PAIR * p : 2 * D + PAIR * (p + 1)]
        outs = []
        for side in range(2):
            own = first if side == 0 else jnp.logical_not(first)
            s = dot_rows(jnp.where(own, q, jnp.zeros_like(q)), k) + bias
            s = jnp.exp(s - jnp.max(s, axis=-1, keepdims=True))
            pr = (s * (1.0 / jnp.sum(s, axis=-1, keepdims=True))).astype(BF16)
            probs[2 * p + side] = pr
            outs.append(dot(pr, v))
        facts[:, MIX + PAIR * p : MIX + PAIR * (p + 1)] = jnp.where(first, outs[0], outs[1]).astype(BF16)
    weight(1, "wait")
    resid = x + dot(facts[:, MIX : MIX + D], wo[...]) + small[4:5, :]
    resid_ref[...] = resid
    unit, _ = unit_rows(resid)
    n2 = (unit * small[1:2, :] + small[3:4, :]).astype(BF16)
    facts[:, N2 : N2 + D] = n2
    weight(2, "wait")
    weight(3, "wait")
    y = resid + small[5:6, :]
    for j in range(FF // D):
        cols = slice(D * j, D * (j + 1))
        pre = dot(n2, wu[:, cols]) + small[6 + j : 7 + j, :]
        act, sl = gelu_parts(pre)
        act = act.astype(BF16)
        facts[:, cols] = act
        slope[:, cols] = sl.astype(BF16)
        y = y + dot(act, wd[cols, :])
    y_ref[...] = y.astype(y_ref.dtype)


def shape(s, t):
    return jax.ShapeDtypeStruct(s, t)


def cost(flops, nbytes, trans=0):
    return pl.CostEstimate(flops=flops, bytes_accessed=nbytes, transcendentals=trans)


def block_forward(block, scal, x, small, weights, out_type):
    wq, wo, wu, wd = weights
    return pl.pallas_call(
        partial(forward_kernel, block),
        in_specs=[SMEM, VMEM, VMEM] + [ANY] * 8,
        out_specs=[VMEM] * 6,
        out_shape=[
            shape((ROWS, D), out_type), shape((ROWS, FACTS), BF16), shape((ROWS, 3 * D), BF16),
            shape((HEADS, ROWS, ROWS), BF16), shape((ROWS, D), F32), shape((ROWS, FF), BF16),
        ],
        scratch_shapes=[
            pltpu.VMEM((D, 3 * D), BF16), pltpu.VMEM((D, D), BF16), pltpu.VMEM((D, FF), BF16),
            pltpu.VMEM((FF, D), BF16), pltpu.SemaphoreType.DMA((4,)),
        ],
        compiler_params=pltpu.CompilerParams(vmem_limit_bytes=ROOM),
        cost_estimate=cost(2 * ROWS * D * 12 * D, 26 * 2**20, 2 * ROWS * FF),
        name=f"forward_{block}",
    )(scal, x, small, *wq, *wo, *wu, *wd)


HALF_UP = FF // 2
HALF = D // 2
HALF_QKV = 3 * D // 2


def ffn_backward_kernel(block, scal, g_ref, slope, resid_ref, small, wu_a, wu_b, wd_a, wd_b,
                        keep, send, dres_ref, sums, wu, wd, sems):
    jobs = ((wd_a, wd_b, wd), (wu_a, wu_b, wu))

    def weight(i, action):
        own, other, dst = jobs[i]
        fetch(scal, block, own, other, dst, sems.at[i], action)

    def store(half, cols, value):
        @pl.when(scal[0] == half)
        def _():
            keep[:, cols] = value

        @pl.when(scal[0] != half)
        def _():
            send[:, cols] = value

    weight(0, "start")
    weight(1, "start")
    g = g_ref[...].astype(F32)
    gl = g.astype(BF16)
    for half in range(2):
        store(half, slice(HALF_UP, HALF_UP + HALF), gl[:, HALF * half : HALF * (half + 1)])
    sums[2:3, :] = jnp.sum(g, axis=0, keepdims=True)
    weight(0, "wait")
    weight(1, "wait")
    d_n2 = jnp.zeros((ROWS, D), F32)
    for j in range(FF // D):
        cols = slice(D * j, D * (j + 1))
        d_act = dot_rows(gl, wd[cols, :])
        d_pre = (d_act * slope[:, cols].astype(F32)).astype(BF16)
        store(j // 2, slice(D * (j % 2), D * (j % 2 + 1)), d_pre)
        sums[4 + j : 5 + j, :] = jnp.sum(d_pre.astype(F32), axis=0, keepdims=True)
        d_n2 = d_n2 + dot_rows(d_pre, wu[:, cols])
    unit, inverse = unit_rows(resid_ref[...])
    sums[0:1, :] = jnp.sum(d_n2 * unit, axis=0, keepdims=True)
    sums[1:2, :] = jnp.sum(d_n2, axis=0, keepdims=True)
    d_resid = g + norm_back(d_n2 * small[1:2, :], unit, inverse)
    dres_ref[...] = d_resid
    sums[3:4, :] = jnp.sum(d_resid, axis=0, keepdims=True)


def ffn_backward(block, scal, g, slope, resid, small, weights):
    _, _, wu, wd = weights
    return pl.pallas_call(
        partial(ffn_backward_kernel, block),
        in_specs=[SMEM] + [VMEM] * 4 + [ANY] * 4,
        out_specs=[VMEM] * 4,
        out_shape=[
            shape((ROWS, HALF_UP + HALF), BF16), shape((ROWS, HALF_UP + HALF), BF16),
            shape((ROWS, D), F32), shape((8, D), F32),
        ],
        scratch_shapes=[
            pltpu.VMEM((D, FF), BF16), pltpu.VMEM((FF, D), BF16), pltpu.SemaphoreType.DMA((2,)),
        ],
        compiler_params=pltpu.CompilerParams(vmem_limit_bytes=ROOM),
        cost_estimate=cost(2 * ROWS * D * 8 * D, 16 * 2**20),
        name=f"ffn_backward_{block}",
    )(scal, g, slope, resid, small, *wu, *wd)


def att_backward_kernel(block, final, scal, dres_ref, qkv, probs, x_ref, small, wq_a, wq_b, wo_a, wo_b, *rest):
    if final:
        keep, send, gx_ref, sums, d_qkv, wq, wo, sems = rest
    else:
        mean_ref, keep, send, code_ref, inner_ref, sums, d_qkv, wq, wo, sems = rest
    jobs = ((wo_a, wo_b, wo), (wq_a, wq_b, wq))

    def weight(i, action):
        own, other, dst = jobs[i]
        fetch(scal, block, own, other, dst, sems.at[i], action)

    def store(half, cols, value):
        @pl.when(scal[0] == half)
        def _():
            keep[:, cols] = value

        @pl.when(scal[0] != half)
        def _():
            send[:, cols] = value

    weight(0, "start")
    weight(1, "start")
    d_resid = dres_ref[...]
    rl = d_resid.astype(BF16)
    for half in range(2):
        store(half, slice(HALF_QKV, HALF_QKV + HALF), rl[:, HALF * half : HALF * (half + 1)])
    first = lax.broadcasted_iota(jnp.int32, (1, PAIR), 1) < HD
    weight(0, "wait")
    d_mixed = dot_rows(rl, wo[...]).astype(BF16)
    scale = jnp.asarray(HD**-0.5, BF16)
    for p in range(HEADS // 2):
        q = qkv[:, PAIR * p : PAIR * (p + 1)] * scale
        k = qkv[:, D + PAIR * p : D + PAIR * (p + 1)]
        v = qkv[:, 2 * D + PAIR * p : 2 * D + PAIR * (p + 1)]
        dm = d_mixed[:, PAIR * p : PAIR * (p + 1)]
        dq, dk, dv = [], [], []
        for side in range(2):
            own = first if side == 0 else jnp.logical_not(first)
            pr = probs[2 * p + side]
            dp = dot_rows(jnp.where(own, dm, jnp.zeros_like(dm)), v)
            prf = pr.astype(F32)
            ds = (prf * (dp - jnp.sum(dp * prf, axis=-1, keepdims=True))).astype(BF16)
            dv.append(dot_cols(pr, dm))
            dq.append(dot(ds, k))
            dk.append(dot_cols(ds, q))
        for at, parts in ((0, dq), (D, dk), (2 * D, dv)):
            value = jnp.where(first, parts[0], parts[1])
            if at == 0:
                value = value * HD**-0.5
            d_qkv[:, at + PAIR * p : at + PAIR * (p + 1)] = value.astype(BF16)
    for half in range(2):
        store(half, slice(0, HALF_QKV), d_qkv[:, HALF_QKV * half : HALF_QKV * (half + 1)])
    weight(1, "wait")
    d_n1 = dot_rows(d_qkv[...], wq[...])
    x = x_ref[...].astype(F32)
    unit, inverse = unit_rows(x)
    sums[0:1, :] = jnp.sum(d_n1 * unit, axis=0, keepdims=True)
    sums[1:2, :] = jnp.sum(d_n1, axis=0, keepdims=True)
    sums[2:8, :] = jnp.zeros((6, D), F32)
    grad_x = d_resid + norm_back(d_n1 * small[0:1, :], unit, inverse)
    if final:
        gx_ref[...] = grad_x
    else:
        mean_code = mean_ref[...]
        inv = lax.rsqrt(jnp.mean(mean_code * mean_code, axis=-1, keepdims=True) + EPS)
        code = inv * (grad_x - x * jnp.mean(grad_x * x, axis=-1, keepdims=True))
        code = code.astype(BF16)
        code_ref[...] = code
        inner_ref[...] = jnp.sum(code.astype(F32) * mean_code, axis=-1, keepdims=True)


def att_backward(block, scal, d_resid, qkv, probs, x, small, weights, mean_code=None):
    wq, wo, _, _ = weights
    final = mean_code is None
    wide = HALF_QKV + HALF
    if final:
        extra, outs = [], [shape((ROWS, D), F32)]
    else:
        extra, outs = [mean_code], [shape((ROWS, D), BF16), shape((ROWS, 1), F32)]
    return pl.pallas_call(
        partial(att_backward_kernel, block, final),
        in_specs=[SMEM] + [VMEM] * 5 + [ANY] * 4 + [VMEM] * len(extra),
        out_specs=[VMEM] * (3 + len(outs)),
        out_shape=[shape((ROWS, wide), BF16), shape((ROWS, wide), BF16), *outs, shape((8, D), F32)],
        scratch_shapes=[
            pltpu.VMEM((ROWS, 3 * D), BF16), pltpu.VMEM((D, 3 * D), BF16), pltpu.VMEM((D, D), BF16),
            pltpu.SemaphoreType.DMA((2,)),
        ],
        compiler_params=pltpu.CompilerParams(vmem_limit_bytes=ROOM),
        cost_estimate=cost(2 * ROWS * D * 6 * D, 12 * 2**20),
        name=f"att_backward_{block}",
    )(scal, d_resid, qkv, probs, x, small, *wq, *wo, *extra)


def ffn_weight_kernel(facts_a, facts_b, cot_a, cot_b, down, up):
    parts = ((facts_a, cot_a), (facts_b, cot_b))
    for j in range(FF // D):
        cols = slice(D * j, D * (j + 1))
        down[cols, :] = sum(
            dot_cols(f[:, cols], c[:, HALF_UP : HALF_UP + HALF]) for f, c in parts
        ).astype(BF16)
    for j in range(HALF_UP // HALF):
        cols = slice(HALF * j, HALF * (j + 1))
        up[j] = sum(dot_cols(f[:, N2 : N2 + D], c[:, cols]) for f, c in parts).astype(BF16)


def ffn_weight_grads(facts, cots):
    return pl.pallas_call(
        ffn_weight_kernel,
        in_specs=[VMEM] * 4,
        out_specs=[VMEM] * 2,
        out_shape=[shape((FF, HALF), BF16), shape((HALF_UP // HALF, D, HALF), BF16)],
        compiler_params=pltpu.CompilerParams(vmem_limit_bytes=ROOM),
        cost_estimate=cost(2 * 2 * ROWS * FF * D, 16 * 2**20),
        name="ffn_weight_grads",
    )(*facts, *cots)


def att_weight_kernel(facts_a, facts_b, cot_a, cot_b, left, right):
    parts = ((facts_a, cot_a), (facts_b, cot_b))
    for j in range(4):
        at = N1 if j < 3 else MIX
        cols = slice(HALF * j, HALF * (j + 1))
        value = sum(dot_cols(f[:, at : at + D], c[:, cols]) for f, c in parts).astype(BF16)
        (left if j < 2 else right)[j % 2] = value


def att_weight_grads(facts, cots):
    return pl.pallas_call(
        att_weight_kernel,
        in_specs=[VMEM] * 4,
        out_specs=[VMEM] * 2,
        out_shape=[shape((2, D, HALF), BF16)] * 2,
        compiler_params=pltpu.CompilerParams(vmem_limit_bytes=ROOM),
        cost_estimate=cost(2 * 2 * ROWS * D * 2 * D, 10 * 2**20),
        name="att_weight_grads",
    )(*facts, *cots)


TILE = 1024


def lookup_kernel(last, hid, table, *rest):
    if last:
        m_in, l_in, a_in, mean_ref, unit_ref, lse_ref, m_ref, l_ref, acc = rest
    else:
        m_ref, l_ref, acc = rest
    step = pl.program_id(0)

    @pl.when(step == 0)
    def _():
        if last:
            m_ref[...] = m_in[...]
            l_ref[...] = l_in[...]
            acc[...] = a_in[...]
        else:
            m_ref[...] = jnp.full((ROWS, 1), MASKED, F32)
            l_ref[...] = jnp.zeros((ROWS, 1), F32)
            acc[...] = jnp.zeros((ROWS, D), F32)

    s = dot_rows(hid[...], table[...]) * D**-0.5
    top = jnp.maximum(m_ref[...], jnp.max(s, axis=-1, keepdims=True))
    fade = jnp.exp(m_ref[...] - top)
    s = jnp.exp(s - top)
    m_ref[...] = top
    l_ref[...] = l_ref[...] * fade + jnp.sum(s, axis=-1, keepdims=True)
    high = s.astype(BF16)
    low = (s - high.astype(F32)).astype(BF16)
    acc[...] = acc[...] * fade + (dot(high, table[...]) + dot(low, table[...]))
    if last:
        @pl.when(step == pl.num_programs(0) - 1)
        def _():
            totals = l_ref[...]
            mean_code = acc[...] / totals
            mean_ref[...] = mean_code
            unit_ref[...] = mean_code * lax.rsqrt(
                jnp.mean(mean_code * mean_code, axis=-1, keepdims=True) + EPS
            )
            lse_ref[...] = m_ref[...] + jnp.log(totals)


def whole(s):
    return pl.BlockSpec(s, lambda i: (0,) * len(s))


def lookup(hidden, table, state=None):
    last = state is not None
    tile = min(TILE, table.shape[0])
    col, mat = (ROWS, 1), (ROWS, D)
    if last:
        outs = [mat, mat, col]
        scratch = [pltpu.VMEM(col, F32), pltpu.VMEM(col, F32), pltpu.VMEM(mat, F32)]
    else:
        outs, scratch = [col, col, mat], []
    return pl.pallas_call(
        partial(lookup_kernel, last),
        grid=(table.shape[0] // tile,),
        in_specs=[whole(mat), pl.BlockSpec((tile, D), lambda i: (i, 0))]
        + ([whole(col), whole(col), whole(mat)] if last else []),
        out_specs=[whole(o) for o in outs],
        out_shape=[shape(o, F32) for o in outs],
        scratch_shapes=scratch,
        compiler_params=pltpu.CompilerParams(vmem_limit_bytes=ROOM),
        cost_estimate=cost(6 * ROWS * D * table.shape[0], 2 * table.size, ROWS * table.shape[0]),
        name=f"lookup_{int(last)}",
    )(hidden, table, *(state if last else ()))


def lookup_back_kernel(hid, code, lse, inner, table_a, table_b, out):
    step = pl.program_id(0)

    @pl.when(step == 0)
    def _():
        out[...] = jnp.zeros_like(out)

    for table in (table_a, table_b):
        s = dot_rows(hid[...], table[...]) * D**-0.5
        p = jnp.exp(s - lse[...])
        dp = dot_rows(code[...], table[...])
        ds = (p * (dp - inner[...])).astype(BF16)
        out[...] += dot(ds, table[...])

    @pl.when(step == pl.num_programs(0) - 1)
    def _():
        out[...] = out[...] * D**-0.5


def lookup_back(hidden, code, lse, inner, table_a, table_b):
    tile = min(TILE, table_a.shape[0])
    col, mat = (ROWS, 1), (ROWS, D)
    spec = pl.BlockSpec((tile, D), lambda i: (i, 0))
    return pl.pallas_call(
        lookup_back_kernel,
        grid=(table_a.shape[0] // tile,),
        in_specs=[whole(mat), whole(mat), whole(col), whole(col), spec, spec],
        out_specs=whole(mat),
        out_shape=shape(mat, F32),
        compiler_params=pltpu.CompilerParams(vmem_limit_bytes=ROOM),
        cost_estimate=cost(12 * ROWS * D * table_a.shape[0], 4 * table_a.size, 2 * ROWS * table_a.shape[0]),
        name="lookup_back",
    )(hidden, code, lse, inner, table_a, table_b)


def swapped(value):
    return lax.ppermute(value, "section", [(0, 1), (1, 0)])


def bit_count():
    size = lax.axis_size("dp")
    count = size.bit_length() - 1
    assert size == 1 << count
    return count


def along(value, bit):
    size = lax.axis_size("dp")
    return lax.ppermute(value, "dp", [(i, i ^ (1 << bit)) for i in range(size)])


def gathered(rows):
    count = bit_count()
    far = list(range(2, count))
    near = list(range(min(count, 2)))
    half = rows.shape[0] // 2
    out = []
    for piece, order in ((rows[:half], far + near), (rows[half:], far + near[::-1])):
        for bit in order:
            piece = jnp.concatenate([piece, along(piece, bit)])
        out.append(piece)
    return jnp.concatenate(out)


def total(terms):
    summed = terms[0].astype(F32)
    for term in terms[1:]:
        summed = summed + term.astype(F32)
    return summed


class Share:
    def __init__(self, groups):
        count = bit_count()
        size = 1 << count
        kinds, rows, cols = groups.shape
        value = groups.reshape((kinds,) + (2,) * count + (rows // size, cols))
        self.live = list(range(count))[::-1]
        self.terms = [jnp.moveaxis(value, 0, count)]

    def split(self, bit):
        axis = self.live.index(bit)
        mine = (lax.axis_index("dp") >> bit) & 1

        def pick(which):
            return [lax.dynamic_index_in_dim(t, which, axis, keepdims=False) for t in self.terms]

        sent = total(pick(1 - mine)).astype(BF16)
        self.terms = pick(mine)
        self.live.remove(bit)
        return sent


def scatter_pair(left, right):
    shares = [Share(left), Share(right)]
    count = bit_count()
    near = list(range(min(count, 2)))
    for bits in zip(near, near[::-1]):
        for share, bit in zip(shares, bits):
            got = along(share.split(bit), bit)
            share.terms.append(got)
    for bit in range(len(near), count):
        got = along(jnp.stack([share.split(bit) for share in shares]), bit)
        for i, share in enumerate(shares):
            share.terms.append(got[i])
    return jnp.stack([total(share.terms) for share in shares])


def per_device(
    patches,
    recon_cot,
    lengths,
    codebook,
    w_qkv,
    w_out,
    w_up,
    w_down,
    norm_gain,
    norm_bias,
    bias_out,
    bias_up,
):
    section = lax.axis_index("section")
    on_first = section == 0
    size = lax.axis_size("dp")
    lens = lax.dynamic_index_in_dim(lengths, section, 0, keepdims=False)
    scal = jnp.concatenate([section[None].astype(jnp.int32), lens])
    own_small = jnp.concatenate([norm_gain[0], norm_bias[0], bias_out[0], bias_up.reshape(-1, D)])
    small_other = swapped(own_small)
    small = [jnp.where(on_first, own_small, small_other), jnp.where(on_first, small_other, own_small)]
    weights = [(w[0], swapped(w[0])) for w in (w_qkv, w_out, w_up, w_down)]
    table = gathered(codebook)
    table_other = swapped(table)
    x = lax.dynamic_slice_in_dim(patches, section * ROWS, ROWS)
    g = lax.dynamic_slice_in_dim(recon_cot, section * ROWS, ROWS)

    hidden, facts_e, qkv_e, probs_e, resid_e, slope_e = block_forward(0, scal, x, small[0], weights, BF16)
    facts_e = (facts_e, swapped(facts_e))
    mean_code, unit, lse = lookup(hidden, table_other, lookup(hidden, table))
    recon, facts_d, qkv_d, probs_d, resid_d, slope_d = block_forward(1, scal, unit, small[1], weights, F32)
    facts_d = (facts_d, swapped(facts_d))
    recon_first = lax.ppermute(recon, "section", [(0, 1)])
    lse_other = swapped(lse)

    keep, send, d_resid, sums_df = ffn_backward(1, scal, g, slope_d, resid_d, small[1], weights)
    down, up = ffn_weight_grads(facts_d, (keep, swapped(send)))
    ffn_d = scatter_pair(down.reshape(size, -1, D // size, HALF).swapaxes(0, 1).reshape(-1, D, HALF), up)
    keep, send, code, inner, sums_da = att_backward(
        1, scal, d_resid, qkv_d, probs_d, unit, small[1], weights, mean_code
    )
    att_d = scatter_pair(*att_weight_grads(facts_d, (keep, swapped(send))))
    d_hidden = lookup_back(hidden, code, lse, inner, table, table_other)
    keep, send, d_resid, sums_ef = ffn_backward(0, scal, d_hidden, slope_e, resid_e, small[0], weights)
    down, up = ffn_weight_grads(facts_e, (keep, swapped(send)))
    ffn_e = scatter_pair(down.reshape(size, -1, D // size, HALF).swapaxes(0, 1).reshape(-1, D, HALF), up)
    keep, send, grad_x, sums_ea = att_backward(0, scal, d_resid, qkv_e, probs_e, x, small[0], weights)
    att_e = scatter_pair(*att_weight_grads(facts_e, (keep, swapped(send))))
    grad_second = lax.ppermute(grad_x, "section", [(1, 0)])

    def own_halves(enc, dec):
        kept = jnp.where(on_first, enc, dec)
        got = swapped(jnp.where(on_first, dec, enc))
        return jnp.where(on_first, kept, got), jnp.where(on_first, got, kept)

    ffn = jnp.stack(own_halves(ffn_e, ffn_d))
    att = jnp.stack(own_halves(att_e, att_d)).reshape(2, 4, -1, HALF)
    width = D // size
    grad_down = ffn[:, 0].reshape(2, 4 * width, HALF).swapaxes(0, 1).reshape(1, 4 * width, D)
    grad_up = ffn[:, 1].transpose(2, 0, 1, 3).reshape(1, width, FF)
    grad_qkv = att[:, :3].transpose(2, 0, 1, 3).reshape(1, width, 3 * D)
    grad_out = att[:, 3].swapaxes(0, 1).reshape(1, width, D)

    sums = jnp.stack([jnp.stack([sums_ef, sums_ea]), jnp.stack([sums_df, sums_da])])
    sums = sums + swapped(sums)
    for bit in range(bit_count()):
        sums = sums + along(sums, bit)
    sums = jnp.where(on_first, sums[0], sums[1])
    cols = lax.axis_index("dp") * width
    rows = lax.dynamic_slice_in_dim(sums, cols, width, axis=2)
    grad_gain = jnp.stack([rows[1, 0], rows[0, 0]])[None]
    grad_nbias = jnp.stack([rows[1, 1], rows[0, 1]])[None]
    grad_bout = jnp.stack([rows[0, 3], rows[0, 2]])[None]
    grad_bup = lax.dynamic_slice_in_dim(sums[0, 4:].reshape(FF), cols * 4, width * 4)[None]

    ends = jnp.where(
        on_first, jnp.concatenate([grad_x, grad_second]), jnp.concatenate([recon_first, recon])
    )[None]
    lse, lse_other = lse[:, 0], lse_other[:, 0]
    codes = jnp.where(on_first, jnp.concatenate([lse, lse_other]), jnp.concatenate([lse_other, lse]))
    return (ends, codes, grad_qkv, grad_out, grad_up, grad_down, grad_gain, grad_nbias, grad_bout, grad_bup)


def solution(mesh):
    placed = (
        P("dp", None),
        P("dp", None),
        P("dp", None),
        P(("dp", "section"), None),
        P("section", None, None),
        P("section", None, None),
        P("section", None, None),
        P("section", None, None),
        P("section", None, None),
        P("section", None, None),
        P("section", None, None),
        P("section", None),
    )
    return jax.shard_map(
        per_device,
        mesh=mesh,
        in_specs=placed,
        out_specs=(
            P("section", "dp", None),
            P("dp"),
            P("section", "dp", None),
            P("section", "dp", None),
            P("section", "dp", None),
            P("section", "dp", None),
            P("section", None, "dp"),
            P("section", None, "dp"),
            P("section", None, "dp"),
            P("section", "dp"),
        ),
        check_vma=False,
    )
```

```python
from functools import partial

import jax
import jax.numpy as jnp
from jax import lax
from jax.experimental import pallas as pl
from jax.experimental.pallas import tpu as pltpu
from jax.sharding import PartitionSpec as P

D = 768
HEADS = 12
HD = 64
FF = 3072
ROWS = 256
PAIR = 2 * HD
EPS = 1e-06
MASKED = -1e30
F32 = jnp.float32
BF16 = jnp.bfloat16
N2, FFN_FACTS = FF, FF + D
MIX, ATT_FACTS = D, 2 * D
HALF = D // 2
HALF_UP = FF // 2
HALF_QKV = 3 * D // 2
TAIL_P = 0.35
TAIL = (0.19620077326315646, 0.2185939781557991, 0.05480664657447366, 0.5651487076988272,
        -0.5574354264567037, 0.7060774515721405, -0.18339209581143395)
VMEM = pl.BlockSpec(memory_space=pltpu.VMEM)
SMEM = pl.BlockSpec(memory_space=pltpu.SMEM)
ANY = pl.BlockSpec(memory_space=pl.ANY)
ROOM = 58 * 1024 * 1024


def dot(a, b):
    return jnp.dot(a, b, preferred_element_type=F32)


def dot_rows(a, b):
    return lax.dot_general(a, b, (((1,), (1,)), ((), ())), preferred_element_type=F32)


def dot_cols(a, b):
    return lax.dot_general(a, b, (((0,), (0,)), ((), ())), preferred_element_type=F32)


def unit_rows(values):
    centre = values - jnp.mean(values, axis=-1, keepdims=True)
    inverse = lax.rsqrt(jnp.mean(centre * centre, axis=-1, keepdims=True) + EPS)
    return centre * inverse, inverse


def norm_back(scaled, unit, inverse):
    return inverse * (
        scaled
        - jnp.mean(scaled, axis=-1, keepdims=True)
        - unit * jnp.mean(scaled * unit, axis=-1, keepdims=True)
    )


def gelu_parts(z):
    bell = jnp.exp(-0.5 * z * z)
    t = 1.0 / (1.0 + (TAIL_P * 0.5**0.5) * jnp.abs(z))
    poly = TAIL[6] * t + TAIL[5]
    for c in TAIL[4::-1]:
        poly = poly * t + c
    tail = 0.5 * poly * t * bell
    cdf = jnp.where(z >= 0, 1.0 - tail, tail)
    return z * cdf, cdf + z * bell * 0.3989422804014327


def image_ids(scal, shape, axis):
    position = lax.broadcasted_iota(jnp.int32, shape, axis)
    limit = jnp.int32(0)
    ids = jnp.zeros(shape, jnp.int32)
    for i in range(4):
        limit = limit + scal[1 + i]
        ids = ids + (position >= limit).astype(jnp.int32)
    return ids


def shape(s, t):
    return jax.ShapeDtypeStruct(s, t)


class Moves:
    def __init__(self, sems):
        self.sems = sems
        self.used = 0
        self.leaving = []

    def sem(self):
        self.used += 1
        return self.sems.at[self.used - 1]

    def load(self, src, dst):
        copy = pltpu.make_async_copy(src, dst, self.sem())
        copy.start()
        return copy.wait

    def load_either(self, first, src, other, dst):
        sem = self.sem()

        def act(name):
            for take, ref in ((first, src), (jnp.logical_not(first), other)):
                @pl.when(take)
                def _():
                    getattr(pltpu.make_async_copy(ref, dst, sem), name)()

        act("start")
        return partial(act, "wait")

    def store(self, src, dst):
        copy = pltpu.make_async_copy(src, dst, self.sem())
        copy.start()
        self.leaving.append(copy.wait)

    def finish(self):
        for wait in self.leaving:
            wait()


SEMS = 32


def call(body, name, scal, inputs, outs, scratch, flops, small=()):
    def kernel(*refs):
        moves = Moves(refs[-1])
        body(moves, *refs[:-1])
        moves.finish()

    size = sum(a.size * a.dtype.itemsize for a in (*inputs, *outs))
    return pl.pallas_call(
        kernel,
        in_specs=[SMEM] + [VMEM] * len(small) + [ANY] * len(inputs),
        out_specs=[ANY] * len(outs),
        out_shape=outs,
        scratch_shapes=[*(pltpu.VMEM(s, t) for s, t in scratch), pltpu.SemaphoreType.DMA((SEMS,))],
        compiler_params=pltpu.CompilerParams(vmem_limit_bytes=ROOM),
        cost_estimate=pl.CostEstimate(flops=flops, bytes_accessed=size, transcendentals=0),
        name=name,
    )(scal, *small, *inputs)


W_QKV = ((D, 3 * D), BF16)
W_OUT = ((D, D), BF16)
W_UP = ((D, FF), BF16)
W_DOWN = ((FF, D), BF16)
MAT = ((ROWS, D), F32)
LOW = ((ROWS, D), BF16)
COL = ((ROWS, 1), F32)


def rows_of(scal, own=True):
    which = scal[0] if own else 1 - scal[0]
    return pl.ds(pl.multiple_of(which * ROWS, ROWS), ROWS)


def half_of(scal, width, own=True):
    which = scal[0] if own else 1 - scal[0]
    return pl.ds(pl.multiple_of(which * width, 128), width)


def att_forward_part(moves, scal, x, small, wq, wait, facts, qkv, probs, out):
    facts_hbm, qkv_hbm, probs_hbm = out
    unit, _ = unit_rows(x)
    n1 = (unit * small[0:1, :] + small[2:3, :]).astype(BF16)
    facts[:, :D] = n1
    same = image_ids(scal, (ROWS, ROWS), 0) == image_ids(scal, (ROWS, ROWS), 1)
    bias = jnp.where(same, 0.0, MASKED)
    first = lax.broadcasted_iota(jnp.int32, (1, PAIR), 1) < HD
    wait()
    for j in range(3):
        qkv[:, D * j : D * (j + 1)] = dot(n1, wq[:, D * j : D * (j + 1)]).astype(BF16)
    moves.store(qkv, qkv_hbm)
    for p in range(HEADS // 2):
        q = qkv[:, PAIR * p : PAIR * (p + 1)] * jnp.asarray(HD**-0.5, BF16)
        k = qkv[:, D + PAIR * p : D + PAIR * (p + 1)]
        v = qkv[:, 2 * D + PAIR * p : 2 * D + PAIR * (p + 1)]
        outs = []
        for side in range(2):
            own = first if side == 0 else jnp.logical_not(first)
            s = dot_rows(jnp.where(own, q, jnp.zeros_like(q)), k) + bias
            s = jnp.exp(s - jnp.max(s, axis=-1, keepdims=True))
            pr = (s * (1.0 / jnp.sum(s, axis=-1, keepdims=True))).astype(BF16)
            probs[2 * p + side] = pr
            outs.append(dot(pr, v))
        facts[:, MIX + PAIR * p : MIX + PAIR * (p + 1)] = jnp.where(first, outs[0], outs[1]).astype(BF16)
    moves.store(probs, probs_hbm)
    moves.store(facts, facts_hbm)


def ffn_forward_part(moves, x, small, mixed, wo, wu, wd, waits, facts, resid_ref, slope, y_ref, out):
    y_hbm, facts_hbm, resid_hbm, slope_hbm = out
    waits[0]()
    resid = x + dot(mixed, wo[...]) + small[4:5, :]
    resid_ref[...] = resid
    moves.store(resid_ref, resid_hbm)
    unit, _ = unit_rows(resid)
    n2 = (unit * small[1:2, :] + small[3:4, :]).astype(BF16)
    facts[:, N2 : N2 + D] = n2
    waits[1]()
    waits[2]()
    y = resid + small[5:6, :]
    for j in range(FF // D):
        cols = slice(D * j, D * (j + 1))
        pre = dot(n2, wu[:, cols]) + small[6 + j : 7 + j, :]
        act, sl = gelu_parts(pre)
        act = act.astype(BF16)
        facts[:, cols] = act
        slope[:, cols] = sl.astype(BF16)
        y = y + dot(act, wd[cols, :])
    moves.store(facts, facts_hbm)
    moves.store(slope, slope_hbm)
    y_ref[...] = y.astype(y_ref.dtype)
    moves.store(y_ref, y_hbm)


FACTS_A = ((ROWS, ATT_FACTS), BF16)
FACTS_F = ((ROWS, FFN_FACTS), BF16)
QKV = ((ROWS, 3 * D), BF16)
PROBS = ((HEADS, ROWS, ROWS), BF16)
SLOPE = ((ROWS, FF), BF16)


def outputs(*kinds):
    return [shape(*kind) for kind in kinds]


def block_forward(block, scal, x, small, weights):
    def body(moves, scal, small, x_in, wq_a, wq_b, wo_a, wo_b, wu_a, wu_b, wd_a, wd_b,
             y_o, facts_fo, facts_ao, qkv_o, probs_o, resid_o, slope_o,
             x, wq, wo, wu, wd, y, facts_f, facts_a, qkv, probs, resid, slope):
        own = scal[0] == block
        wait_x = moves.load(x_in, x)
        waits = [
            moves.load_either(own, a, b, w)
            for a, b, w in ((wq_a, wq_b, wq), (wo_a, wo_b, wo), (wu_a, wu_b, wu), (wd_a, wd_b, wd))
        ]
        wait_x()
        xs = x[...]
        att_forward_part(moves, scal, xs, small, wq, waits[0], facts_a, qkv, probs, (facts_ao, qkv_o, probs_o))
        ffn_forward_part(
            moves, xs, small, facts_a[:, MIX : MIX + D], wo, wu, wd, waits[1:], facts_f, resid, slope, y,
            (y_o, facts_fo, resid_o, slope_o),
        )

    kinds = (MAT, FACTS_F, FACTS_A, QKV, PROBS, MAT, SLOPE)
    return call(
        body, f"forward_{block}", scal, [x, *sum(weights, ())], outputs(*kinds),
        [MAT, W_QKV, W_OUT, W_UP, W_DOWN, *kinds], 2 * ROWS * D * 13 * D, [small],
    )


def att_forward(block, scal, patches, small, weights):
    def body(moves, scal, small, x_in, wq_a, wq_b, facts_o, qkv_o, probs_o, x, wq, facts, qkv, probs):
        wait_x = moves.load(x_in.at[rows_of(scal), :], x)
        wait_w = moves.load_either(scal[0] == block, wq_a, wq_b, wq)
        wait_x()
        att_forward_part(
            moves, scal, x[...].astype(F32), small, wq, wait_w, facts, qkv, probs, (facts_o, qkv_o, probs_o)
        )

    kinds = (FACTS_A, QKV, PROBS)
    return call(
        body, f"att_forward_{block}", scal, [patches, *weights[0]], outputs(*kinds),
        [LOW, W_QKV, *kinds], 2 * ROWS * D * 4 * D, [small],
    )


def ffn_forward(block, scal, patches, small, facts_a, weights):
    def body(moves, scal, small, x_in, facts_ai, wo_a, wo_b, wu_a, wu_b, wd_a, wd_b,
             y_o, facts_o, resid_o, slope_o, x, mixed, wo, wu, wd, y, facts, resid, slope):
        own = scal[0] == block
        wait_x = moves.load(x_in.at[rows_of(scal), :], x)
        wait_m = moves.load(facts_ai.at[:, pl.ds(MIX, D)], mixed)
        waits = [
            moves.load_either(own, a, b, w) for a, b, w in ((wo_a, wo_b, wo), (wu_a, wu_b, wu), (wd_a, wd_b, wd))
        ]
        wait_x()
        wait_m()
        ffn_forward_part(
            moves, x[...].astype(F32), small, mixed[...], wo, wu, wd, waits, facts, resid, slope, y,
            (y_o, facts_o, resid_o, slope_o),
        )

    kinds = (LOW, FACTS_F, MAT, SLOPE)
    return call(
        body, f"ffn_forward_{block}", scal, [patches, facts_a, *sum(weights[1:], ())], outputs(*kinds),
        [LOW, LOW, W_OUT, W_UP, W_DOWN, *kinds], 2 * ROWS * D * 9 * D, [small],
    )


COT_UP = ((ROWS, HALF_UP), BF16)
COT_ATT = ((ROWS, HALF_QKV + HALF), BF16)
SUMS = ((8, D), F32)


def ffn_backward(block, scal, g, slope, resid, small, weights, own_rows):
    def body(moves, scal, small, g_in, slope_in, resid_in, wu_a, wu_b, wd_a, wd_b,
             keep_o, send_o, dres_o, sums, g_ref, slope, resid, wu, wd, d_pre_ref, dres):
        own = scal[0] == block
        wait_g = moves.load(g_in.at[rows_of(scal), :] if own_rows else g_in, g_ref)
        wait_d = moves.load_either(own, wd_a, wd_b, wd)
        wait_s = moves.load(slope_in, slope)
        wait_u = moves.load_either(own, wu_a, wu_b, wu)
        wait_r = moves.load(resid_in, resid)
        wait_g()
        g = g_ref[...].astype(F32)
        gl = g.astype(BF16)
        small_sums = [None] * 4
        small_sums[2] = jnp.sum(g, axis=0, keepdims=True)
        wait_d()
        wait_s()
        wait_u()
        d_n2 = jnp.zeros((ROWS, D), F32)
        up_sums = []
        for j in range(FF // D):
            cols = slice(D * j, D * (j + 1))
            d_act = dot_rows(gl, wd[cols, :])
            d_pre = (d_act * slope[:, cols].astype(F32)).astype(BF16)
            d_pre_ref[:, cols] = d_pre
            up_sums.append(jnp.sum(d_pre.astype(F32), axis=0, keepdims=True))
            d_n2 = d_n2 + dot_rows(d_pre, wu[:, cols])
        moves.store(d_pre_ref.at[:, half_of(scal, HALF_UP)], keep_o)
        moves.store(d_pre_ref.at[:, half_of(scal, HALF_UP, False)], send_o)
        wait_r()
        unit, inverse = unit_rows(resid[...])
        small_sums[0] = jnp.sum(d_n2 * unit, axis=0, keepdims=True)
        small_sums[1] = jnp.sum(d_n2, axis=0, keepdims=True)
        d_resid = g + norm_back(d_n2 * small[1:2, :], unit, inverse)
        dres[...] = d_resid
        moves.store(dres, dres_o)
        small_sums[3] = jnp.sum(d_resid, axis=0, keepdims=True)
        for i, value in enumerate(small_sums + up_sums):
            sums[i : i + 1, :] = value

    def with_sums(moves, *refs):
        *head, sums_buffer = refs
        sums_o = head[12]
        head[12] = sums_buffer
        body(moves, *head)
        moves.store(sums_buffer, sums_o)

    g_kind = (tuple(g.shape), g.dtype) if not own_rows else ((ROWS, D), g.dtype)
    return call(
        with_sums, f"ffn_backward_{block}", scal, [g, slope, resid, *weights[2], *weights[3]],
        outputs(COT_UP, COT_UP, MAT, SUMS),
        [g_kind, SLOPE, MAT, W_UP, W_DOWN, SLOPE, MAT, SUMS], 2 * ROWS * D * 8 * D, [small],
    )


def att_backward(block, scal, d_resid, qkv, probs, x, small, weights, mean_code=None):
    final = mean_code is None

    def body(moves, scal, small, dres_in, qkv_in, probs_in, x_in, wq_a, wq_b, wo_a, wo_b, *rest):
        if final:
            keep_o, send_o, sums_o, gx_o, dres, qkv, probs, x_ref, wq, wo, d_qkv, rl_ref, sums, gx = rest
        else:
            (mean_in, keep_o, send_o, sums_o, code_o, inner_o,
             dres, qkv, probs, x_ref, wq, wo, d_qkv, rl_ref, sums, mean_ref, code_ref, inner_ref) = rest
        own = scal[0] == block
        wait_g = moves.load(dres_in, dres)
        wait_o = moves.load_either(own, wo_a, wo_b, wo)
        wait_k = moves.load(qkv_in, qkv)
        wait_p = moves.load(probs_in, probs)
        wait_q = moves.load_either(own, wq_a, wq_b, wq)
        wait_x = moves.load(x_in.at[rows_of(scal), :] if final else x_in, x_ref)
        if not final:
            wait_m = moves.load(mean_in, mean_ref)
        wait_g()
        d_resid = dres[...]
        rl = d_resid.astype(BF16)
        rl_ref[...] = rl
        for out, mine in ((keep_o, True), (send_o, False)):
            moves.store(rl_ref.at[:, half_of(scal, HALF, mine)], out.at[:, pl.ds(HALF_QKV, HALF)])
        first = lax.broadcasted_iota(jnp.int32, (1, PAIR), 1) < HD
        wait_o()
        d_mixed = dot_rows(rl, wo[...]).astype(BF16)
        wait_k()
        wait_p()
        scale = jnp.asarray(HD**-0.5, BF16)
        for p in range(HEADS // 2):
            q = qkv[:, PAIR * p : PAIR * (p + 1)] * scale
            k = qkv[:, D + PAIR * p : D + PAIR * (p + 1)]
            v = qkv[:, 2 * D + PAIR * p : 2 * D + PAIR * (p + 1)]
            dm = d_mixed[:, PAIR * p : PAIR * (p + 1)]
            dq, dk, dv = [], [], []
            for side in range(2):
                mine = first if side == 0 else jnp.logical_not(first)
                pr = probs[2 * p + side]
                dp = dot_rows(jnp.where(mine, dm, jnp.zeros_like(dm)), v)
                prf = pr.astype(F32)
                ds = (prf * (dp - jnp.sum(dp * prf, axis=-1, keepdims=True))).astype(BF16)
                dv.append(dot_cols(pr, dm))
                dq.append(dot(ds, k))
                dk.append(dot_cols(ds, q))
            for at, parts in ((0, dq), (D, dk), (2 * D, dv)):
                value = jnp.where(first, parts[0], parts[1])
                if at == 0:
                    value = value * HD**-0.5
                d_qkv[:, at + PAIR * p : at + PAIR * (p + 1)] = value.astype(BF16)
        for out, mine in ((keep_o, True), (send_o, False)):
            moves.store(d_qkv.at[:, half_of(scal, HALF_QKV, mine)], out.at[:, pl.ds(0, HALF_QKV)])
        wait_q()
        d_n1 = dot_rows(d_qkv[...], wq[...])
        wait_x()
        x = x_ref[...].astype(F32)
        unit, inverse = unit_rows(x)
        sums[0:1, :] = jnp.sum(d_n1 * unit, axis=0, keepdims=True)
        sums[1:2, :] = jnp.sum(d_n1, axis=0, keepdims=True)
        sums[2:8, :] = jnp.zeros((6, D), F32)
        moves.store(sums, sums_o)
        grad_x = d_resid + norm_back(d_n1 * small[0:1, :], unit, inverse)
        if final:
            gx[...] = grad_x
            moves.store(gx, gx_o)
        else:
            wait_m()
            mean_code = mean_ref[...]
            inv = lax.rsqrt(jnp.mean(mean_code * mean_code, axis=-1, keepdims=True) + EPS)
            code = inv * (grad_x - x * jnp.mean(grad_x * x, axis=-1, keepdims=True))
            code = code.astype(BF16)
            code_ref[...] = code
            moves.store(code_ref, code_o)
            inner_ref[...] = jnp.sum(code.astype(F32) * mean_code, axis=-1, keepdims=True)
            moves.store(inner_ref, inner_o)

    more_in, more = ([], [MAT]) if final else ([mean_code], [LOW, COL])
    return call(
        body, f"att_backward_{block}", scal, [d_resid, qkv, probs, x, *weights[0], *weights[1], *more_in],
        outputs(COT_ATT, COT_ATT, SUMS, *more),
        [MAT, QKV, PROBS, LOW if final else MAT, W_QKV, W_OUT, QKV, LOW, SUMS,
         *([] if final else [MAT]), *more],
        2 * ROWS * D * 6 * D, [small],
    )


def split_kinds(kinds, bit, count):
    size = 1 << count
    width = D // size
    if width % 16:
        return None
    high = size >> (bit + 1)
    return (kinds, high, 2, 1 << bit, width, HALF), (kinds, high, 1 << bit, width, HALF)


def group_outputs(kinds, bit, count):
    split = split_kinds(kinds, bit, count)
    if split is None:
        return [((kinds, D, HALF), BF16)], ((kinds, D, HALF), BF16)
    return [(split[1], BF16)] * 2, (split[0], BF16)


def put(buffer, kind, value):
    buffer[kind] = value.astype(BF16).reshape(buffer.shape[1:])


def leave(moves, buffer, outs, mine):
    if len(outs) == 1:
        moves.store(buffer, outs[0])
    else:
        moves.store(buffer.at[:, :, mine], outs[0])
        moves.store(buffer.at[:, :, 1 - mine], outs[1])


def down_grads(scal, facts, cots, count, both):
    outs, buffer = group_outputs(FF // D, 0, count)
    width = D >> count

    def body(moves, scal, *refs):
        ins, out, (fa, fb, ca, cb, buf) = refs[: 2 + len(cots)], refs[2 + len(cots) : -5], refs[-5:]
        waits = [moves.load(ins[i].at[:, pl.ds(0, FF)], f) for i, f in ((0, fa), (1, fb))]
        if both:
            for c, own in ((ca, True), (cb, False)):
                waits.append(moves.load(ins[2].at[rows_of(scal, own), half_of(scal, HALF)], c))
        else:
            waits += [moves.load(ref, c) for ref, c in zip(ins[2:], (ca, cb))]
        for wait in waits:
            wait()
        for j in range(FF // D):
            cols = slice(D * j, D * (j + 1))
            value = dot_cols(fa[:, cols], ca[...]) + dot_cols(fb[:, cols], cb[...])
            value = value.astype(BF16)
            owners = value.reshape(D // (4 * width), 4, width, HALF)
            for kind in range(4):
                part = owners[:, kind]
                if len(out) == 1:
                    rows = D // 4
                    buf[kind, rows * j : rows * (j + 1), :] = part.reshape(rows, HALF)
                else:
                    high = part.shape[0] // 2
                    buf[kind, high * j : high * (j + 1)] = part.reshape((high, 2, 1, width, HALF))
        leave(moves, buf, out, scal[6])

    return call(
        body, "down_grads", scal, [*facts, *cots], outputs(*outs),
        [((ROWS, FF), BF16)] * 2 + [((ROWS, HALF), BF16)] * 2 + [buffer], 4 * ROWS * FF * HALF,
    )


def up_grads(scal, facts, cots, count):
    outs, buffer = group_outputs(HALF_UP // HALF, 1, count)

    def body(moves, scal, *refs):
        ins, out, (fa, fb, ca, cb, buf) = refs[:4], refs[4:-5], refs[-5:]
        waits = [moves.load(ins[i].at[:, pl.ds(N2, D)], f) for i, f in ((0, fa), (1, fb))]
        waits += [moves.load(ref, c) for ref, c in zip(ins[2:], (ca, cb))]
        for wait in waits:
            wait()
        for j in range(HALF_UP // HALF):
            cols = slice(HALF * j, HALF * (j + 1))
            put(buf, j, dot_cols(fa[...], ca[:, cols]) + dot_cols(fb[...], cb[:, cols]))
        leave(moves, buf, out, scal[7])

    return call(
        body, "up_grads", scal, [*facts, *cots], outputs(*outs),
        [LOW] * 2 + [COT_UP] * 2 + [buffer], 4 * ROWS * FF * HALF,
    )


def att_grads(scal, facts, cots, count):
    left, left_buffer = group_outputs(2, 0, count)
    right, right_buffer = group_outputs(2, 1, count)

    def body(moves, scal, *refs):
        ins, outs, (fa, fb, ca, cb, buf_l, buf_r) = refs[:4], refs[4:-6], refs[-6:]
        waits = [moves.load(src, dst) for src, dst in zip(ins, (fa, fb, ca, cb))]
        for wait in waits:
            wait()
        for j in range(4):
            at = slice(0, D) if j < 3 else slice(MIX, MIX + D)
            cols = slice(HALF * j, HALF * (j + 1))
            value = dot_cols(fa[:, at], ca[:, cols]) + dot_cols(fb[:, at], cb[:, cols])
            put(buf_l if j < 2 else buf_r, j % 2, value)
        cut = len(outs) // 2
        leave(moves, buf_l, outs[:cut], scal[6])
        leave(moves, buf_r, outs[cut:], scal[7])

    result = call(
        body, "att_grads", scal, [*facts, *cots], outputs(*left, *right),
        [FACTS_A] * 2 + [COT_ATT] * 2 + [left_buffer, right_buffer], 4 * ROWS * D * 4 * HALF,
    )
    cut = len(result) // 2
    return result[:cut], result[cut:]


TILE = 512


def lookup_kernel(count, last, hid, *rest):
    tables, rest = rest[:count], rest[count:]
    if last:
        m_in, l_in, a_in, mean_ref, unit_ref, lse_ref, m_ref, l_ref, acc = rest
    else:
        m_ref, l_ref, acc = rest
    step = pl.program_id(0)

    @pl.when(step == 0)
    def _():
        if last:
            m_ref[...] = m_in[...]
            l_ref[...] = l_in[...]
            acc[...] = a_in[...]
        else:
            m_ref[...] = jnp.full((ROWS, 1), MASKED, F32)
            l_ref[...] = jnp.zeros((ROWS, 1), F32)
            acc[...] = jnp.zeros((ROWS, D), F32)

    scores = [dot_rows(hid[...], table[...]) * D**-0.5 for table in tables]
    top = m_ref[...]
    for s in scores:
        top = jnp.maximum(top, jnp.max(s, axis=-1, keepdims=True))
    fade = jnp.exp(m_ref[...] - top)
    m_ref[...] = top
    total_l = l_ref[...] * fade
    total_a = acc[...] * fade
    for s, table in zip(scores, tables):
        p = jnp.exp(s - top)
        total_l = total_l + jnp.sum(p, axis=-1, keepdims=True)
        high = p.astype(BF16)
        low = (p - high.astype(F32)).astype(BF16)
        total_a = total_a + dot(high, table[...]) + dot(low, table[...])
    l_ref[...] = total_l
    acc[...] = total_a
    if last:
        @pl.when(step == pl.num_programs(0) - 1)
        def _():
            totals = l_ref[...]
            mean_code = acc[...] / totals
            mean_ref[...] = mean_code
            unit_ref[...] = mean_code * lax.rsqrt(
                jnp.mean(mean_code * mean_code, axis=-1, keepdims=True) + EPS
            )
            lse_ref[...] = m_ref[...] + jnp.log(totals)


def fixed(s):
    return pl.BlockSpec(s, lambda i, *_: (0,) * len(s))


def lookup_cost(work):
    return pl.CostEstimate(flops=6 * ROWS * D * work, bytes_accessed=2 * work * D, transcendentals=ROWS * work)


def lookup(hidden, tables, state=None):
    last = state is not None
    rows = tables[0].shape[0]
    tile = min(TILE, rows)
    col, mat = (ROWS, 1), (ROWS, D)
    if last:
        outs = [mat, mat, col]
        scratch = [pltpu.VMEM(col, F32), pltpu.VMEM(col, F32), pltpu.VMEM(mat, F32)]
    else:
        outs, scratch = [col, col, mat], []
    return pl.pallas_call(
        partial(lookup_kernel, len(tables), last),
        grid=(rows // tile,),
        in_specs=[fixed(mat)]
        + [pl.BlockSpec((tile, D), lambda i: (i, 0))] * len(tables)
        + ([fixed(col), fixed(col), fixed(mat)] if last else []),
        out_specs=[fixed(o) for o in outs],
        out_shape=[shape(o, F32) for o in outs],
        scratch_shapes=scratch,
        compiler_params=pltpu.CompilerParams(vmem_limit_bytes=ROOM),
        cost_estimate=lookup_cost(rows * len(tables)),
        name=f"lookup_{int(last)}",
    )(hidden, *tables, *(state if last else ()))


def lookup_back_kernel(scal, hid, code, lse, inner, *rest):
    tables, (out, keep, send) = rest[:-3], rest[-3:]
    step = pl.program_id(0)

    @pl.when(step == 0)
    def _():
        out[...] = jnp.zeros_like(out)

    gained = out[...]
    for table in tables:
        s = dot_rows(hid[...], table[...]) * D**-0.5
        p = jnp.exp(s - lse[...])
        dp = dot_rows(code[...], table[...])
        ds = (p * (dp - inner[...])).astype(BF16)
        gained = gained + dot(ds, table[...])
    out[...] = gained

    @pl.when(step == pl.num_programs(0) - 1)
    def _():
        value = out[...] * D**-0.5
        out[...] = value
        low = value.astype(BF16)
        for half in range(2):
            part = low[:, HALF * half : HALF * (half + 1)]

            @pl.when(scal[0] == half)
            def _():
                keep[...] = part

            @pl.when(scal[0] != half)
            def _():
                send[...] = part


def lookup_back(scal, hidden, code, lse, inner, tables):
    rows = tables[0].shape[0]
    tile = min(TILE, rows)
    col, mat, part = (ROWS, 1), (ROWS, D), (ROWS, HALF)
    return pl.pallas_call(
        lookup_back_kernel,
        grid_spec=pltpu.PrefetchScalarGridSpec(
            num_scalar_prefetch=1,
            grid=(rows // tile,),
            in_specs=[fixed(mat), fixed(mat), fixed(col), fixed(col)]
            + [pl.BlockSpec((tile, D), lambda i, *_: (i, 0))] * len(tables),
            out_specs=[fixed(mat), fixed(part), fixed(part)],
        ),
        out_shape=[shape(mat, F32), shape(part, BF16), shape(part, BF16)],
        compiler_params=pltpu.CompilerParams(vmem_limit_bytes=ROOM),
        cost_estimate=lookup_cost(rows * len(tables)),
        name="lookup_back",
    )(scal, hidden, code, lse, inner, *tables)


def swapped(value):
    return lax.ppermute(value, "section", [(0, 1), (1, 0)])


def bit_count():
    size = lax.axis_size("dp")
    count = size.bit_length() - 1
    assert size == 1 << count
    return count


def along(value, bit):
    size = lax.axis_size("dp")
    return lax.ppermute(value, "dp", [(i, i ^ (1 << bit)) for i in range(size)])


def after(value, *others):
    return lax.optimization_barrier((value, *others))[0]


def total(terms):
    summed = terms[0].astype(F32)
    for term in terms[1:]:
        summed = summed + term.astype(F32)
    return summed


class Share:
    def __init__(self, parts, first):
        count = bit_count()
        order = [first, 1 - first] if count > 1 else [0]
        self.order = order + list(range(len(order), count))
        self.live = list(range(count))[::-1]
        self.ready = None
        if len(parts) == 2:
            self.live.remove(first)
            self.ready = parts[1]
        self.terms = [self.laid(parts[0])]

    def laid(self, value):
        return value.reshape(value.shape[:1] + (2,) * len(self.live) + (-1, HALF))

    def split(self, stage):
        if stage == 0 and self.ready is not None:
            return self.ready
        bit = self.order[stage]
        axis = 1 + self.live.index(bit)
        mine = (lax.axis_index("dp") >> bit) & 1

        def pick(which):
            return [lax.dynamic_index_in_dim(t, which, axis, keepdims=False) for t in self.terms]

        sent = total(pick(1 - mine)).astype(BF16)
        self.terms = pick(mine)
        self.live.remove(bit)
        return sent

    def send(self, stage):
        self.sent = self.split(stage)
        self.got = along(self.sent, self.order[stage])

    def receive(self, *values):
        self.terms.append(self.laid(after(self.got, *values)))


class Pair:
    def __init__(self, left, right):
        self.shares = [left, right]
        self.order = left.order

    def send(self, stage):
        if stage < 2:
            for share in self.shares:
                share.send(stage)
            self.sent = [share.sent for share in self.shares]
        else:
            self.sent = [jnp.stack([share.split(stage) for share in self.shares])]
            self.got = along(self.sent[0], self.order[stage])

    def receive(self, stage, *values):
        if stage < 2:
            for share in self.shares:
                share.receive(*values)
        else:
            got = after(self.got, *values)
            for i, share in enumerate(self.shares):
                share.terms.append(share.laid(got[i]))

    def result(self):
        return jnp.stack([total(share.terms) for share in self.shares])


def per_device(
    patches,
    recon_cot,
    lengths,
    codebook,
    w_qkv,
    w_out,
    w_up,
    w_down,
    norm_gain,
    norm_bias,
    bias_out,
    bias_up,
):
    section = lax.axis_index("section")
    on_first = section == 0
    size = lax.axis_size("dp")
    count = bit_count()
    me = lax.axis_index("dp")
    lens = lax.dynamic_index_in_dim(lengths, section, 0, keepdims=False)
    place = jnp.stack([section, jnp.int32(0), me & 1, (me >> 1) & 1]).astype(jnp.int32)
    scal = jnp.concatenate([place[:1], lens, place[1:]])
    own_small = jnp.concatenate([norm_gain[0], norm_bias[0], bias_out[0], bias_up.reshape(-1, D)])
    small_other = swapped(own_small)
    small = [jnp.where(on_first, own_small, small_other), jnp.where(on_first, small_other, own_small)]
    weights = [(w[0], swapped(w[0])) for w in (w_qkv, w_out, w_up, w_down)]

    table = codebook
    for bit in range(count - 1, 1, -1):
        got = along(table, bit)
        table = jnp.concatenate([table, got])
    facts_ea, qkv_e, probs_e = att_forward(0, after(scal, table), patches, small[0], weights)
    half = table.shape[0] // 2
    pieces = [table[:half], table[half:]]
    got = [after(along(piece, bit), facts_ea) for piece, bit in zip(pieces, (1, 0))]
    pieces = [jnp.concatenate(pair) for pair in zip(pieces, got)]
    pieces_other = [swapped(piece) for piece in pieces]
    late = [along(piece, bit) for piece, bit in zip(pieces, (0, 1))]
    hidden, facts_ef, resid_e, slope_e = ffn_forward(
        0, after(scal, *pieces), patches, small[0], facts_ea, weights
    )
    state = lookup(hidden, pieces + pieces_other)
    late = after(late, state[0])
    late_other = [swapped(piece) for piece in late]
    tables = pieces + pieces_other + late + late_other
    mean_code, unit, lse = lookup(hidden, late + late_other, state)
    facts_ea = (facts_ea, swapped(after(facts_ea, lse)))
    facts_ef = (facts_ef, swapped(after(facts_ef, lse)))
    recon, facts_df, facts_da, qkv_d, probs_d, resid_d, slope_d = block_forward(
        1, scal, unit, small[1], weights
    )
    facts_df = (facts_df, swapped(facts_df))
    facts_da = (facts_da, swapped(facts_da))
    recon_first = lax.ppermute(recon, "section", [(0, 1)])
    lse_other = swapped(lse)

    keep, send, d_resid, sums_df = ffn_backward(
        1, scal, recon_cot, slope_d, resid_d, small[1], weights, True
    )
    got = swapped(send)
    left = Share(down_grads(after(scal, keep), facts_df, [recon_cot], count, True), 0)
    left.send(0)
    right = Share(up_grads(after(scal, left.sent), facts_df, (keep, got), count), 1)
    right.send(0)
    first_f = Pair(left, right)
    keep, send, sums_da, code, inner = att_backward(
        1, after(scal, right.sent), d_resid, qkv_d, probs_d, unit, small[1], weights, mean_code
    )
    got = swapped(send)
    d_hidden, g_keep, g_send = lookup_back(scal, hidden, code, lse, inner, tables)
    g_got = swapped(g_send)
    left, right = att_grads(after(scal, d_hidden), facts_da, (keep, got), count)
    first_f.receive(0, left[0])
    first_f.send(1)
    first_a = Pair(Share(left, 0), Share(right, 1))
    first_a.send(0)
    keep, send, d_resid, sums_ef = ffn_backward(
        0, after(scal, *first_f.sent, *first_a.sent), d_hidden, slope_e, resid_e, small[0], weights, False
    )
    got = swapped(send)
    left = Share(down_grads(after(scal, keep), facts_ef, (g_keep, g_got), count, False), 0)
    left.send(0)
    first_f.receive(1, left.sent)
    first_f.send(2)
    first_a.receive(0, *first_f.sent)
    first_a.send(1)
    right = Share(up_grads(after(scal, *first_a.sent), facts_ef, (keep, got), count), 1)
    right.send(0)
    second_f = Pair(left, right)
    keep, send, sums_ea, grad_x = att_backward(
        0, after(scal, right.sent), d_resid, qkv_e, probs_e, patches, small[0], weights
    )
    got = swapped(send)
    sums = jnp.stack([jnp.concatenate([sums_ef, sums_ea[:2]]), jnp.concatenate([sums_df, sums_da[:2]])])
    sums_got = swapped(jnp.where(on_first, sums[1], sums[0]))
    first_f.receive(2, sums_ea)
    first_f.send(3)
    first_a.receive(1, *first_f.sent)
    sums = jnp.where(on_first, sums[0], sums[1]) + after(sums_got, *first_f.sent)
    sums_got = along(sums, 0)
    first_a.send(2)
    left, right = att_grads(after(scal, sums, *first_a.sent), facts_ea, (keep, got), count)
    sums = sums + after(sums_got, left[0])
    sums_got = along(sums, 1)
    second_a = Pair(Share(left, 0), Share(right, 1))
    second_f.receive(0, sums)
    second_f.send(1)
    second_a.send(0)
    first_a.receive(2, *second_a.sent, *second_f.sent)
    first_a.send(3)
    for bit in range(2, count):
        sums = sums + after(sums_got, *first_a.sent)
        sums_got = along(sums, bit)
    grad_second = lax.ppermute(after(grad_x, *first_a.sent), "section", [(1, 0)])
    second_f.receive(1, *first_a.sent)
    second_f.send(2)
    last = second_f.sent
    for stage in range(count):
        second_a.receive(stage, *last)
        if stage + 1 < count:
            second_a.send(stage + 1)
            last = second_a.sent
        if stage + 2 < count:
            second_f.receive(stage + 2, *last)
            if stage + 3 < count:
                second_f.send(stage + 3)
                last = second_f.sent
        if stage == 0:
            for more in range(3, count):
                first_f.receive(more, *last)
                if more + 1 < count:
                    first_f.send(more + 1)
                    last = first_f.sent
                first_a.receive(more, *last)
                if more + 1 < count:
                    first_a.send(more + 1)
                    last = first_a.sent
    ffn_d, att_d, ffn_e, att_e = [pair.result() for pair in (first_f, first_a, second_f, second_a)]

    def own_halves(enc, dec):
        kept = jnp.where(on_first, enc, dec)
        got = swapped(jnp.where(on_first, dec, enc))
        return jnp.where(on_first, kept, got), jnp.where(on_first, got, kept)

    ffn = jnp.stack(own_halves(ffn_e, ffn_d))
    att = jnp.stack(own_halves(att_e, att_d)).reshape(2, 4, -1, HALF)
    width = D // size
    grad_down = ffn[:, 0].reshape(2, 4 * width, HALF).swapaxes(0, 1).reshape(1, 4 * width, D)
    grad_up = ffn[:, 1].transpose(2, 0, 1, 3).reshape(1, width, FF)
    grad_qkv = att[:, :3].transpose(2, 0, 1, 3).reshape(1, width, 3 * D)
    grad_out = att[:, 3].swapaxes(0, 1).reshape(1, width, D)

    cols = me * width
    sums = sums + after(sums_got, last)
    rows = lax.dynamic_slice_in_dim(sums, cols, width, axis=1)
    grad_gain = jnp.stack([rows[8], rows[0]])[None]
    grad_nbias = jnp.stack([rows[9], rows[1]])[None]
    grad_bout = jnp.stack([rows[3], rows[2]])[None]
    grad_bup = lax.dynamic_slice_in_dim(sums[4:8].reshape(FF), cols * 4, width * 4)[None]

    ends = jnp.where(
        on_first, jnp.concatenate([grad_x, grad_second]), jnp.concatenate([recon_first, recon])
    )[None]
    lse, lse_other = lse[:, 0], lse_other[:, 0]
    codes = jnp.where(on_first, jnp.concatenate([lse, lse_other]), jnp.concatenate([lse_other, lse]))
    return (ends, codes, grad_qkv, grad_out, grad_up, grad_down, grad_gain, grad_nbias, grad_bout, grad_bup)


def solution(mesh):
    placed = (
        P("dp", None),
        P("dp", None),
        P("dp", None),
        P(("dp", "section"), None),
        P("section", None, None),
        P("section", None, None),
        P("section", None, None),
        P("section", None, None),
        P("section", None, None),
        P("section", None, None),
        P("section", None, None),
        P("section", None),
    )
    return jax.shard_map(
        per_device,
        mesh=mesh,
        in_specs=placed,
        out_specs=(
            P("section", "dp", None),
            P("dp"),
            P("section", "dp", None),
            P("section", "dp", None),
            P("section", "dp", None),
            P("section", "dp", None),
            P("section", None, "dp"),
            P("section", None, "dp"),
            P("section", None, "dp"),
            P("section", "dp"),
        ),
        check_vma=False,
    )
```

```python
from functools import partial

import jax
import jax.numpy as jnp
from jax import lax
from jax.experimental import pallas as pl
from jax.experimental.pallas import tpu as pltpu
from jax.sharding import PartitionSpec as P

D = 768
HEADS = 12
HD = 64
FF = 3072
ROWS = 256
PAIR = 2 * HD
EPS = 1e-06
MASKED = -1e30
F32 = jnp.float32
BF16 = jnp.bfloat16
N2, FFN_FACTS = FF, FF + D
MIX, ATT_FACTS = D, 2 * D
HALF = D // 2
HALF_UP = FF // 2
HALF_QKV = 3 * D // 2
TAIL_P = 0.35
TAIL = (0.19620077326315646, 0.2185939781557991, 0.05480664657447366, 0.5651487076988272,
        -0.5574354264567037, 0.7060774515721405, -0.18339209581143395)
VMEM = pl.BlockSpec(memory_space=pltpu.VMEM)
SMEM = pl.BlockSpec(memory_space=pltpu.SMEM)
ANY = pl.BlockSpec(memory_space=pl.ANY)
ROOM = 58 * 1024 * 1024


def dot(a, b):
    return jnp.dot(a, b, preferred_element_type=F32)


def dot_rows(a, b):
    return lax.dot_general(a, b, (((1,), (1,)), ((), ())), preferred_element_type=F32)


def dot_cols(a, b):
    return lax.dot_general(a, b, (((0,), (0,)), ((), ())), preferred_element_type=F32)


def unit_rows(values):
    centre = values - jnp.mean(values, axis=-1, keepdims=True)
    inverse = lax.rsqrt(jnp.mean(centre * centre, axis=-1, keepdims=True) + EPS)
    return centre * inverse, inverse


def norm_back(scaled, unit, inverse):
    return inverse * (
        scaled
        - jnp.mean(scaled, axis=-1, keepdims=True)
        - unit * jnp.mean(scaled * unit, axis=-1, keepdims=True)
    )


def gelu_parts(z):
    bell = jnp.exp(-0.5 * z * z)
    t = 1.0 / (1.0 + (TAIL_P * 0.5**0.5) * jnp.abs(z))
    poly = TAIL[6] * t + TAIL[5]
    for c in TAIL[4::-1]:
        poly = poly * t + c
    tail = 0.5 * poly * t * bell
    cdf = jnp.where(z >= 0, 1.0 - tail, tail)
    return z * cdf, cdf + z * bell * 0.3989422804014327


def image_ids(scal, lens, shape, axis):
    position = lax.broadcasted_iota(jnp.int32, shape, axis)
    limit = jnp.int32(0)
    ids = jnp.zeros(shape, jnp.int32)
    for i in range(4):
        limit = limit + lens[scal[0], i]
        ids = ids + (position >= limit).astype(jnp.int32)
    return ids


def shape(s, t):
    return jax.ShapeDtypeStruct(s, t)


class Moves:
    def __init__(self, sems):
        self.sems = sems
        self.used = 0
        self.leaving = []

    def sem(self):
        self.used += 1
        return self.sems.at[self.used - 1]

    def load(self, src, dst):
        copy = pltpu.make_async_copy(src, dst, self.sem())
        copy.start()
        return copy.wait

    def load_either(self, first, src, other, dst):
        sem = self.sem()
        for take, ref in ((first, src), (jnp.logical_not(first), other)):
            @pl.when(take)
            def _():
                pltpu.make_async_copy(ref, dst, sem).start()

        return pltpu.make_async_copy(src, dst, sem).wait

    def load_tiles(self, first, src, other, dst, axis):
        tiles = []
        for j in range(dst.shape[axis] // D):
            at = (pl.ds(D * j, D),) if axis == 0 else (slice(None), pl.ds(D * j, D))
            tiles.append((at, self.sem()))
        for take, ref in ((first, src), (jnp.logical_not(first), other)):
            @pl.when(take)
            def _():
                for at, sem in tiles:
                    pltpu.make_async_copy(ref.at[at], dst.at[at], sem).start()

        return [pltpu.make_async_copy(src.at[at], dst.at[at], sem).wait for at, sem in tiles]

    def store(self, src, dst):
        copy = pltpu.make_async_copy(src, dst, self.sem())
        copy.start()
        self.leaving.append(copy.wait)

    def finish(self):
        for wait in self.leaving:
            wait()


SEMS = 32
SMALL_COST = pl.CostEstimate(flops=1000, bytes_accessed=1000, transcendentals=0)


def call(body, name, scal, inputs, outs, scratch, small=None):
    extra = () if small is None else small[1:]

    def kernel(*refs):
        scal, *refs = refs
        moves = Moves(refs[-1])
        if small is None:
            body(moves, scal, *refs[:-1])
        else:
            lens, own, other, *refs = refs
            chosen = refs[-2]
            chosen[...] = jnp.where(scal[0] == small[0], own[...], other[...])
            body(moves, scal, lens, chosen, *refs[:-2])
        moves.finish()

    return pl.pallas_call(
        kernel,
        in_specs=[SMEM] + [SMEM, VMEM, VMEM][: len(extra)] + [ANY] * len(inputs),
        out_specs=[ANY] * len(outs),
        out_shape=outs,
        scratch_shapes=[
            *(pltpu.VMEM(s, t) for s, t in (*scratch, *([SMALL] if extra else []))),
            pltpu.SemaphoreType.DMA((SEMS,)),
        ],
        compiler_params=pltpu.CompilerParams(vmem_limit_bytes=ROOM),
        cost_estimate=SMALL_COST,
        name=name,
    )(scal, *extra, *inputs)


SMALL = ((10, D), F32)
W_QKV = ((D, 3 * D), BF16)
W_OUT = ((D, D), BF16)
W_UP = ((D, FF), BF16)
W_DOWN = ((FF, D), BF16)
MAT = ((ROWS, D), F32)
LOW = ((ROWS, D), BF16)
COL = ((ROWS, 1), F32)


def rows_of(scal, own=True):
    which = scal[0] if own else 1 - scal[0]
    return pl.ds(pl.multiple_of(which * ROWS, ROWS), ROWS)


def half_of(scal, width, own=True):
    which = scal[0] if own else 1 - scal[0]
    return pl.ds(pl.multiple_of(which * width, 128), width)


def pack_small(gains, shifts, bias_out, bias_up):
    def kernel(gains, shifts, bias_out, bias_up, out):
        for i, ref in enumerate((gains, shifts, bias_out)):
            out[2 * i : 2 * i + 2, :] = ref[0]
        for j in range(FF // D):
            out[6 + j : 7 + j, :] = bias_up[:, D * j : D * (j + 1)]

    return pl.pallas_call(
        kernel, in_specs=[VMEM] * 4, out_specs=VMEM, out_shape=shape(*SMALL), cost_estimate=SMALL_COST, name="pack_small",
    )(gains, shifts, bias_out, bias_up)


def att_forward_part(moves, scal, lens, x, small, wq, wait, facts, qkv, probs, out):
    facts_hbm, qkv_hbm, probs_hbm = out
    unit, _ = unit_rows(x)
    n1 = (unit * small[0:1, :] + small[2:3, :]).astype(BF16)
    facts[:, :D] = n1
    same = image_ids(scal, lens, (ROWS, ROWS), 0) == image_ids(scal, lens, (ROWS, ROWS), 1)
    bias = jnp.where(same, 0.0, MASKED)
    first = lax.broadcasted_iota(jnp.int32, (1, PAIR), 1) < HD
    for j in range(3):
        wait[j]()
        qkv[:, D * j : D * (j + 1)] = dot(n1, wq[:, D * j : D * (j + 1)]).astype(BF16)
    moves.store(qkv, qkv_hbm)
    for p in range(HEADS // 2):
        q = qkv[:, PAIR * p : PAIR * (p + 1)] * jnp.asarray(HD**-0.5, BF16)
        k = qkv[:, D + PAIR * p : D + PAIR * (p + 1)]
        v = qkv[:, 2 * D + PAIR * p : 2 * D + PAIR * (p + 1)]
        outs = []
        for side in range(2):
            own = first if side == 0 else jnp.logical_not(first)
            s = dot_rows(jnp.where(own, q, jnp.zeros_like(q)), k) + bias
            s = jnp.exp(s - jnp.max(s, axis=-1, keepdims=True))
            pr = (s * (1.0 / jnp.sum(s, axis=-1, keepdims=True))).astype(BF16)
            probs[2 * p + side] = pr
            outs.append(dot(pr, v))
        facts[:, MIX + PAIR * p : MIX + PAIR * (p + 1)] = jnp.where(first, outs[0], outs[1]).astype(BF16)
    moves.store(probs, probs_hbm)
    moves.store(facts, facts_hbm)


def ffn_forward_part(moves, x, small, mixed, wo, wu, wd, waits, facts, resid_ref, slope, y_ref, out):
    y_hbm, facts_hbm, resid_hbm, slope_hbm = out
    waits[0]()
    resid = x + dot(mixed, wo[...]) + small[4:5, :]
    resid_ref[...] = resid
    moves.store(resid_ref, resid_hbm)
    unit, _ = unit_rows(resid)
    n2 = (unit * small[1:2, :] + small[3:4, :]).astype(BF16)
    facts[:, N2 : N2 + D] = n2
    y = resid + small[5:6, :]
    tiles = FF // D

    def pre_tile(j):
        waits[1][j]()
        return dot(n2, wu[:, D * j : D * (j + 1)]) + small[6 + j : 7 + j, :]

    pre = pre_tile(0)
    for j in range(tiles):
        cols = slice(D * j, D * (j + 1))
        waits[2][j]()
        later = pre_tile(j + 1) if j + 1 < tiles else None
        act, sl = gelu_parts(pre)
        act = act.astype(BF16)
        facts[:, cols] = act
        slope[:, cols] = sl.astype(BF16)
        y = y + dot(act, wd[cols, :])
        pre = later
    moves.store(facts, facts_hbm)
    moves.store(slope, slope_hbm)
    y_ref[...] = y.astype(y_ref.dtype)
    moves.store(y_ref, y_hbm)


FACTS_A = ((ROWS, ATT_FACTS), BF16)
FACTS_F = ((ROWS, FFN_FACTS), BF16)
QKV = ((ROWS, 3 * D), BF16)
PROBS = ((HEADS, ROWS, ROWS), BF16)
SLOPE = ((ROWS, FF), BF16)


def outputs(*kinds):
    return [shape(*kind) for kind in kinds]


def block_forward(block, scal, x, small, weights):
    def body(moves, scal, lens, small, x_in, wq_a, wq_b, wo_a, wo_b, wu_a, wu_b, wd_a, wd_b,
             y_o, facts_fo, facts_ao, qkv_o, probs_o, resid_o, slope_o,
             x, wq, wo, wu, wd, y, facts_f, facts_a, qkv, probs, resid, slope):
        own = scal[0] == block
        wait_x = moves.load(x_in, x)
        wait_q = moves.load_tiles(own, wq_a, wq_b, wq, 1)
        waits = [moves.load_either(own, a, b, w) for a, b, w in ((wo_a, wo_b, wo), (wu_a, wu_b, wu), (wd_a, wd_b, wd))]
        waits = [waits[0]] + [[wait] + [lambda: None] * 3 for wait in waits[1:]]
        wait_x()
        xs = x[...]
        att_forward_part(moves, scal, lens, xs, small, wq, wait_q, facts_a, qkv, probs, (facts_ao, qkv_o, probs_o))
        ffn_forward_part(
            moves, xs, small, facts_a[:, MIX : MIX + D], wo, wu, wd, waits, facts_f, resid, slope, y,
            (y_o, facts_fo, resid_o, slope_o),
        )

    kinds = (MAT, FACTS_F, FACTS_A, QKV, PROBS, MAT, SLOPE)
    return call(
        body, f"forward_{block}", scal, [x, *sum(weights, ())], outputs(*kinds),
        [MAT, W_QKV, W_OUT, W_UP, W_DOWN, *kinds], (block, *small),
    )


def att_forward(block, scal, patches, small, weights):
    def body(moves, scal, lens, small, x_in, wq_a, wq_b, facts_o, qkv_o, probs_o, x, wq, facts, qkv, probs):
        wait_x = moves.load(x_in.at[rows_of(scal), :], x)
        wait_w = moves.load_tiles(scal[0] == block, wq_a, wq_b, wq, 1)
        wait_x()
        att_forward_part(
            moves, scal, lens, x[...].astype(F32), small, wq, wait_w, facts, qkv, probs, (facts_o, qkv_o, probs_o)
        )

    kinds = (FACTS_A, QKV, PROBS)
    return call(
        body, f"att_forward_{block}", scal, [patches, *weights[0]], outputs(*kinds),
        [LOW, W_QKV, *kinds], (block, *small),
    )


def ffn_forward(block, scal, patches, small, facts_a, weights):
    def body(moves, scal, lens, small, x_in, facts_ai, wo_a, wo_b, wu_a, wu_b, wd_a, wd_b,
             y_o, facts_o, resid_o, slope_o, x, mixed, wo, wu, wd, y, facts, resid, slope):
        own = scal[0] == block
        wait_x = moves.load(x_in.at[rows_of(scal), :], x)
        wait_m = moves.load(facts_ai.at[:, pl.ds(MIX, D)], mixed)
        waits = [
            moves.load_either(own, wo_a, wo_b, wo),
            moves.load_tiles(own, wu_a, wu_b, wu, 1),
            moves.load_tiles(own, wd_a, wd_b, wd, 0),
        ]
        wait_x()
        wait_m()
        ffn_forward_part(
            moves, x[...].astype(F32), small, mixed[...], wo, wu, wd, waits, facts, resid, slope, y,
            (y_o, facts_o, resid_o, slope_o),
        )

    kinds = (LOW, FACTS_F, MAT, SLOPE)
    return call(
        body, f"ffn_forward_{block}", scal, [patches, facts_a, *sum(weights[1:], ())], outputs(*kinds),
        [LOW, LOW, W_OUT, W_UP, W_DOWN, *kinds], (block, *small),
    )


COT_UP = ((ROWS, HALF_UP), BF16)
COT_ATT = ((ROWS, HALF_QKV + HALF), BF16)
SUMS = ((8, D), F32)


def ffn_backward(block, scal, g, slope, resid, small, weights, own_rows):
    def body(moves, scal, lens, small, g_in, slope_in, resid_in, wu_a, wu_b, wd_a, wd_b,
             keep_o, send_o, dres_o, sums, g_ref, slope, resid, wu, wd, d_pre_ref, dres):
        own = scal[0] == block
        wait_g = moves.load(g_in.at[rows_of(scal), :] if own_rows else g_in, g_ref)
        wait_d = moves.load_tiles(own, wd_a, wd_b, wd, 0)
        wait_s = moves.load(slope_in, slope)
        wait_u = moves.load_tiles(own, wu_a, wu_b, wu, 1)
        wait_r = moves.load(resid_in, resid)
        wait_g()
        g = g_ref[...].astype(F32)
        gl = g.astype(BF16)
        small_sums = [None] * 4
        small_sums[2] = jnp.sum(g, axis=0, keepdims=True)
        d_n2 = jnp.zeros((ROWS, D), F32)
        up_sums = []
        tiles = FF // D

        def act_tile(j):
            wait_d[j]()
            return dot_rows(gl, wd[D * j : D * (j + 1), :])

        later = act_tile(0)
        wait_s()
        for j in range(tiles):
            cols = slice(D * j, D * (j + 1))
            wait_u[j]()
            d_act = later
            later = act_tile(j + 1) if j + 1 < tiles else None
            d_pre = (d_act * slope[:, cols].astype(F32)).astype(BF16)
            d_pre_ref[:, cols] = d_pre
            up_sums.append(jnp.sum(d_pre.astype(F32), axis=0, keepdims=True))
            d_n2 = d_n2 + dot_rows(d_pre, wu[:, cols])
        moves.store(d_pre_ref.at[:, half_of(scal, HALF_UP)], keep_o)
        moves.store(d_pre_ref.at[:, half_of(scal, HALF_UP, False)], send_o)
        wait_r()
        unit, inverse = unit_rows(resid[...])
        small_sums[0] = jnp.sum(d_n2 * unit, axis=0, keepdims=True)
        small_sums[1] = jnp.sum(d_n2, axis=0, keepdims=True)
        d_resid = g + norm_back(d_n2 * small[1:2, :], unit, inverse)
        dres[...] = d_resid
        moves.store(dres, dres_o)
        small_sums[3] = jnp.sum(d_resid, axis=0, keepdims=True)
        for i, value in enumerate(small_sums + up_sums):
            sums[i : i + 1, :] = value

    def with_sums(moves, *refs):
        *head, sums_buffer = refs
        sums_o = head[13]
        head[13] = sums_buffer
        body(moves, *head)
        moves.store(sums_buffer, sums_o)

    g_kind = (tuple(g.shape), g.dtype) if not own_rows else ((ROWS, D), g.dtype)
    return call(
        with_sums, f"ffn_backward_{block}", scal, [g, slope, resid, *weights[2], *weights[3]],
        outputs(COT_UP, COT_UP, MAT, SUMS),
        [g_kind, SLOPE, MAT, W_UP, W_DOWN, SLOPE, MAT, SUMS], (block, *small),
    )


def att_backward(block, scal, d_resid, qkv, probs, x, small, weights, mean_code=None):
    final = mean_code is None

    def body(moves, scal, lens, small, dres_in, qkv_in, probs_in, x_in, wq_a, wq_b, wo_a, wo_b, *rest):
        if final:
            keep_o, send_o, sums_o, gx_o, dres, qkv, probs, x_ref, wq, wo, d_qkv, rl_ref, sums, gx = rest
        else:
            (mean_in, keep_o, send_o, sums_o, code_o, inner_o,
             dres, qkv, probs, x_ref, wq, wo, d_qkv, rl_ref, sums, mean_ref, code_ref, inner_ref) = rest
        own = scal[0] == block
        wait_g = moves.load(dres_in, dres)
        wait_o = moves.load_either(own, wo_a, wo_b, wo)
        wait_k = moves.load(qkv_in, qkv)
        wait_p = moves.load(probs_in, probs)
        wait_q = moves.load_either(own, wq_a, wq_b, wq)
        wait_x = moves.load(x_in.at[rows_of(scal), :] if final else x_in, x_ref)
        if not final:
            wait_m = moves.load(mean_in, mean_ref)
        wait_g()
        d_resid = dres[...]
        rl = d_resid.astype(BF16)
        rl_ref[...] = rl
        for out, mine in ((keep_o, True), (send_o, False)):
            moves.store(rl_ref.at[:, half_of(scal, HALF, mine)], out.at[:, pl.ds(HALF_QKV, HALF)])
        first = lax.broadcasted_iota(jnp.int32, (1, PAIR), 1) < HD
        wait_o()
        d_mixed = dot_rows(rl, wo[...]).astype(BF16)
        wait_k()
        wait_p()
        scale = jnp.asarray(HD**-0.5, BF16)
        for p in range(HEADS // 2):
            q = qkv[:, PAIR * p : PAIR * (p + 1)] * scale
            k = qkv[:, D + PAIR * p : D + PAIR * (p + 1)]
            v = qkv[:, 2 * D + PAIR * p : 2 * D + PAIR * (p + 1)]
            dm = d_mixed[:, PAIR * p : PAIR * (p + 1)]
            dq, dk, dv = [], [], []
            for side in range(2):
                mine = first if side == 0 else jnp.logical_not(first)
                pr = probs[2 * p + side]
                dp = dot_rows(jnp.where(mine, dm, jnp.zeros_like(dm)), v)
                prf = pr.astype(F32)
                ds = (prf * (dp - jnp.sum(dp * prf, axis=-1, keepdims=True))).astype(BF16)
                dv.append(dot_cols(pr, dm))
                dq.append(dot(ds, k))
                dk.append(dot_cols(ds, q))
            for at, parts in ((0, dq), (D, dk), (2 * D, dv)):
                value = jnp.where(first, parts[0], parts[1])
                if at == 0:
                    value = value * HD**-0.5
                d_qkv[:, at + PAIR * p : at + PAIR * (p + 1)] = value.astype(BF16)
        for out, mine in ((keep_o, True), (send_o, False)):
            moves.store(d_qkv.at[:, half_of(scal, HALF_QKV, mine)], out.at[:, pl.ds(0, HALF_QKV)])
        wait_q()
        d_n1 = dot_rows(d_qkv[...], wq[...])
        wait_x()
        x = x_ref[...].astype(F32)
        unit, inverse = unit_rows(x)
        sums[0:1, :] = jnp.sum(d_n1 * unit, axis=0, keepdims=True)
        sums[1:2, :] = jnp.sum(d_n1, axis=0, keepdims=True)
        sums[2:8, :] = jnp.zeros((6, D), F32)
        moves.store(sums, sums_o)
        grad_x = d_resid + norm_back(d_n1 * small[0:1, :], unit, inverse)
        if final:
            gx[...] = grad_x
            moves.store(gx, gx_o)
        else:
            wait_m()
            mean_code = mean_ref[...]
            inv = lax.rsqrt(jnp.mean(mean_code * mean_code, axis=-1, keepdims=True) + EPS)
            code = inv * (grad_x - x * jnp.mean(grad_x * x, axis=-1, keepdims=True))
            code = code.astype(BF16)
            code_ref[...] = code
            moves.store(code_ref, code_o)
            inner_ref[...] = jnp.sum(code.astype(F32) * mean_code, axis=-1, keepdims=True)
            moves.store(inner_ref, inner_o)

    more_in, more = ([], [MAT]) if final else ([mean_code], [LOW, COL])
    return call(
        body, f"att_backward_{block}", scal, [d_resid, qkv, probs, x, *weights[0], *weights[1], *more_in],
        outputs(COT_ATT, COT_ATT, SUMS, *more),
        [MAT, QKV, PROBS, LOW if final else MAT, W_QKV, W_OUT, QKV, LOW, SUMS,
         *([] if final else [MAT]), *more],
        (block, *small),
    )


def split_kinds(kinds, bit, count):
    size = 1 << count
    width = D // size
    if width % 16:
        return None
    high = size >> (bit + 1)
    return (kinds, high, 2, 1 << bit, width, HALF), (kinds, high, 1 << bit, width, HALF)


def group_outputs(kinds, bit, count):
    split = split_kinds(kinds, bit, count)
    if split is None:
        return [((kinds, D, HALF), BF16)], ((kinds, D, HALF), BF16)
    return [(split[1], BF16)] * 2, (split[0], BF16)


def put(buffer, kind, value):
    buffer[kind] = value.astype(BF16).reshape(buffer.shape[1:])


def leave(moves, buffer, outs, mine):
    if len(outs) == 1:
        moves.store(buffer, outs[0])
    else:
        moves.store(buffer.at[:, :, mine], outs[0])
        moves.store(buffer.at[:, :, 1 - mine], outs[1])


def ffn_grads(scal, facts, cots, outs_g, count, both):
    down, down_buffer = group_outputs(FF // D, 0, count)
    up, up_buffer = group_outputs(HALF_UP // HALF, 1, count)
    width = D >> count
    given = 4 + len(outs_g)

    def body(moves, scal, *refs):
        ins, outs, (fa, fb, ca, cb, ga, gb, buf_d, buf_u) = refs[:given], refs[given:-8], refs[-8:]
        if both:
            wait_g = [
                moves.load(ins[4].at[rows_of(scal, own), half_of(scal, HALF)], g)
                for g, own in ((ga, True), (gb, False))
            ]
        else:
            wait_g = [moves.load(ref, g) for ref, g in zip(ins[4:], (ga, gb))]
        wait_f = []
        for j in range(FFN_FACTS // D):
            cols = pl.ds(D * j, D)
            wait_f.append([moves.load(src.at[:, cols], dst.at[:, cols]) for src, dst in zip(ins, (fa, fb))])
        wait_c = [moves.load(ref, c) for ref, c in zip(ins[2:4], (ca, cb))]
        for wait in wait_g:
            wait()
        for j in range(FF // D):
            cols = slice(D * j, D * (j + 1))
            for wait in wait_f[j]:
                wait()
            value = dot_cols(fa[:, cols], ga[...]) + dot_cols(fb[:, cols], gb[...])
            value = value.astype(BF16)
            owners = value.reshape(D // (4 * width), 4, width, HALF)
            for kind in range(4):
                part = owners[:, kind]
                if len(down) == 1:
                    rows = D // 4
                    buf_d[kind, rows * j : rows * (j + 1), :] = part.reshape(rows, HALF)
                else:
                    high = part.shape[0] // 2
                    buf_d[kind, high * j : high * (j + 1)] = part.reshape((high, 2, 1, width, HALF))
        leave(moves, buf_d, outs[: len(down)], scal[1])
        for wait in wait_f[-1] + wait_c:
            wait()
        n2 = slice(N2, N2 + D)
        for j in range(HALF_UP // HALF):
            cols = slice(HALF * j, HALF * (j + 1))
            put(buf_u, j, dot_cols(fa[:, n2], ca[:, cols]) + dot_cols(fb[:, n2], cb[:, cols]))
        leave(moves, buf_u, outs[len(down) :], scal[2])

    result = call(
        body, "ffn_grads", scal, [*facts, *cots, *outs_g], outputs(*down, *up),
        [FACTS_F] * 2 + [COT_UP] * 2 + [((ROWS, HALF), BF16)] * 2 + [down_buffer, up_buffer],
    )
    return result[: len(down)], result[len(down) :]


def att_grads(scal, facts, cots, count):
    left, left_buffer = group_outputs(2, 0, count)
    right, right_buffer = group_outputs(2, 1, count)

    def body(moves, scal, *refs):
        ins, outs, (fa, fb, ca, cb, buf_l, buf_r) = refs[:4], refs[4:-6], refs[-6:]
        waits = [moves.load(src, dst) for src, dst in zip(ins, (fa, fb, ca, cb))]
        for wait in waits:
            wait()
        for j in range(4):
            at = slice(0, D) if j < 3 else slice(MIX, MIX + D)
            cols = slice(HALF * j, HALF * (j + 1))
            value = dot_cols(fa[:, at], ca[:, cols]) + dot_cols(fb[:, at], cb[:, cols])
            put(buf_l if j < 2 else buf_r, j % 2, value)
        cut = len(outs) // 2
        leave(moves, buf_l, outs[:cut], scal[1])
        leave(moves, buf_r, outs[cut:], scal[2])

    result = call(
        body, "att_grads", scal, [*facts, *cots], outputs(*left, *right),
        [FACTS_A] * 2 + [COT_ATT] * 2 + [left_buffer, right_buffer],
    )
    cut = len(result) // 2
    return result[:cut], result[cut:]


def finish_att(scal, kept, got):
    width = kept.shape[2]

    def kernel(scal, kept, got, qkv, out):
        mine = scal[0] == 0
        for half in range(2):
            for j in range(4):
                a, b = kept[j // 2, j % 2], got[j // 2, j % 2]
                value = jnp.where(mine, a, b) if half == 0 else jnp.where(mine, b, a)
                if j < 3:
                    at = HALF_QKV * half + HALF * j
                    qkv[0, :, at : at + HALF] = value
                else:
                    out[0, :, HALF * half : HALF * (half + 1)] = value

    return pl.pallas_call(
        kernel,
        in_specs=[SMEM, VMEM, VMEM],
        out_specs=[VMEM] * 2,
        out_shape=[shape((1, width, 3 * D), F32), shape((1, width, D), F32)],
        cost_estimate=SMALL_COST,
        name="finish_att",
    )(scal, kept, got)


TILE = 512


def lookup_kernel(count, last, hid, *rest):
    tables, rest = rest[:count], rest[count:]
    if last:
        m_in, l_in, a_in, mean_ref, unit_ref, lse_ref, m_ref, l_ref, acc = rest
    else:
        m_ref, l_ref, acc = rest
    step = pl.program_id(0)

    @pl.when(step == 0)
    def _():
        if last:
            m_ref[...] = m_in[...]
            l_ref[...] = l_in[...]
            acc[...] = a_in[...]
        else:
            m_ref[...] = jnp.full((ROWS, 1), MASKED, F32)
            l_ref[...] = jnp.zeros((ROWS, 1), F32)
            acc[...] = jnp.zeros((ROWS, D), F32)

    scores = [dot_rows(hid[...], table[...]) * D**-0.5 for table in tables]
    top = m_ref[...]
    for s in scores:
        top = jnp.maximum(top, jnp.max(s, axis=-1, keepdims=True))
    fade = jnp.exp(m_ref[...] - top)
    m_ref[...] = top
    total_l = l_ref[...] * fade
    total_a = acc[...] * fade
    for s, table in zip(scores, tables):
        p = jnp.exp(s - top)
        total_l = total_l + jnp.sum(p, axis=-1, keepdims=True)
        high = p.astype(BF16)
        low = (p - high.astype(F32)).astype(BF16)
        total_a = total_a + dot(high, table[...]) + dot(low, table[...])
    l_ref[...] = total_l
    acc[...] = total_a
    if last:
        @pl.when(step == pl.num_programs(0) - 1)
        def _():
            totals = l_ref[...]
            mean_code = acc[...] / totals
            mean_ref[...] = mean_code
            unit_ref[...] = mean_code * lax.rsqrt(
                jnp.mean(mean_code * mean_code, axis=-1, keepdims=True) + EPS
            )
            lse_ref[...] = m_ref[...] + jnp.log(totals)


def fixed(s):
    return pl.BlockSpec(s, lambda i, *_: (0,) * len(s))


def lookup(hidden, tables, state=None):
    last = state is not None
    rows = tables[0].shape[0]
    tile = min(TILE, rows)
    col, mat = (ROWS, 1), (ROWS, D)
    if last:
        outs = [mat, mat, col]
        scratch = [pltpu.VMEM(col, F32), pltpu.VMEM(col, F32), pltpu.VMEM(mat, F32)]
    else:
        outs, scratch = [col, col, mat], []
    return pl.pallas_call(
        partial(lookup_kernel, len(tables), last),
        grid=(rows // tile,),
        in_specs=[fixed(mat)]
        + [pl.BlockSpec((tile, D), lambda i: (i, 0))] * len(tables)
        + ([fixed(col), fixed(col), fixed(mat)] if last else []),
        out_specs=[fixed(o) for o in outs],
        out_shape=[shape(o, F32) for o in outs],
        scratch_shapes=scratch,
        compiler_params=pltpu.CompilerParams(vmem_limit_bytes=ROOM),
        cost_estimate=SMALL_COST,
        name=f"lookup_{int(last)}",
    )(hidden, *tables, *(state if last else ()))


def lookup_back_kernel(scal, hid, code, lse, inner, *rest):
    tables, (out, keep, send) = rest[:-3], rest[-3:]
    step = pl.program_id(0)

    @pl.when(step == 0)
    def _():
        out[...] = jnp.zeros_like(out)

    gained = out[...]
    for table in tables:
        s = dot_rows(hid[...], table[...]) * D**-0.5
        p = jnp.exp(s - lse[...])
        dp = dot_rows(code[...], table[...])
        ds = (p * (dp - inner[...])).astype(BF16)
        gained = gained + dot(ds, table[...])
    out[...] = gained

    @pl.when(step == pl.num_programs(0) - 1)
    def _():
        value = out[...] * D**-0.5
        out[...] = value
        low = value.astype(BF16)
        for half in range(2):
            part = low[:, HALF * half : HALF * (half + 1)]

            @pl.when(scal[0] == half)
            def _():
                keep[...] = part

            @pl.when(scal[0] != half)
            def _():
                send[...] = part


def lookup_back(scal, hidden, code, lse, inner, tables):
    rows = tables[0].shape[0]
    tile = min(TILE, rows)
    col, mat, part = (ROWS, 1), (ROWS, D), (ROWS, HALF)
    return pl.pallas_call(
        lookup_back_kernel,
        grid_spec=pltpu.PrefetchScalarGridSpec(
            num_scalar_prefetch=1,
            grid=(rows // tile,),
            in_specs=[fixed(mat), fixed(mat), fixed(col), fixed(col)]
            + [pl.BlockSpec((tile, D), lambda i, *_: (i, 0))] * len(tables),
            out_specs=[fixed(mat), fixed(part), fixed(part)],
        ),
        out_shape=[shape(mat, F32), shape(part, BF16), shape(part, BF16)],
        compiler_params=pltpu.CompilerParams(vmem_limit_bytes=ROOM),
        cost_estimate=SMALL_COST,
        name="lookup_back",
    )(scal, hidden, code, lse, inner, *tables)


def swapped(value):
    return lax.ppermute(value, "section", [(0, 1), (1, 0)])


def bit_count():
    size = lax.axis_size("dp")
    count = size.bit_length() - 1
    assert size == 1 << count
    return count


def across(value, step):
    size = lax.axis_size("dp")
    return lax.ppermute(value, "dp", [(i, i ^ step) for i in range(size)])


def along(value, bit):
    return across(value, 1 << bit)


def after(value, *others):
    return lax.optimization_barrier((value, *others))[0]


def total(terms):
    summed = terms[0].astype(F32)
    for term in terms[1:]:
        summed = summed + term.astype(F32)
    return summed


class Share:
    def __init__(self, parts, first):
        count = bit_count()
        order = [first, 1 - first] if count > 1 else [0]
        self.order = order + list(range(len(order), count))
        self.live = list(range(count))[::-1]
        self.ready = None
        if len(parts) == 2:
            self.live.remove(first)
            self.ready = parts[1]
        self.terms = [self.laid(parts[0])]

    def laid(self, value):
        return value.reshape(value.shape[:1] + (2,) * len(self.live) + (-1, HALF))

    def split(self, stage):
        if stage == 0 and self.ready is not None:
            return self.ready
        bit = self.order[stage]
        axis = 1 + self.live.index(bit)
        mine = (lax.axis_index("dp") >> bit) & 1

        def pick(which):
            return [lax.dynamic_index_in_dim(t, which, axis, keepdims=False) for t in self.terms]

        sent = total(pick(1 - mine)).astype(BF16)
        self.terms = pick(mine)
        self.live.remove(bit)
        return sent

    def send(self, stage, *values):
        self.sent = after(self.split(stage), *values)
        self.got = along(self.sent, self.order[stage])

    def receive(self, *values):
        self.terms.append(self.laid(after(self.got, *values)))


class Pair:
    def __init__(self, left, right):
        self.shares = [Share(left, 0), Share(right, 1)]
        self.order = self.shares[0].order

    def ready(self):
        return [share.terms[0] for share in self.shares]

    def send(self, stage, *values):
        if stage < 2:
            for share in self.shares:
                share.send(stage, *values)
            self.sent = [share.sent for share in self.shares]
        else:
            self.sent = [jnp.stack([share.split(stage) for share in self.shares])]
            self.got = along(self.sent[0], self.order[stage])

    def receive(self, stage, *values):
        if stage < 2:
            for share in self.shares:
                share.receive(*values)
        else:
            got = after(self.got, *values)
            for i, share in enumerate(self.shares):
                share.terms.append(share.laid(got[i]))

    def result(self):
        return jnp.stack([total(share.terms) for share in self.shares])


def per_device(
    patches,
    recon_cot,
    lengths,
    codebook,
    w_qkv,
    w_out,
    w_up,
    w_down,
    norm_gain,
    norm_bias,
    bias_out,
    bias_up,
):
    section = lax.axis_index("section")
    on_first = section == 0
    size = lax.axis_size("dp")
    count = bit_count()
    me = lax.axis_index("dp")
    scal = jnp.stack([section, *((me >> bit) & 1 for bit in range(count))]).astype(jnp.int32)
    own_small = pack_small(norm_gain, norm_bias, bias_out, bias_up)
    small = (lengths, own_small, swapped(own_small))
    weights = [(w[0], swapped(w[0])) for w in (w_qkv, w_out)]

    table = codebook
    for bit in range(count - 1, 2, -1):
        got = after(along(table, bit), small[2], weights[0][1], weights[1][1])
        table = jnp.concatenate([table, got])
    weights += [(w[0], swapped(after(w[0], table))) for w in (w_up, w_down)]
    got = along(table, 2)
    from_table = along(table, 1)
    facts_ea, qkv_e, probs_e = att_forward(0, after(scal, table), patches, small, weights)
    got = after(got, facts_ea)
    from_got = along(got, 0)
    left = jnp.concatenate([table, after(from_table, got)])
    late = [along(left, 0)]
    right = jnp.concatenate([got, after(from_got, left)])
    late.append(along(right, 1))
    pieces = [left, right]
    pieces_other = [swapped(piece) for piece in pieces]
    hidden, facts_ef, resid_e, slope_e = ffn_forward(
        0, after(scal, *pieces), patches, small, facts_ea, weights
    )
    state = lookup(hidden, pieces + pieces_other)
    late = after(late, state[0])
    late_other = [swapped(piece) for piece in late]
    tables = pieces + pieces_other + late + late_other
    mean_code, unit, lse = lookup(hidden, late + late_other, state)
    facts_ea = (facts_ea, swapped(after(facts_ea, *late_other)))
    facts_ef = (facts_ef, swapped(after(facts_ef, *late_other)))
    recon, facts_df, facts_da, qkv_d, probs_d, resid_d, slope_d = block_forward(
        1, after(scal, facts_ea[1], facts_ef[1]), unit, small, weights
    )
    facts_df = (facts_df, swapped(facts_df))
    facts_da = (facts_da, swapped(facts_da))
    recon_first = lax.ppermute(recon, "section", [(0, 1)])
    lse_other = swapped(lse)

    keep, send, d_resid, sums_df = ffn_backward(
        1, scal, recon_cot, slope_d, resid_d, small, weights, True
    )
    first_f = Pair(*ffn_grads(after(scal, keep), facts_df, (keep, swapped(send)), [recon_cot], count, True))
    first_f.send(0)
    keep, send, sums_da, code, inner = att_backward(
        1, after(scal, facts_da[1], *first_f.sent), d_resid, qkv_d, probs_d, unit, small, weights, mean_code
    )
    got = swapped(send)
    d_hidden, g_keep, g_send = lookup_back(scal, hidden, code, lse, inner, tables)
    g_got = swapped(g_send)
    first_f.receive(0, d_hidden, g_got, recon_first, lse_other)
    first_f.send(1)
    left, right = att_grads(after(scal, *first_f.sent), facts_da, (keep, got), count)
    first_a = Pair(left, right)
    first_a.send(0)
    keep, send, d_resid, sums_ef = ffn_backward(
        0, after(scal, *first_a.sent), d_hidden, slope_e, resid_e, small, weights, False
    )
    got = swapped(send)
    first_f.receive(1, keep)
    first_f.send(2)
    second_f = Pair(
        *ffn_grads(after(scal, keep, *first_f.sent), facts_ef, (keep, got), (g_keep, g_got), count, False)
    )
    first_a.receive(0, *second_f.ready())
    first_a.send(1)
    second_f.send(0)
    keep, send, sums_ea, grad_x = att_backward(
        0, after(scal, *second_f.sent, *first_a.sent), d_resid, qkv_e, probs_e, patches, small, weights
    )
    got = swapped(send)
    first_f.receive(2, sums_ea)
    first_f.send(3)
    left, right = att_grads(after(scal, *first_f.sent), facts_ea, (keep, got), count)
    second_a = Pair(left, right)
    second_f.receive(0, left[0])
    second_f.send(1)
    second_a.send(0, *second_f.sent)
    sums_ef, sums_ea, sums_df, sums_da = after([sums_ef, sums_ea, sums_df, sums_da], *second_a.sent)
    sums = jnp.stack([jnp.concatenate([sums_ef, sums_ea[:2]]), jnp.concatenate([sums_df, sums_da[:2]])])
    sums_got = swapped(jnp.where(on_first, sums[1], sums[0]))
    first_a.receive(1, *second_a.sent)
    first_a.send(2)
    sums = jnp.where(on_first, sums[0], sums[1]) + after(sums_got, *first_a.sent)
    sums_got = along(sums, 2)
    grad_second = lax.ppermute(after(grad_x, sums), "section", [(1, 0)])
    second_f.receive(1, grad_second, *first_a.sent)
    second_f.send(2)
    sums = sums + after(sums_got, *second_f.sent)
    sums_got = along(sums, 3)
    first_a.receive(2, sums)
    first_a.send(3)
    second_a.receive(0, *first_a.sent)
    second_a.send(1)
    sums = sums + after(sums_got, *second_a.sent)
    for bit in range(4, count):
        sums = sums + along(sums, bit)
    sums_got = along(sums, 0)
    second_f.receive(2, sums)
    second_f.send(3)
    sums = sums + after(sums_got, *second_f.sent)
    sums_got = along(sums, 1)
    second_a.receive(1, sums)
    second_a.send(2)
    sums = sums + after(sums_got, *second_a.sent)
    last = [sums]
    waiting = [[first_f, 3], [first_a, 3], [second_f, 3], [second_a, 2]]
    for step in range(count):
        for entry in waiting:
            pair, stage = entry
            if stage < count - (1 if pair is second_a else 0):
                pair.receive(stage, *last)
                if stage + 1 < count:
                    pair.send(stage + 1)
                    last = pair.sent
                entry[1] += 1

    width = D // size
    ffn_e, ffn_d = second_f.result(), first_f.result()
    kept = jnp.where(on_first, ffn_e, ffn_d)
    got = swapped(jnp.where(on_first, ffn_d, ffn_e))
    ffn = jnp.stack([jnp.where(on_first, kept, got), jnp.where(on_first, got, kept)])
    grad_down = ffn[:, 0].reshape(2, 4 * width, HALF).swapaxes(0, 1).reshape(1, 4 * width, D)
    grad_up = ffn[:, 1].transpose(2, 0, 1, 3).reshape(1, width, FF)
    cols = me * width
    rows = lax.dynamic_slice_in_dim(sums, cols, width, axis=1)
    grad_gain = jnp.stack([rows[8], rows[0]])[None]
    grad_nbias = jnp.stack([rows[9], rows[1]])[None]
    grad_bout = jnp.stack([rows[3], rows[2]])[None]
    grad_bup = lax.dynamic_slice_in_dim(sums[4:8].reshape(FF), cols * 4, width * 4)[None]
    ends = jnp.where(
        on_first, jnp.concatenate([grad_x, grad_second]), jnp.concatenate([recon_first, recon])
    )[None]
    lse, lse_other = after([lse, lse_other], *last)
    lse, lse_other = lse[:, 0], lse_other[:, 0]
    codes = jnp.where(on_first, jnp.concatenate([lse, lse_other]), jnp.concatenate([lse_other, lse]))
    second_a.receive(count - 1, grad_down, grad_up, grad_gain, grad_nbias, grad_bout, grad_bup, ends, codes)
    att_e, att_d = second_a.result(), first_a.result()
    got = swapped(jnp.where(on_first, att_d, att_e))
    grad_qkv, grad_out = finish_att(scal, jnp.where(on_first, att_e, att_d), got)
    return (ends, codes, grad_qkv, grad_out, grad_up, grad_down, grad_gain, grad_nbias, grad_bout, grad_bup)


def solution(mesh):
    placed = (
        P("dp", None),
        P("dp", None),
        P("dp", None),
        P(("dp", "section"), None),
        P("section", None, None),
        P("section", None, None),
        P("section", None, None),
        P("section", None, None),
        P("section", None, None),
        P("section", None, None),
        P("section", None, None),
        P("section", None),
    )
    return jax.shard_map(
        per_device,
        mesh=mesh,
        in_specs=placed,
        out_specs=(
            P("section", "dp", None),
            P("dp"),
            P("section", "dp", None),
            P("section", "dp", None),
            P("section", "dp", None),
            P("section", "dp", None),
            P("section", None, "dp"),
            P("section", None, "dp"),
            P("section", None, "dp"),
            P("section", "dp"),
        ),
        check_vma=False,
    )
```

```python
from functools import partial

import jax
import jax.numpy as jnp
from jax import lax
from jax.experimental import pallas as pl
from jax.experimental.layout import Layout, with_layout_constraint
from jax.experimental.pallas import tpu as pltpu
from jax.sharding import PartitionSpec as P

D = 768
HEADS = 12
HD = 64
FF = 3072
ROWS = 256
PAIR = 2 * HD
EPS = 1e-06
MASKED = -1e30
F32 = jnp.float32
BF16 = jnp.bfloat16
N2, FFN_FACTS = FF, FF + D
MIX, ATT_FACTS = D, 2 * D
HALF = D // 2
HALF_UP = FF // 2
HALF_QKV = 3 * D // 2
TAIL_P = 0.35
TAIL = (0.19620077326315646, 0.2185939781557991, 0.05480664657447366, 0.5651487076988272,
        -0.5574354264567037, 0.7060774515721405, -0.18339209581143395)
VMEM = pl.BlockSpec(memory_space=pltpu.VMEM)
SMEM = pl.BlockSpec(memory_space=pltpu.SMEM)
ANY = pl.BlockSpec(memory_space=pl.ANY)
ROOM = 63 * 1024 * 1024


def dot(a, b):
    return jnp.dot(a, b, preferred_element_type=F32)


def dot_rows(a, b):
    return lax.dot_general(a, b, (((1,), (1,)), ((), ())), preferred_element_type=F32)


def dot_cols(a, b):
    return lax.dot_general(a, b, (((0,), (0,)), ((), ())), preferred_element_type=F32)


def unit_rows(values):
    centre = values - jnp.mean(values, axis=-1, keepdims=True)
    inverse = lax.rsqrt(jnp.mean(centre * centre, axis=-1, keepdims=True) + EPS)
    return centre * inverse, inverse


def norm_back(scaled, unit, inverse):
    return inverse * (
        scaled
        - jnp.mean(scaled, axis=-1, keepdims=True)
        - unit * jnp.mean(scaled * unit, axis=-1, keepdims=True)
    )


def gelu_parts(z):
    bell = jnp.exp(-0.5 * z * z)
    t = 1.0 / (1.0 + (TAIL_P * 0.5**0.5) * jnp.abs(z))
    poly = TAIL[6] * t + TAIL[5]
    for c in TAIL[4::-1]:
        poly = poly * t + c
    tail = 0.5 * poly * t * bell
    cdf = jnp.where(z >= 0, 1.0 - tail, tail)
    return z * cdf, cdf + z * bell * 0.3989422804014327


def image_ids(scal, lens, shape, axis):
    position = lax.broadcasted_iota(jnp.int32, shape, axis)
    limit = jnp.int32(0)
    ids = jnp.zeros(shape, jnp.int32)
    for i in range(4):
        limit = limit + lens[scal[0], i]
        ids = ids + (position >= limit).astype(jnp.int32)
    return ids


def shape(s, t):
    return jax.ShapeDtypeStruct(s, t)


class Moves:
    def __init__(self, sems):
        self.sems = sems
        self.used = 0
        self.leaving = []

    def sem(self):
        self.used += 1
        return self.sems.at[self.used - 1]

    def load(self, src, dst):
        copy = pltpu.make_async_copy(src, dst, self.sem())
        copy.start()
        return copy.wait

    def load_either(self, first, src, other, dst):
        sem = self.sem()
        for take, ref in ((first, src), (jnp.logical_not(first), other)):
            @pl.when(take)
            def _():
                pltpu.make_async_copy(ref, dst, sem).start()

        return pltpu.make_async_copy(src, dst, sem).wait

    def load_tiles(self, first, src, other, dst, axis):
        tiles = []
        for j in range(dst.shape[axis] // D):
            at = (pl.ds(D * j, D),) if axis == 0 else (slice(None), pl.ds(D * j, D))
            tiles.append((at, self.sem()))
        for take, ref in ((first, src), (jnp.logical_not(first), other)):
            @pl.when(take)
            def _():
                for at, sem in tiles:
                    pltpu.make_async_copy(ref.at[at], dst.at[at], sem).start()

        return [pltpu.make_async_copy(src.at[at], dst.at[at], sem).wait for at, sem in tiles]

    def store(self, src, dst):
        copy = pltpu.make_async_copy(src, dst, self.sem())
        copy.start()
        self.leaving.append(copy.wait)

    def finish(self):
        for wait in self.leaving:
            wait()


SEMS = 32
SMALL_COST = pl.CostEstimate(flops=1000, bytes_accessed=1000, transcendentals=0)


def call(body, name, scal, inputs, outs, scratch, small=None):
    extra = () if small is None else small[1:]

    def kernel(*refs):
        scal, *refs = refs
        moves = Moves(refs[-1])
        if small is None:
            body(moves, scal, *refs[:-1])
        else:
            lens, own, other, *refs = refs
            chosen = refs[-2]
            chosen[...] = jnp.where(scal[0] == small[0], own[...], other[...])
            body(moves, scal, lens, chosen, *refs[:-2])
        moves.finish()

    return pl.pallas_call(
        kernel,
        in_specs=[SMEM] + [SMEM, VMEM, VMEM][: len(extra)] + [ANY] * len(inputs),
        out_specs=[ANY] * len(outs),
        out_shape=outs,
        scratch_shapes=[
            *(pltpu.VMEM(s, t) for s, t in (*scratch, *([SMALL] if extra else []))),
            pltpu.SemaphoreType.DMA((SEMS,)),
        ],
        compiler_params=pltpu.CompilerParams(vmem_limit_bytes=ROOM),
        cost_estimate=SMALL_COST,
        name=name,
    )(scal, *extra, *inputs)


SMALL = ((10, D), F32)
W_QKV = ((D, 3 * D), BF16)
W_OUT = ((D, D), BF16)
W_UP = ((D, FF), BF16)
W_DOWN = ((FF, D), BF16)
MAT = ((ROWS, D), F32)
LOW = ((ROWS, D), BF16)
COL = ((ROWS, 1), F32)


def rows_of(scal, own=True):
    which = scal[0] if own else 1 - scal[0]
    return pl.ds(pl.multiple_of(which * ROWS, ROWS), ROWS)


def half_of(scal, width, own=True):
    which = scal[0] if own else 1 - scal[0]
    return pl.ds(pl.multiple_of(which * width, 128), width)


def pack_small(gains, shifts, bias_out, bias_up):
    def kernel(gains, shifts, bias_out, bias_up, out):
        for i, ref in enumerate((gains, shifts, bias_out)):
            out[2 * i : 2 * i + 2, :] = ref[0]
        for j in range(FF // D):
            out[6 + j : 7 + j, :] = bias_up[:, D * j : D * (j + 1)]

    return pl.pallas_call(
        kernel, in_specs=[VMEM] * 4, out_specs=VMEM, out_shape=shape(*SMALL), cost_estimate=SMALL_COST, name="pack_small",
    )(gains, shifts, bias_out, bias_up)


def att_forward_part(moves, scal, lens, x, small, wq, wait, facts, qkv, probs, out):
    facts_hbm, qkv_hbm, probs_hbm = out
    unit, _ = unit_rows(x)
    n1 = (unit * small[0:1, :] + small[2:3, :]).astype(BF16)
    facts[:, :D] = n1
    same = image_ids(scal, lens, (ROWS, ROWS), 0) == image_ids(scal, lens, (ROWS, ROWS), 1)
    bias = jnp.where(same, 0.0, MASKED)
    first = lax.broadcasted_iota(jnp.int32, (1, PAIR), 1) < HD
    for j in range(3):
        wait[j]()
        qkv[:, D * j : D * (j + 1)] = dot(n1, wq[:, D * j : D * (j + 1)]).astype(BF16)
    moves.store(qkv, qkv_hbm)
    for p in range(HEADS // 2):
        q = qkv[:, PAIR * p : PAIR * (p + 1)] * jnp.asarray(HD**-0.5, BF16)
        k = qkv[:, D + PAIR * p : D + PAIR * (p + 1)]
        v = qkv[:, 2 * D + PAIR * p : 2 * D + PAIR * (p + 1)]
        outs = []
        for side in range(2):
            own = first if side == 0 else jnp.logical_not(first)
            s = dot_rows(jnp.where(own, q, jnp.zeros_like(q)), k) + bias
            s = jnp.exp(s - jnp.max(s, axis=-1, keepdims=True))
            pr = (s * (1.0 / jnp.sum(s, axis=-1, keepdims=True))).astype(BF16)
            probs[2 * p + side] = pr
            outs.append(dot(pr, v))
        facts[:, MIX + PAIR * p : MIX + PAIR * (p + 1)] = jnp.where(first, outs[0], outs[1]).astype(BF16)
    moves.store(probs, probs_hbm)
    moves.store(facts, facts_hbm)


def ffn_forward_part(moves, x, small, mixed, wo, wu, wd, waits, facts, resid_ref, slope, y_ref, out):
    y_hbm, facts_hbm, resid_hbm, slope_hbm = out
    waits[0]()
    resid = x + dot(mixed, wo[...]) + small[4:5, :]
    resid_ref[...] = resid
    moves.store(resid_ref, resid_hbm)
    unit, _ = unit_rows(resid)
    n2 = (unit * small[1:2, :] + small[3:4, :]).astype(BF16)
    facts[:, N2 : N2 + D] = n2
    y = resid + small[5:6, :]
    tiles = FF // D

    def pre_tile(j):
        waits[1][j]()
        return dot(n2, wu[:, D * j : D * (j + 1)]) + small[6 + j : 7 + j, :]

    pre = pre_tile(0)
    for j in range(tiles):
        cols = slice(D * j, D * (j + 1))
        waits[2][j]()
        later = pre_tile(j + 1) if j + 1 < tiles else None
        act, sl = gelu_parts(pre)
        act = act.astype(BF16)
        facts[:, cols] = act
        slope[:, cols] = sl.astype(BF16)
        y = y + dot(act, wd[cols, :])
        pre = later
    moves.store(facts, facts_hbm)
    moves.store(slope, slope_hbm)
    y_ref[...] = y.astype(y_ref.dtype)
    moves.store(y_ref, y_hbm)


FACTS_A = ((ROWS, ATT_FACTS), BF16)
FACTS_F = ((ROWS, FFN_FACTS), BF16)
QKV = ((ROWS, 3 * D), BF16)
PROBS = ((HEADS, ROWS, ROWS), BF16)
SLOPE = ((ROWS, FF), BF16)


def outputs(*kinds):
    return [shape(*kind) for kind in kinds]


def block_forward(block, scal, x, small, weights):
    def body(moves, scal, lens, small, x_in, wq_a, wq_b, wo_a, wo_b, wu_a, wu_b, wd_a, wd_b,
             y_o, facts_fo, facts_ao, qkv_o, probs_o, resid_o, slope_o,
             x, wq, wo, wu, wd, y, facts_f, facts_a, qkv, probs, resid, slope):
        own = scal[0] == block
        wait_x = moves.load(x_in, x)
        wait_q = moves.load_tiles(own, wq_a, wq_b, wq, 1)
        waits = [moves.load_either(own, a, b, w) for a, b, w in ((wo_a, wo_b, wo), (wu_a, wu_b, wu), (wd_a, wd_b, wd))]
        waits = [waits[0]] + [[wait] + [lambda: None] * 3 for wait in waits[1:]]
        wait_x()
        xs = x[...]
        att_forward_part(moves, scal, lens, xs, small, wq, wait_q, facts_a, qkv, probs, (facts_ao, qkv_o, probs_o))
        ffn_forward_part(
            moves, xs, small, facts_a[:, MIX : MIX + D], wo, wu, wd, waits, facts_f, resid, slope, y,
            (y_o, facts_fo, resid_o, slope_o),
        )

    kinds = (MAT, FACTS_F, FACTS_A, QKV, PROBS, MAT, SLOPE)
    return call(
        body, f"forward_{block}", scal, [x, *sum(weights, ())], outputs(*kinds),
        [MAT, W_QKV, W_OUT, W_UP, W_DOWN, *kinds], (block, *small),
    )


def att_forward(block, scal, patches, small, weights):
    def body(moves, scal, lens, small, x_in, wq_a, wq_b, facts_o, qkv_o, probs_o, x, wq, facts, qkv, probs):
        wait_x = moves.load(x_in.at[rows_of(scal), :], x)
        wait_w = moves.load_tiles(scal[0] == block, wq_a, wq_b, wq, 1)
        wait_x()
        att_forward_part(
            moves, scal, lens, x[...].astype(F32), small, wq, wait_w, facts, qkv, probs, (facts_o, qkv_o, probs_o)
        )

    kinds = (FACTS_A, QKV, PROBS)
    return call(
        body, f"att_forward_{block}", scal, [patches, *weights[0]], outputs(*kinds),
        [LOW, W_QKV, *kinds], (block, *small),
    )


def ffn_forward(block, scal, patches, small, facts_a, weights):
    def body(moves, scal, lens, small, x_in, facts_ai, wo_a, wo_b, wu_a, wu_b, wd_a, wd_b,
             y_o, facts_o, resid_o, slope_o, x, mixed, wo, wu, wd, y, facts, resid, slope):
        own = scal[0] == block
        wait_x = moves.load(x_in.at[rows_of(scal), :], x)
        wait_m = moves.load(facts_ai.at[:, pl.ds(MIX, D)], mixed)
        waits = [
            moves.load_either(own, wo_a, wo_b, wo),
            moves.load_tiles(own, wu_a, wu_b, wu, 1),
            moves.load_tiles(own, wd_a, wd_b, wd, 0),
        ]
        wait_x()
        wait_m()
        ffn_forward_part(
            moves, x[...].astype(F32), small, mixed[...], wo, wu, wd, waits, facts, resid, slope, y,
            (y_o, facts_o, resid_o, slope_o),
        )

    kinds = (LOW, FACTS_F, MAT, SLOPE)
    return call(
        body, f"ffn_forward_{block}", scal, [patches, facts_a, *sum(weights[1:], ())], outputs(*kinds),
        [LOW, LOW, W_OUT, W_UP, W_DOWN, *kinds], (block, *small),
    )


COT_UP = ((ROWS, HALF_UP), BF16)
COT_ATT = ((ROWS, HALF_QKV + HALF), BF16)
SUMS = ((8, D), F32)


def ffn_backward(block, scal, g, slope, resid, small, weights, own_rows):
    def body(moves, scal, lens, small, g_in, slope_in, resid_in, wu_a, wu_b, wd_a, wd_b,
             keep_o, send_o, dres_o, sums, g_ref, slope, resid, wu, wd, d_pre_ref, dres):
        own = scal[0] == block
        wait_g = moves.load(g_in.at[rows_of(scal), :] if own_rows else g_in, g_ref)
        wait_d = moves.load_tiles(own, wd_a, wd_b, wd, 0)
        wait_s = moves.load(slope_in, slope)
        wait_u = moves.load_tiles(own, wu_a, wu_b, wu, 1)
        wait_r = moves.load(resid_in, resid)
        wait_g()
        g = g_ref[...].astype(F32)
        gl = g.astype(BF16)
        small_sums = [None] * 4
        small_sums[2] = jnp.sum(g, axis=0, keepdims=True)
        d_n2 = jnp.zeros((ROWS, D), F32)
        up_sums = []
        tiles = FF // D

        def act_tile(j):
            wait_d[j]()
            return dot_rows(gl, wd[D * j : D * (j + 1), :])

        later = act_tile(0)
        wait_s()
        for j in range(tiles):
            cols = slice(D * j, D * (j + 1))
            wait_u[j]()
            d_act = later
            later = act_tile(j + 1) if j + 1 < tiles else None
            d_pre = (d_act * slope[:, cols].astype(F32)).astype(BF16)
            d_pre_ref[:, cols] = d_pre
            up_sums.append(jnp.sum(d_pre.astype(F32), axis=0, keepdims=True))
            d_n2 = d_n2 + dot_rows(d_pre, wu[:, cols])
        moves.store(d_pre_ref.at[:, half_of(scal, HALF_UP)], keep_o)
        moves.store(d_pre_ref.at[:, half_of(scal, HALF_UP, False)], send_o)
        wait_r()
        unit, inverse = unit_rows(resid[...])
        small_sums[0] = jnp.sum(d_n2 * unit, axis=0, keepdims=True)
        small_sums[1] = jnp.sum(d_n2, axis=0, keepdims=True)
        d_resid = g + norm_back(d_n2 * small[1:2, :], unit, inverse)
        dres[...] = d_resid
        moves.store(dres, dres_o)
        small_sums[3] = jnp.sum(d_resid, axis=0, keepdims=True)
        for i, value in enumerate(small_sums + up_sums):
            sums[i : i + 1, :] = value

    def with_sums(moves, *refs):
        *head, sums_buffer = refs
        sums_o = head[13]
        head[13] = sums_buffer
        body(moves, *head)
        moves.store(sums_buffer, sums_o)

    g_kind = (tuple(g.shape), g.dtype) if not own_rows else ((ROWS, D), g.dtype)
    return call(
        with_sums, f"ffn_backward_{block}", scal, [g, slope, resid, *weights[2], *weights[3]],
        outputs(COT_UP, COT_UP, MAT, SUMS),
        [g_kind, SLOPE, MAT, W_UP, W_DOWN, SLOPE, MAT, SUMS], (block, *small),
    )


def att_backward(block, scal, d_resid, qkv, probs, x, small, weights, mean_code=None, sums_before=None):
    final = mean_code is None

    def body(moves, scal, lens, small, dres_in, qkv_in, probs_in, x_in, wq_a, wq_b, wo_a, wo_b, *rest):
        if final:
            (ef_in, df_in, da_in, keep_o, send_o, own_o, other_o, gx_o,
             dres, qkv, probs, x_ref, wq, wo, d_qkv, rl_ref, sums, ef, df, da, packed, gx) = rest
            wait_sums = [moves.load(src, dst) for src, dst in ((ef_in, ef), (df_in, df), (da_in, da))]
        else:
            (mean_in, keep_o, send_o, sums_o, code_o, inner_o,
             dres, qkv, probs, x_ref, wq, wo, d_qkv, rl_ref, sums, mean_ref, code_ref, inner_ref) = rest
        own = scal[0] == block
        wait_g = moves.load(dres_in, dres)
        wait_o = moves.load_either(own, wo_a, wo_b, wo)
        wait_k = moves.load(qkv_in, qkv)
        wait_p = moves.load(probs_in, probs)
        wait_q = moves.load_either(own, wq_a, wq_b, wq)
        wait_x = moves.load(x_in.at[rows_of(scal), :] if final else x_in, x_ref)
        if not final:
            wait_m = moves.load(mean_in, mean_ref)
        wait_g()
        d_resid = dres[...]
        rl = d_resid.astype(BF16)
        rl_ref[...] = rl
        for out, mine in ((keep_o, True), (send_o, False)):
            moves.store(rl_ref.at[:, half_of(scal, HALF, mine)], out.at[:, pl.ds(HALF_QKV, HALF)])
        first = lax.broadcasted_iota(jnp.int32, (1, PAIR), 1) < HD
        wait_o()
        d_mixed = dot_rows(rl, wo[...]).astype(BF16)
        wait_k()
        wait_p()
        scale = jnp.asarray(HD**-0.5, BF16)
        for p in range(HEADS // 2):
            q = qkv[:, PAIR * p : PAIR * (p + 1)] * scale
            k = qkv[:, D + PAIR * p : D + PAIR * (p + 1)]
            v = qkv[:, 2 * D + PAIR * p : 2 * D + PAIR * (p + 1)]
            dm = d_mixed[:, PAIR * p : PAIR * (p + 1)]
            dq, dk, dv = [], [], []
            for side in range(2):
                mine = first if side == 0 else jnp.logical_not(first)
                pr = probs[2 * p + side]
                dp = dot_rows(jnp.where(mine, dm, jnp.zeros_like(dm)), v)
                prf = pr.astype(F32)
                ds = (prf * (dp - jnp.sum(dp * prf, axis=-1, keepdims=True))).astype(BF16)
                dv.append(dot_cols(pr, dm))
                dq.append(dot(ds, k))
                dk.append(dot_cols(ds, q))
            for at, parts in ((0, dq), (D, dk), (2 * D, dv)):
                value = jnp.where(first, parts[0], parts[1])
                if at == 0:
                    value = value * HD**-0.5
                d_qkv[:, at + PAIR * p : at + PAIR * (p + 1)] = value.astype(BF16)
        for out, mine in ((keep_o, True), (send_o, False)):
            moves.store(d_qkv.at[:, half_of(scal, HALF_QKV, mine)], out.at[:, pl.ds(0, HALF_QKV)])
        wait_q()
        d_n1 = dot_rows(d_qkv[...], wq[...])
        wait_x()
        x = x_ref[...].astype(F32)
        unit, inverse = unit_rows(x)
        sums[0:1, :] = jnp.sum(d_n1 * unit, axis=0, keepdims=True)
        sums[1:2, :] = jnp.sum(d_n1, axis=0, keepdims=True)
        if final:
            for wait in wait_sums:
                wait()
            for i, (ffn, att) in enumerate(((ef, sums), (df, da))):
                packed[i, 0:8, :] = ffn[...]
                packed[i, 8:10, :] = att[0:2, :]
            moves.store(packed.at[scal[0]], own_o)
            moves.store(packed.at[1 - scal[0]], other_o)
        else:
            sums[2:8, :] = jnp.zeros((6, D), F32)
            moves.store(sums, sums_o)
        grad_x = d_resid + norm_back(d_n1 * small[0:1, :], unit, inverse)
        if final:
            gx[...] = grad_x
            moves.store(gx, gx_o)
        else:
            wait_m()
            mean_code = mean_ref[...]
            inv = lax.rsqrt(jnp.mean(mean_code * mean_code, axis=-1, keepdims=True) + EPS)
            code = inv * (grad_x - x * jnp.mean(grad_x * x, axis=-1, keepdims=True))
            code = code.astype(BF16)
            code_ref[...] = code
            moves.store(code_ref, code_o)
            inner_ref[...] = jnp.sum(code.astype(F32) * mean_code, axis=-1, keepdims=True)
            moves.store(inner_ref, inner_o)

    if final:
        more_in, more, sums_out = [*sums_before], [MAT], [SMALL, SMALL]
        more_scratch = [SUMS, SUMS, SUMS, ((2, 10, D), F32)]
    else:
        more_in, more, sums_out = [mean_code], [LOW, COL], [SUMS]
        more_scratch = [MAT]
    return call(
        body, f"att_backward_{block}", scal, [d_resid, qkv, probs, x, *weights[0], *weights[1], *more_in],
        outputs(COT_ATT, COT_ATT, *sums_out, *more),
        [MAT, QKV, PROBS, LOW if final else MAT, W_QKV, W_OUT, QKV, LOW, SUMS, *more_scratch, *more],
        (block, *small),
    )


def group_outputs(kinds, order, count):
    width = D >> count
    if width % 16:
        return [((kinds, D, HALF), BF16)], ((kinds, D, HALF), BF16)
    tail = (kinds, width, HALF)
    return [((2,) * (count - 1) + tail, BF16)] * 2, ((2,) * count + tail, BF16)


def put(buffer, order, kind, value, owner=0):
    if len(buffer.shape) == 3:
        width = D >> len(order)
        buffer[kind, width * owner : width * owner + value.shape[0], :] = value
        return
    width = buffer.shape[-2]
    for i in range(value.shape[0] // width):
        place = tuple((owner + i) >> bit & 1 for bit in order)
        buffer[place + (kind,)] = value[width * i : width * (i + 1)]


def leave(moves, buffer, outs, mine):
    if len(outs) == 1:
        moves.store(buffer, outs[0])
    else:
        moves.store(buffer.at[mine], outs[0])
        moves.store(buffer.at[1 - mine], outs[1])


def ffn_grads(scal, facts, cots, outs_g, count, orders, both):
    down, down_buffer = group_outputs(FF // D, orders[0], count)
    up, up_buffer = group_outputs(HALF_UP // HALF, orders[1], count)
    width = D >> count
    given = 4 + len(outs_g)

    def body(moves, scal, *refs):
        ins, outs, (fa, fb, ca, cb, ga, gb, buf_d, buf_u) = refs[:given], refs[given:-8], refs[-8:]
        if both:
            wait_g = [
                moves.load(ins[4].at[rows_of(scal, own), half_of(scal, HALF)], g)
                for g, own in ((ga, True), (gb, False))
            ]
        else:
            wait_g = [moves.load(ref, g) for ref, g in zip(ins[4:], (ga, gb))]
        wait_f = []
        for j in range(FFN_FACTS // D):
            cols = pl.ds(D * j, D)
            wait_f.append([moves.load(src.at[:, cols], dst.at[:, cols]) for src, dst in zip(ins, (fa, fb))])
        wait_c = [moves.load(ref, c) for ref, c in zip(ins[2:4], (ca, cb))]
        for wait in wait_g:
            wait()
        for j in range(FF // D):
            cols = slice(D * j, D * (j + 1))
            for wait in wait_f[j]:
                wait()
            value = dot_cols(fa[:, cols], ga[...]) + dot_cols(fb[:, cols], gb[...])
            value = value.astype(BF16)
            owners = D // (4 * width)
            for i in range(owners):
                for kind in range(4):
                    at = width * (4 * i + kind)
                    put(buf_d, orders[0], kind, value[at : at + width], owners * j + i)
        leave(moves, buf_d, outs[: len(down)], scal[1 + orders[0][0]])
        for wait in wait_f[-1] + wait_c:
            wait()
        n2 = slice(N2, N2 + D)
        for j in range(HALF_UP // HALF):
            cols = slice(HALF * j, HALF * (j + 1))
            value = dot_cols(fa[:, n2], ca[:, cols]) + dot_cols(fb[:, n2], cb[:, cols])
            put(buf_u, orders[1], j, value.astype(BF16))
        leave(moves, buf_u, outs[len(down) :], scal[1 + orders[1][0]])

    result = call(
        body, "ffn_grads", scal, [*facts, *cots, *outs_g], outputs(*down, *up),
        [FACTS_F] * 2 + [COT_UP] * 2 + [((ROWS, HALF), BF16)] * 2 + [down_buffer, up_buffer],
    )
    return result[: len(down)], result[len(down) :]


def att_grads(scal, facts, cots, count, orders):
    each = 4 // len(orders)
    plans = [group_outputs(each, order, count) for order in orders]
    outs = [out for plan in plans for out in plan[0]]

    def body(moves, scal, *refs):
        ins, outs_ref, rest = refs[:4], refs[4 : 4 + len(outs)], refs[4 + len(outs) :]
        (fa, fb, ca, cb), buffers = rest[:4], rest[4:]
        waits = [moves.load(src, dst) for src, dst in zip(ins, (fa, fb, ca, cb))]
        for wait in waits:
            wait()
        for j in range(4):
            at = slice(0, D) if j < 3 else slice(MIX, MIX + D)
            cols = slice(HALF * j, HALF * (j + 1))
            value = dot_cols(fa[:, at], ca[:, cols]) + dot_cols(fb[:, at], cb[:, cols])
            put(buffers[j // each], orders[j // each], j % each, value.astype(BF16))
        step = len(outs) // len(orders)
        for i, order in enumerate(orders):
            leave(moves, buffers[i], outs_ref[step * i : step * (i + 1)], scal[1 + order[0]])

    result = call(
        body, "att_grads", scal, [*facts, *cots], outputs(*outs),
        [FACTS_A] * 2 + [COT_ATT] * 2 + [plan[1] for plan in plans],
    )
    step = len(outs) // len(orders)
    return [result[i : i + step] for i in range(0, len(outs), step)]


def finish(scal, ffn_kept, ffn_got, att_kept, att_got):
    width = ffn_kept.shape[2]

    def kernel(scal, ffn_kept, ffn_got, att_kept, att_got, qkv, out, up, down):
        mine = scal[0] == 0
        for half in range(2):

            def group(kept, got, i, j):
                a, b = kept[i, j], got[i, j]
                return jnp.where(mine, a, b) if half == 0 else jnp.where(mine, b, a)

            for j in range(4):
                down[0, width * j : width * (j + 1), HALF * half : HALF * (half + 1)] = group(ffn_kept, ffn_got, 0, j)
                at = HALF_UP * half + HALF * j
                up[0, :, at : at + HALF] = group(ffn_kept, ffn_got, 1, j)
                value = group(att_kept, att_got, j // 2, j % 2)
                if j < 3:
                    at = HALF_QKV * half + HALF * j
                    qkv[0, :, at : at + HALF] = value
                else:
                    out[0, :, HALF * half : HALF * (half + 1)] = value

    return pl.pallas_call(
        kernel,
        in_specs=[SMEM] + [VMEM] * 4,
        out_specs=[VMEM] * 4,
        out_shape=[shape((1, *s), F32) for s in ((width, 3 * D), (width, D), (width, FF), (4 * width, D))],
        cost_estimate=SMALL_COST,
        name="finish",
    )(scal, ffn_kept, ffn_got, att_kept, att_got)


TILE = 512


def lookup_kernel(count, last, hid, *rest):
    tables, rest = rest[:count], rest[count:]
    if last:
        m_in, l_in, a_in, mean_ref, unit_ref, lse_ref, m_ref, l_ref, acc = rest
    else:
        m_ref, l_ref, acc = rest
    step = pl.program_id(0)

    @pl.when(step == 0)
    def _():
        if last:
            m_ref[...] = m_in[...]
            l_ref[...] = l_in[...]
            acc[...] = a_in[...]
        else:
            m_ref[...] = jnp.full((ROWS, 1), MASKED, F32)
            l_ref[...] = jnp.zeros((ROWS, 1), F32)
            acc[...] = jnp.zeros((ROWS, D), F32)

    scores = [dot_rows(hid[...], table[...]) * D**-0.5 for table in tables]
    top = m_ref[...]
    for s in scores:
        top = jnp.maximum(top, jnp.max(s, axis=-1, keepdims=True))
    fade = jnp.exp(m_ref[...] - top)
    m_ref[...] = top
    total_l = l_ref[...] * fade
    total_a = acc[...] * fade
    for s, table in zip(scores, tables):
        p = jnp.exp(s - top)
        total_l = total_l + jnp.sum(p, axis=-1, keepdims=True)
        high = p.astype(BF16)
        low = (p - high.astype(F32)).astype(BF16)
        total_a = total_a + dot(high, table[...]) + dot(low, table[...])
    l_ref[...] = total_l
    acc[...] = total_a
    if last:
        @pl.when(step == pl.num_programs(0) - 1)
        def _():
            totals = l_ref[...]
            mean_code = acc[...] / totals
            mean_ref[...] = mean_code
            unit_ref[...] = mean_code * lax.rsqrt(
                jnp.mean(mean_code * mean_code, axis=-1, keepdims=True) + EPS
            )
            lse_ref[...] = m_ref[...] + jnp.log(totals)


def fixed(s):
    return pl.BlockSpec(s, lambda i, *_: (0,) * len(s))


def lookup(hidden, tables, state=None):
    last = state is not None
    rows = tables[0].shape[0]
    tile = min(TILE, rows)
    col, mat = (ROWS, 1), (ROWS, D)
    if last:
        outs = [mat, mat, col]
        scratch = [pltpu.VMEM(col, F32), pltpu.VMEM(col, F32), pltpu.VMEM(mat, F32)]
    else:
        outs, scratch = [col, col, mat], []
    return pl.pallas_call(
        partial(lookup_kernel, len(tables), last),
        grid=(rows // tile,),
        in_specs=[fixed(mat)]
        + [pl.BlockSpec((tile, D), lambda i: (i, 0))] * len(tables)
        + ([fixed(col), fixed(col), fixed(mat)] if last else []),
        out_specs=[fixed(o) for o in outs],
        out_shape=[shape(o, F32) for o in outs],
        scratch_shapes=scratch,
        compiler_params=pltpu.CompilerParams(vmem_limit_bytes=ROOM),
        cost_estimate=SMALL_COST,
        name=f"lookup_{int(last)}",
    )(hidden, *tables, *(state if last else ()))


WIDE = 1024


def over_table(moves, tables, buffer, fold):
    count = len(tables)
    tile = buffer.shape[0] // count
    steps = tables[0].shape[0] // tile
    wide = min(WIDE, buffer.shape[0])
    sems = [moves.sem() for _ in tables]

    def step(i):
        copies = []
        for n, (table, sem) in enumerate(zip(tables, sems)):
            src = table if steps == 1 else table.at[pl.ds(pl.multiple_of(i * tile, tile), tile), :]
            copies.append(pltpu.make_async_copy(src, buffer.at[pl.ds(tile * n, tile), :], sem))
            copies[-1].start()
        for j in range(buffer.shape[0] // wide):
            for copy in copies[wide * j // tile : wide * (j + 1) // tile]:
                copy.wait()
            fold(slice(wide * j, wide * (j + 1)))

    if steps == 1:
        step(0)
    else:
        lax.fori_loop(0, steps, lambda i, carry: (step(i), carry)[1], 0)


def table_buffer(tables):
    return ((len(tables) * min(TILE, tables[0].shape[0]), D), BF16)


def lookup_back(scal, hidden, code, lse, inner, tables):
    count = len(tables)

    def body(moves, scal, *refs):
        ins, tables, refs = refs[:4], refs[4 : 4 + count], refs[4 + count :]
        out_o, keep_o, send_o, hid, code, lse, inner, buffer, out, low = refs
        for wait in [moves.load(src, dst) for src, dst in zip(ins, (hid, code, lse, inner))]:
            wait()
        out[...] = jnp.zeros((ROWS, D), F32)

        def fold(rows):
            s = dot_rows(hid[...], buffer[rows, :]) * D**-0.5
            p = jnp.exp(s - lse[...])
            dp = dot_rows(code[...], buffer[rows, :])
            ds = (p * (dp - inner[...])).astype(BF16)
            out[...] += dot(ds, buffer[rows, :])

        over_table(moves, tables, buffer, fold)
        value = out[...] * D**-0.5
        out[...] = value
        moves.store(out, out_o)
        low[...] = value.astype(BF16)
        moves.store(low.at[:, half_of(scal, HALF)], keep_o)
        moves.store(low.at[:, half_of(scal, HALF, False)], send_o)

    part = ((ROWS, HALF), BF16)
    return call(
        body, "lookup_back", scal, [hidden, code, lse, inner, *tables], outputs(MAT, part, part),
        [LOW, LOW, COL, COL, table_buffer(tables), MAT, LOW],
    )


def swapped(value):
    return lax.ppermute(value, "section", [(0, 1), (1, 0)])


def bit_count():
    size = lax.axis_size("dp")
    count = size.bit_length() - 1
    assert size == 1 << count
    return count


def across(value, step):
    size = lax.axis_size("dp")
    return lax.ppermute(value, "dp", [(i, i ^ step) for i in range(size)])


def along(value, bit):
    return across(value, 1 << bit)


def after(value, *others):
    return lax.optimization_barrier((value, *others))[0]


def total(terms):
    summed = terms[0].astype(F32)
    for term in terms[1:]:
        summed = summed + term.astype(F32)
    return summed


class Share:
    def __init__(self, parts, order):
        self.order = order
        if len(parts) == 2:
            self.terms, self.ready = [parts[0]], parts[1]
        else:
            count = len(order)
            value = parts[0].reshape((-1,) + (2,) * count + (D >> count, HALF))
            axes = [count - bit for bit in order]
            self.terms, self.ready = [value.transpose(axes + [0, count + 1, count + 2])], None

    def split(self, stage):
        if stage == 0 and self.ready is not None:
            return self.ready
        mine = (lax.axis_index("dp") >> self.order[stage]) & 1

        def pick(which):
            return [lax.dynamic_index_in_dim(t, which, 0, keepdims=False) for t in self.terms]

        sent = total(pick(1 - mine)).astype(BF16)
        self.terms = pick(mine)
        return sent

    def send(self, stage, *values):
        self.sent = after(self.split(stage), *values)
        self.got = along(self.sent, self.order[stage])

    def receive(self, *values):
        self.terms.append(after(self.got, *values))


class Group:
    def __init__(self, parts, orders, joint):
        self.shares = [Share(part, order) for part, order in zip(parts, orders)]
        self.joint = joint

    def ready(self):
        return [share.terms[0] for share in self.shares]

    def send(self, stage, *values):
        if stage < self.joint:
            for share in self.shares:
                share.send(stage, *values)
            self.sent = [share.sent for share in self.shares]
        else:
            self.sent = [after(jnp.stack([share.split(stage) for share in self.shares]), *values)]
            self.got = along(self.sent[0], self.shares[0].order[stage])

    def receive(self, stage, *values):
        if stage < self.joint:
            for share in self.shares:
                share.receive(*values)
        else:
            got = after(self.got, *values)
            for i, share in enumerate(self.shares):
                share.terms.append(got[i])

    def result(self):
        sums = jnp.concatenate([total(share.terms) for share in self.shares])
        return sums.reshape((2, -1) + sums.shape[-2:])


def pair_orders():
    far = list(range(2, bit_count()))
    return [0, 1] + far, [1, 0] + far


def pair(parts):
    return Group(parts, pair_orders(), 2)


def far_order():
    return [list(range(2, bit_count())) + [0, 1]]


def per_device(
    patches,
    recon_cot,
    lengths,
    codebook,
    w_qkv,
    w_out,
    w_up,
    w_down,
    norm_gain,
    norm_bias,
    bias_out,
    bias_up,
):
    section = lax.axis_index("section")
    on_first = section == 0
    size = lax.axis_size("dp")
    count = bit_count()
    me = lax.axis_index("dp")
    scal = jnp.stack([section, *((me >> bit) & 1 for bit in range(count))]).astype(jnp.int32)
    own_small = pack_small(norm_gain, norm_bias, bias_out, bias_up)
    small = (lengths, own_small, swapped(own_small))
    weights = [(w[0], swapped(w[0])) for w in (w_qkv, w_out)]

    table = codebook
    for bit in range(count - 1, 2, -1):
        got = after(along(table, bit), small[2], weights[0][1], weights[1][1])
        table = jnp.concatenate([table, got])
    weights += [(w[0], swapped(after(w[0], table))) for w in (w_up, w_down)]
    got = along(table, 2)
    from_table = along(table, 1)
    facts_ea, qkv_e, probs_e = att_forward(0, after(scal, table), patches, small, weights)
    got = after(got, facts_ea)
    from_got = along(got, 0)
    left = jnp.concatenate([table, after(from_table, got)])
    late = [along(left, 0)]
    right = jnp.concatenate([got, after(from_got, left)])
    late.append(along(right, 1))
    pieces = [left, right]
    pieces_other = [swapped(piece) for piece in pieces]
    hidden, facts_ef, resid_e, slope_e = ffn_forward(
        0, after(scal, *pieces), patches, small, facts_ea, weights
    )
    state = lookup(hidden, pieces + pieces_other)
    late = after(late, state[0])
    late_other = [swapped(piece) for piece in late]
    tables = pieces + pieces_other + late + late_other
    mean_code, unit, lse = lookup(hidden, late + late_other, state)
    facts_ea = (facts_ea, swapped(after(facts_ea, *late_other)))
    facts_ef = (facts_ef, swapped(after(facts_ef, *late_other)))
    recon, facts_df, facts_da, qkv_d, probs_d, resid_d, slope_d = block_forward(
        1, after(scal, facts_ea[1], facts_ef[1]), unit, small, weights
    )
    facts_df = (facts_df, swapped(facts_df))
    facts_da = (facts_da, swapped(facts_da))
    recon_first = lax.ppermute(recon, "section", [(0, 1)])
    lse_other = swapped(lse)

    keep, send, d_resid, sums_df = ffn_backward(
        1, scal, recon_cot, slope_d, resid_d, small, weights, True
    )
    first_f = pair(ffn_grads(after(scal, keep), facts_df, (keep, swapped(send)), [recon_cot], count, pair_orders(), True))
    first_f.send(0)
    keep, send, sums_da, code, inner = att_backward(
        1, after(scal, facts_da[1], *first_f.sent), d_resid, qkv_d, probs_d, unit, small, weights, mean_code
    )
    got = swapped(send)
    d_hidden, g_keep, g_send = lookup_back(scal, hidden, code, lse, inner, tables)
    g_got = swapped(g_send)
    first_f.receive(0, d_hidden, recon_first, lse_other)
    first_f.send(1)
    first_a = pair(att_grads(after(scal, *first_f.sent), facts_da, (keep, got), count, pair_orders()))
    first_a.send(0)
    keep, send, d_resid, sums_ef = ffn_backward(
        0, after(scal, g_got, *first_a.sent), d_hidden, slope_e, resid_e, small, weights, False
    )
    got = swapped(send)
    first_f.receive(1, keep)
    first_f.send(2)
    second_f = pair(
        ffn_grads(after(scal, keep, *first_f.sent), facts_ef, (keep, got), (g_keep, g_got), count, pair_orders(), False)
    )
    second_f.send(0)
    first_a.receive(0, *second_f.ready())
    first_a.send(1)
    keep, send, sums, sums_send, grad_x = att_backward(
        0, after(scal, *second_f.sent, *first_a.sent), d_resid, qkv_e, probs_e, patches, small, weights,
        sums_before=(sums_ef, sums_df, sums_da),
    )
    got = swapped(send)
    sums_got = swapped(sums_send)
    first_f.receive(2, sums)
    first_f.send(3)
    second_a = pair(att_grads(after(scal, sums_got, *first_f.sent), facts_ea, (keep, got), count, pair_orders()))
    second_f.receive(0, *second_a.ready())
    second_f.send(1)
    first_a.receive(1, *second_f.sent)
    closed = [share.terms[-1] for share in first_a.shares]
    if count == 4:
        first_f.receive(3, *closed)
        closed = [first_f.shares[0].terms[-1]]
    second_a.send(0, *closed)
    first_a.send(2, *second_a.sent)
    second_f.receive(1, *first_a.sent)
    second_f.send(2)
    sums = sums + after(sums_got, *second_f.sent)
    sums_got = along(sums, 2)
    first_a.receive(2, sums)
    first_a.send(3)
    grad_second = lax.ppermute(after(grad_x, sums), "section", [(1, 0)])
    second_a.receive(0, *first_a.sent)
    second_a.send(1)
    first_a.receive(3, grad_second, *second_a.sent)
    second_f.receive(2, first_a.shares[0].terms[-1])
    second_f.send(3)
    sums = sums + after(sums_got, *second_f.sent)
    sums_got = along(sums, 0)
    second_a.receive(1, sums)
    second_a.send(2)
    sums = sums + after(sums_got, *second_a.sent)
    sums_got = along(sums, 1)
    last = second_a.sent
    if count > 4:
        first_a.send(4)
        waiting = [[first_f, 3], [first_a, 4], [second_f, 3]]
        for step in range(count):
            for entry in waiting:
                group, stage = entry
                if stage < count - (1 if group is second_f else 0):
                    group.receive(stage, *last)
                    if stage + 1 < count:
                        group.send(stage + 1)
                        last = group.sent
                    entry[1] += 1
    ends = jnp.where(
        on_first, jnp.concatenate([grad_x, grad_second]), jnp.concatenate([recon_first, recon])
    )[None]
    lse, lse_other = after([lse, lse_other], *last)
    lse, lse_other = lse[:, 0], lse_other[:, 0]
    codes = jnp.where(on_first, jnp.concatenate([lse, lse_other]), jnp.concatenate([lse_other, lse]))
    sums = sums + after(sums_got, *last)
    sums_got = along(sums, 3)
    for bit in range(4, count):
        sums = sums + sums_got
        sums_got = along(sums, bit)
    for stage in range(2, count - 1):
        second_a.receive(stage, sums, codes)
        second_a.send(stage + 1)
    sums = sums + after(sums_got, *second_a.sent)
    width = D // size
    rows = lax.dynamic_slice_in_dim(sums, me * width, width, axis=1)
    grad_gain = jnp.stack([rows[8], rows[0]])[None]
    grad_nbias = jnp.stack([rows[9], rows[1]])[None]
    grad_bout = jnp.stack([rows[3], rows[2]])[None]
    grad_bup = lax.dynamic_slice_in_dim(sums[4:8].reshape(FF), me * width * 4, width * 4)[None]
    second_f.receive(count - 1, grad_gain, grad_nbias, grad_bout, grad_bup, ends)

    def shared_out(encoder, decoder):
        encoder, decoder = encoder.result(), decoder.result()
        return jnp.where(on_first, encoder, decoder), swapped(jnp.where(on_first, decoder, encoder))

    ffn = shared_out(second_f, first_f)
    second_a.receive(count - 1, ffn[0])
    att = shared_out(second_a, first_a)
    grad_qkv, grad_out, grad_up, grad_down = finish(scal, *ffn, *att)
    return (ends, codes, grad_qkv, grad_out, grad_up, grad_down, grad_gain, grad_nbias, grad_bout, grad_bup)


def solution(mesh):
    placed = (
        P("dp", None),
        P("dp", None),
        P("dp", None),
        P(("dp", "section"), None),
        P("section", None, None),
        P("section", None, None),
        P("section", None, None),
        P("section", None, None),
        P("section", None, None),
        P("section", None, None),
        P("section", None, None),
        P("section", None),
    )
    return jax.shard_map(
        per_device,
        mesh=mesh,
        in_specs=placed,
        out_specs=(
            P("section", "dp", None),
            P("dp"),
            P("section", "dp", None),
            P("section", "dp", None),
            P("section", "dp", None),
            P("section", "dp", None),
            P("section", None, "dp"),
            P("section", None, "dp"),
            P("section", None, "dp"),
            P("section", "dp"),
        ),
        check_vma=False,
    )
```

```python
from functools import partial

import jax
import jax.numpy as jnp
from jax import lax
from jax.experimental import pallas as pl
from jax.experimental.layout import Layout, with_layout_constraint
from jax.experimental.pallas import tpu as pltpu
from jax.sharding import PartitionSpec as P

D = 768
HEADS = 12
HD = 64
FF = 3072
ROWS = 256
PAIR = 2 * HD
EPS = 1e-06
MASKED = -1e30
F32 = jnp.float32
BF16 = jnp.bfloat16
N2, FFN_FACTS = FF, FF + D
MIX, ATT_FACTS = D, 2 * D
HALF = D // 2
HALF_UP = FF // 2
HALF_QKV = 3 * D // 2
TAIL_P = 0.35
TAIL = (0.19620077326315646, 0.2185939781557991, 0.05480664657447366, 0.5651487076988272,
        -0.5574354264567037, 0.7060774515721405, -0.18339209581143395)
VMEM = pl.BlockSpec(memory_space=pltpu.VMEM)
SMEM = pl.BlockSpec(memory_space=pltpu.SMEM)
ANY = pl.BlockSpec(memory_space=pl.ANY)
ROOM = 63 * 1024 * 1024


def dot(a, b):
    return jnp.dot(a, b, preferred_element_type=F32)


def dot_rows(a, b):
    return lax.dot_general(a, b, (((1,), (1,)), ((), ())), preferred_element_type=F32)


def dot_cols(a, b):
    return lax.dot_general(a, b, (((0,), (0,)), ((), ())), preferred_element_type=F32)


def unit_rows(values):
    centre = values - jnp.mean(values, axis=-1, keepdims=True)
    inverse = lax.rsqrt(jnp.mean(centre * centre, axis=-1, keepdims=True) + EPS)
    return centre * inverse, inverse


def norm_back(scaled, unit, inverse):
    return inverse * (
        scaled
        - jnp.mean(scaled, axis=-1, keepdims=True)
        - unit * jnp.mean(scaled * unit, axis=-1, keepdims=True)
    )


def gelu_parts(z):
    bell = jnp.exp(-0.5 * z * z)
    t = 1.0 / (1.0 + (TAIL_P * 0.5**0.5) * jnp.abs(z))
    poly = TAIL[6] * t + TAIL[5]
    for c in TAIL[4::-1]:
        poly = poly * t + c
    tail = 0.5 * poly * t * bell
    cdf = jnp.where(z >= 0, 1.0 - tail, tail)
    return z * cdf, cdf + z * bell * 0.3989422804014327


def image_ids(scal, lens, shape, axis):
    position = lax.broadcasted_iota(jnp.int32, shape, axis)
    limit = jnp.int32(0)
    ids = jnp.zeros(shape, jnp.int32)
    for i in range(4):
        limit = limit + lens[scal[0], i]
        ids = ids + (position >= limit).astype(jnp.int32)
    return ids


def shape(s, t):
    return jax.ShapeDtypeStruct(s, t)


class Moves:
    def __init__(self, sems):
        self.sems = sems
        self.used = 0
        self.leaving = []

    def sem(self):
        self.used += 1
        return self.sems.at[self.used - 1]

    def load(self, src, dst):
        copy = pltpu.make_async_copy(src, dst, self.sem())
        copy.start()
        return copy.wait

    def load_either(self, first, src, other, dst):
        sem = self.sem()
        for take, ref in ((first, src), (jnp.logical_not(first), other)):
            @pl.when(take)
            def _():
                pltpu.make_async_copy(ref, dst, sem).start()

        return pltpu.make_async_copy(src, dst, sem).wait

    def load_tiles(self, first, src, other, dst, axis):
        tiles = []
        for j in range(dst.shape[axis] // D):
            at = (pl.ds(D * j, D),) if axis == 0 else (slice(None), pl.ds(D * j, D))
            tiles.append((at, self.sem()))
        for take, ref in ((first, src), (jnp.logical_not(first), other)):
            @pl.when(take)
            def _():
                for at, sem in tiles:
                    pltpu.make_async_copy(ref.at[at], dst.at[at], sem).start()

        return [pltpu.make_async_copy(src.at[at], dst.at[at], sem).wait for at, sem in tiles]

    def store(self, src, dst):
        copy = pltpu.make_async_copy(src, dst, self.sem())
        copy.start()
        self.leaving.append(copy.wait)

    def finish(self):
        for wait in self.leaving:
            wait()


SEMS = 32
SMALL_COST = pl.CostEstimate(flops=1000, bytes_accessed=1000, transcendentals=0)


def call(body, name, scal, inputs, outs, scratch, small=None):
    extra = () if small is None else small[1:]

    def kernel(*refs):
        scal, *refs = refs
        moves = Moves(refs[-1])
        if small is None:
            body(moves, scal, *refs[:-1])
        else:
            lens, own, other, *refs = refs
            chosen = refs[-2]
            chosen[...] = jnp.where(scal[0] == small[0], own[...], other[...])
            body(moves, scal, lens, chosen, *refs[:-2])
        moves.finish()

    return pl.pallas_call(
        kernel,
        in_specs=[SMEM] + [SMEM, VMEM, VMEM][: len(extra)] + [ANY] * len(inputs),
        out_specs=[ANY] * len(outs),
        out_shape=outs,
        scratch_shapes=[
            *(pltpu.VMEM(s, t) for s, t in (*scratch, *([SMALL] if extra else []))),
            pltpu.SemaphoreType.DMA((SEMS,)),
        ],
        compiler_params=pltpu.CompilerParams(vmem_limit_bytes=ROOM),
        cost_estimate=SMALL_COST,
        name=name,
    )(scal, *extra, *inputs)


SMALL = ((10, D), F32)
W_QKV = ((D, 3 * D), BF16)
W_OUT = ((D, D), BF16)
W_UP = ((D, FF), BF16)
W_DOWN = ((FF, D), BF16)
MAT = ((ROWS, D), F32)
LOW = ((ROWS, D), BF16)
COL = ((ROWS, 1), F32)


def rows_of(scal, own=True):
    which = scal[0] if own else 1 - scal[0]
    return pl.ds(pl.multiple_of(which * ROWS, ROWS), ROWS)


def half_of(scal, width, own=True):
    which = scal[0] if own else 1 - scal[0]
    return pl.ds(pl.multiple_of(which * width, 128), width)


def pack_small(gains, shifts, bias_out, bias_up):
    def kernel(gains, shifts, bias_out, bias_up, out):
        for i, ref in enumerate((gains, shifts, bias_out)):
            out[2 * i : 2 * i + 2, :] = ref[0]
        for j in range(FF // D):
            out[6 + j : 7 + j, :] = bias_up[:, D * j : D * (j + 1)]

    return pl.pallas_call(
        kernel, in_specs=[VMEM] * 4, out_specs=VMEM, out_shape=shape(*SMALL), cost_estimate=SMALL_COST, name="pack_small",
    )(gains, shifts, bias_out, bias_up)


def by_head(pair, first):
    zero = jnp.zeros_like(pair)
    return jnp.concatenate([jnp.where(first, pair, zero), jnp.where(first, zero, pair)])


def att_forward_part(moves, scal, lens, x, small, wq, wait, facts, qkv, probs, out):
    facts_hbm, qkv_hbm, probs_hbm = out
    unit, _ = unit_rows(x)
    n1 = (unit * small[0:1, :] + small[2:3, :]).astype(BF16)
    facts[:, :D] = n1
    same = image_ids(scal, lens, (ROWS, ROWS), 0) == image_ids(scal, lens, (ROWS, ROWS), 1)
    bias = jnp.where(same, 0.0, MASKED)
    first = lax.broadcasted_iota(jnp.int32, (1, PAIR), 1) < HD
    for j in range(3):
        wait[j]()
        qkv[:, D * j : D * (j + 1)] = dot(n1, wq[:, D * j : D * (j + 1)]).astype(BF16)
    moves.store(qkv, qkv_hbm)
    both = jnp.concatenate([bias, bias])
    for p in range(HEADS // 2):
        q = by_head(qkv[:, PAIR * p : PAIR * (p + 1)] * jnp.asarray(HD**-0.5, BF16), first)
        k = qkv[:, D + PAIR * p : D + PAIR * (p + 1)]
        v = qkv[:, 2 * D + PAIR * p : 2 * D + PAIR * (p + 1)]
        s = dot_rows(q, k) + both
        s = jnp.exp(s - jnp.max(s, axis=-1, keepdims=True))
        pr = (s * (1.0 / jnp.sum(s, axis=-1, keepdims=True))).astype(BF16)
        probs[2 * p : 2 * p + 2] = pr.reshape(2, ROWS, ROWS)
        out = dot(pr, v)
        facts[:, MIX + PAIR * p : MIX + PAIR * (p + 1)] = jnp.where(first, out[:ROWS], out[ROWS:]).astype(BF16)
    moves.store(probs, probs_hbm)
    moves.store(facts, facts_hbm)


def ffn_forward_part(moves, x, small, mixed, wo, wu, wd, waits, facts, resid_ref, slope, y_ref, out):
    y_hbm, facts_hbm, resid_hbm, slope_hbm = out
    waits[0]()
    resid = x + dot(mixed, wo[...]) + small[4:5, :]
    resid_ref[...] = resid
    moves.store(resid_ref, resid_hbm)
    unit, _ = unit_rows(resid)
    n2 = (unit * small[1:2, :] + small[3:4, :]).astype(BF16)
    facts[:, N2 : N2 + D] = n2
    y = resid + small[5:6, :]
    tiles = FF // D

    def pre_tile(j):
        waits[1][j]()
        return dot(n2, wu[:, D * j : D * (j + 1)]) + small[6 + j : 7 + j, :]

    pre = pre_tile(0)
    for j in range(tiles):
        cols = slice(D * j, D * (j + 1))
        waits[2][j]()
        later = pre_tile(j + 1) if j + 1 < tiles else None
        act, sl = gelu_parts(pre)
        act = act.astype(BF16)
        facts[:, cols] = act
        slope[:, cols] = sl.astype(BF16)
        y = y + dot(act, wd[cols, :])
        pre = later
    moves.store(facts, facts_hbm)
    moves.store(slope, slope_hbm)
    y_ref[...] = y.astype(y_ref.dtype)
    moves.store(y_ref, y_hbm)


FACTS_A = ((ROWS, ATT_FACTS), BF16)
FACTS_F = ((ROWS, FFN_FACTS), BF16)
QKV = ((ROWS, 3 * D), BF16)
PROBS = ((HEADS, ROWS, ROWS), BF16)
SLOPE = ((ROWS, FF), BF16)


def outputs(*kinds):
    return [shape(*kind) for kind in kinds]


def block_forward(block, scal, x, small, weights):
    def body(moves, scal, lens, small, x_in, wq_a, wq_b, wo_a, wo_b, wu_a, wu_b, wd_a, wd_b,
             y_o, facts_fo, facts_ao, qkv_o, probs_o, resid_o, slope_o,
             x, wq, wo, wu, wd, y, facts_f, facts_a, qkv, probs, resid, slope):
        own = scal[0] == block
        wait_x = moves.load(x_in, x)
        wait_q = moves.load_tiles(own, wq_a, wq_b, wq, 1)
        waits = [moves.load_either(own, a, b, w) for a, b, w in ((wo_a, wo_b, wo), (wu_a, wu_b, wu), (wd_a, wd_b, wd))]
        waits = [waits[0]] + [[wait] + [lambda: None] * 3 for wait in waits[1:]]
        wait_x()
        xs = x[...]
        att_forward_part(moves, scal, lens, xs, small, wq, wait_q, facts_a, qkv, probs, (facts_ao, qkv_o, probs_o))
        ffn_forward_part(
            moves, xs, small, facts_a[:, MIX : MIX + D], wo, wu, wd, waits, facts_f, resid, slope, y,
            (y_o, facts_fo, resid_o, slope_o),
        )

    kinds = (MAT, FACTS_F, FACTS_A, QKV, PROBS, MAT, SLOPE)
    return call(
        body, f"forward_{block}", scal, [x, *sum(weights, ())], outputs(*kinds),
        [MAT, W_QKV, W_OUT, W_UP, W_DOWN, *kinds], (block, *small),
    )


def att_forward(block, scal, patches, small, weights):
    def body(moves, scal, lens, small, x_in, wq_a, wq_b, facts_o, qkv_o, probs_o, x, wq, facts, qkv, probs):
        wait_x = moves.load(x_in.at[rows_of(scal), :], x)
        wait_w = moves.load_tiles(scal[0] == block, wq_a, wq_b, wq, 1)
        wait_x()
        att_forward_part(
            moves, scal, lens, x[...].astype(F32), small, wq, wait_w, facts, qkv, probs, (facts_o, qkv_o, probs_o)
        )

    kinds = (FACTS_A, QKV, PROBS)
    return call(
        body, f"att_forward_{block}", scal, [patches, *weights[0]], outputs(*kinds),
        [LOW, W_QKV, *kinds], (block, *small),
    )


def ffn_forward(block, scal, patches, small, facts_a, weights):
    def body(moves, scal, lens, small, x_in, facts_ai, wo_a, wo_b, wu_a, wu_b, wd_a, wd_b,
             y_o, facts_o, resid_o, slope_o, x, mixed, wo, wu, wd, y, facts, resid, slope):
        own = scal[0] == block
        wait_x = moves.load(x_in.at[rows_of(scal), :], x)
        wait_m = moves.load(facts_ai.at[:, pl.ds(MIX, D)], mixed)
        waits = [
            moves.load_either(own, wo_a, wo_b, wo),
            moves.load_tiles(own, wu_a, wu_b, wu, 1),
            moves.load_tiles(own, wd_a, wd_b, wd, 0),
        ]
        wait_x()
        wait_m()
        ffn_forward_part(
            moves, x[...].astype(F32), small, mixed[...], wo, wu, wd, waits, facts, resid, slope, y,
            (y_o, facts_o, resid_o, slope_o),
        )

    kinds = (LOW, FACTS_F, MAT, SLOPE)
    return call(
        body, f"ffn_forward_{block}", scal, [patches, facts_a, *sum(weights[1:], ())], outputs(*kinds),
        [LOW, LOW, W_OUT, W_UP, W_DOWN, *kinds], (block, *small),
    )


COT_UP = ((ROWS, HALF_UP), BF16)
COT_ATT = ((ROWS, HALF_QKV + HALF), BF16)
SUMS = ((8, D), F32)


def ffn_backward(block, scal, g, slope, resid, small, weights, own_rows):
    def body(moves, scal, lens, small, g_in, slope_in, resid_in, wu_a, wu_b, wd_a, wd_b,
             keep_o, send_o, dres_o, sums, g_ref, slope, resid, wu, wd, d_pre_ref, dres):
        own = scal[0] == block
        wait_g = moves.load(g_in.at[rows_of(scal), :] if own_rows else g_in, g_ref)
        wait_d = moves.load_tiles(own, wd_a, wd_b, wd, 0)
        wait_s = moves.load(slope_in, slope)
        wait_u = moves.load_tiles(own, wu_a, wu_b, wu, 1)
        wait_r = moves.load(resid_in, resid)
        wait_g()
        g = g_ref[...].astype(F32)
        gl = g.astype(BF16)
        small_sums = [None] * 4
        small_sums[2] = jnp.sum(g, axis=0, keepdims=True)
        d_n2 = jnp.zeros((ROWS, D), F32)
        up_sums = []
        tiles = FF // D

        def act_tile(j):
            wait_d[j]()
            return dot_rows(gl, wd[D * j : D * (j + 1), :])

        later = act_tile(0)
        wait_s()
        for j in range(tiles):
            cols = slice(D * j, D * (j + 1))
            wait_u[j]()
            d_act = later
            later = act_tile(j + 1) if j + 1 < tiles else None
            d_pre = (d_act * slope[:, cols].astype(F32)).astype(BF16)
            d_pre_ref[:, cols] = d_pre
            up_sums.append(jnp.sum(d_pre.astype(F32), axis=0, keepdims=True))
            d_n2 = d_n2 + dot_rows(d_pre, wu[:, cols])
        moves.store(d_pre_ref.at[:, half_of(scal, HALF_UP)], keep_o)
        moves.store(d_pre_ref.at[:, half_of(scal, HALF_UP, False)], send_o)
        wait_r()
        unit, inverse = unit_rows(resid[...])
        small_sums[0] = jnp.sum(d_n2 * unit, axis=0, keepdims=True)
        small_sums[1] = jnp.sum(d_n2, axis=0, keepdims=True)
        d_resid = g + norm_back(d_n2 * small[1:2, :], unit, inverse)
        dres[...] = d_resid
        moves.store(dres, dres_o)
        small_sums[3] = jnp.sum(d_resid, axis=0, keepdims=True)
        for i, value in enumerate(small_sums + up_sums):
            sums[i : i + 1, :] = value

    def with_sums(moves, *refs):
        *head, sums_buffer = refs
        sums_o = head[13]
        head[13] = sums_buffer
        body(moves, *head)
        moves.store(sums_buffer, sums_o)

    g_kind = (tuple(g.shape), g.dtype) if not own_rows else ((ROWS, D), g.dtype)
    return call(
        with_sums, f"ffn_backward_{block}", scal, [g, slope, resid, *weights[2], *weights[3]],
        outputs(COT_UP, COT_UP, MAT, SUMS),
        [g_kind, SLOPE, MAT, W_UP, W_DOWN, SLOPE, MAT, SUMS], (block, *small),
    )


def att_backward(block, scal, d_resid, qkv, probs, x, small, weights, mean_code=None, sums_before=None):
    final = mean_code is None

    def body(moves, scal, lens, small, dres_in, qkv_in, probs_in, x_in, wq_a, wq_b, wo_a, wo_b, *rest):
        if final:
            (ef_in, df_in, da_in, keep_o, send_o, own_o, other_o, gx_o,
             dres, qkv, probs, x_ref, wq, wo, d_qkv, rl_ref, sums, ef, df, da, packed, gx) = rest
            wait_sums = [moves.load(src, dst) for src, dst in ((ef_in, ef), (df_in, df), (da_in, da))]
        else:
            (mean_in, keep_o, send_o, sums_o, code_o, inner_o,
             dres, qkv, probs, x_ref, wq, wo, d_qkv, rl_ref, sums, mean_ref, code_ref, inner_ref) = rest
        own = scal[0] == block
        wait_g = moves.load(dres_in, dres)
        wait_o = moves.load_either(own, wo_a, wo_b, wo)
        wait_k = moves.load(qkv_in, qkv)
        wait_p = moves.load(probs_in, probs)
        wait_q = moves.load_either(own, wq_a, wq_b, wq)
        wait_x = moves.load(x_in.at[rows_of(scal), :] if final else x_in, x_ref)
        if not final:
            wait_m = moves.load(mean_in, mean_ref)
        wait_g()
        d_resid = dres[...]
        rl = d_resid.astype(BF16)
        rl_ref[...] = rl
        for out, mine in ((keep_o, True), (send_o, False)):
            moves.store(rl_ref.at[:, half_of(scal, HALF, mine)], out.at[:, pl.ds(HALF_QKV, HALF)])
        first = lax.broadcasted_iota(jnp.int32, (1, PAIR), 1) < HD
        wait_o()
        d_mixed = dot_rows(rl, wo[...]).astype(BF16)
        wait_k()
        wait_p()
        scale = jnp.asarray(HD**-0.5, BF16)
        for p in range(HEADS // 2):
            q = qkv[:, PAIR * p : PAIR * (p + 1)] * scale
            k = qkv[:, D + PAIR * p : D + PAIR * (p + 1)]
            v = qkv[:, 2 * D + PAIR * p : 2 * D + PAIR * (p + 1)]
            dm = d_mixed[:, PAIR * p : PAIR * (p + 1)]
            dm = by_head(dm, first)
            pr = probs[2 * p : 2 * p + 2].reshape(2 * ROWS, ROWS)
            dp = dot_rows(dm, v)
            prf = pr.astype(F32)
            ds = (prf * (dp - jnp.sum(dp * prf, axis=-1, keepdims=True))).astype(BF16)
            dq = dot(ds, k)
            dq = jnp.where(first, dq[:ROWS], dq[ROWS:]) * HD**-0.5
            for at, value in ((0, dq), (D, dot_cols(ds, by_head(q, first))), (2 * D, dot_cols(pr, dm))):
                d_qkv[:, at + PAIR * p : at + PAIR * (p + 1)] = value.astype(BF16)
        for out, mine in ((keep_o, True), (send_o, False)):
            moves.store(d_qkv.at[:, half_of(scal, HALF_QKV, mine)], out.at[:, pl.ds(0, HALF_QKV)])
        wait_q()
        d_n1 = dot_rows(d_qkv[...], wq[...])
        wait_x()
        x = x_ref[...].astype(F32)
        unit, inverse = unit_rows(x)
        sums[0:1, :] = jnp.sum(d_n1 * unit, axis=0, keepdims=True)
        sums[1:2, :] = jnp.sum(d_n1, axis=0, keepdims=True)
        if final:
            for wait in wait_sums:
                wait()
            for i, (ffn, att) in enumerate(((ef, sums), (df, da))):
                packed[i, 0:8, :] = ffn[...]
                packed[i, 8:10, :] = att[0:2, :]
            moves.store(packed.at[scal[0]], own_o)
            moves.store(packed.at[1 - scal[0]], other_o)
        else:
            sums[2:8, :] = jnp.zeros((6, D), F32)
            moves.store(sums, sums_o)
        grad_x = d_resid + norm_back(d_n1 * small[0:1, :], unit, inverse)
        if final:
            gx[...] = grad_x
            moves.store(gx, gx_o)
        else:
            wait_m()
            mean_code = mean_ref[...]
            inv = lax.rsqrt(jnp.mean(mean_code * mean_code, axis=-1, keepdims=True) + EPS)
            code = inv * (grad_x - x * jnp.mean(grad_x * x, axis=-1, keepdims=True))
            code = code.astype(BF16)
            code_ref[...] = code
            moves.store(code_ref, code_o)
            inner_ref[...] = jnp.sum(code.astype(F32) * mean_code, axis=-1, keepdims=True)
            moves.store(inner_ref, inner_o)

    if final:
        more_in, more, sums_out = [*sums_before], [MAT], [SMALL, SMALL]
        more_scratch = [SUMS, SUMS, SUMS, ((2, 10, D), F32)]
    else:
        more_in, more, sums_out = [mean_code], [LOW, COL], [SUMS]
        more_scratch = [MAT]
    return call(
        body, f"att_backward_{block}", scal, [d_resid, qkv, probs, x, *weights[0], *weights[1], *more_in],
        outputs(COT_ATT, COT_ATT, *sums_out, *more),
        [MAT, QKV, PROBS, LOW if final else MAT, W_QKV, W_OUT, QKV, LOW, SUMS, *more_scratch, *more],
        (block, *small),
    )


def group_outputs(kinds, order, count):
    width = D >> count
    if width % 16:
        return [((kinds, D, HALF), BF16)], ((kinds, D, HALF), BF16)
    tail = (kinds, width, HALF)
    return [((2,) * (count - 1) + tail, BF16)] * 2, ((2,) * count + tail, BF16)


def put(buffer, order, kind, value, owner=0):
    if len(buffer.shape) == 3:
        width = D >> len(order)
        buffer[kind, width * owner : width * owner + value.shape[0], :] = value
        return
    width = buffer.shape[-2]
    for i in range(value.shape[0] // width):
        place = tuple((owner + i) >> bit & 1 for bit in order)
        buffer[place + (kind,)] = value[width * i : width * (i + 1)]


def leave(moves, buffer, outs, mine):
    if len(outs) == 1:
        moves.store(buffer, outs[0])
    else:
        moves.store(buffer.at[mine], outs[0])
        moves.store(buffer.at[1 - mine], outs[1])


def ffn_grads(scal, facts, cots, outs_g, count, orders, both):
    down, down_buffer = group_outputs(FF // D, orders[0], count)
    up, up_buffer = group_outputs(HALF_UP // HALF, orders[1], count)
    width = D >> count
    given = 4 + len(outs_g)

    def body(moves, scal, *refs):
        ins, outs, (fa, fb, ca, cb, ga, gb, buf_d, buf_u) = refs[:given], refs[given:-8], refs[-8:]
        if both:
            wait_g = [
                moves.load(ins[4].at[rows_of(scal, own), half_of(scal, HALF)], g)
                for g, own in ((ga, True), (gb, False))
            ]
        else:
            wait_g = [moves.load(ref, g) for ref, g in zip(ins[4:], (ga, gb))]
        wait_f = []
        for j in range(FFN_FACTS // D):
            cols = pl.ds(D * j, D)
            wait_f.append([moves.load(src.at[:, cols], dst.at[:, cols]) for src, dst in zip(ins, (fa, fb))])
        wait_c = [moves.load(ref, c) for ref, c in zip(ins[2:4], (ca, cb))]
        for wait in wait_g:
            wait()
        for j in range(FF // D):
            cols = slice(D * j, D * (j + 1))
            for wait in wait_f[j]:
                wait()
            value = dot_cols(fa[:, cols], ga[...]) + dot_cols(fb[:, cols], gb[...])
            value = value.astype(BF16)
            owners = D // (4 * width)
            for i in range(owners):
                for kind in range(4):
                    at = width * (4 * i + kind)
                    put(buf_d, orders[0], kind, value[at : at + width], owners * j + i)
        leave(moves, buf_d, outs[: len(down)], scal[1 + orders[0][0]])
        for wait in wait_f[-1] + wait_c:
            wait()
        n2 = slice(N2, N2 + D)
        for j in range(HALF_UP // HALF):
            cols = slice(HALF * j, HALF * (j + 1))
            value = dot_cols(fa[:, n2], ca[:, cols]) + dot_cols(fb[:, n2], cb[:, cols])
            put(buf_u, orders[1], j, value.astype(BF16))
        leave(moves, buf_u, outs[len(down) :], scal[1 + orders[1][0]])

    result = call(
        body, "ffn_grads", scal, [*facts, *cots, *outs_g], outputs(*down, *up),
        [FACTS_F] * 2 + [COT_UP] * 2 + [((ROWS, HALF), BF16)] * 2 + [down_buffer, up_buffer],
    )
    return result[: len(down)], result[len(down) :]


def att_grads(scal, facts, cots, count, orders):
    each = 4 // len(orders)
    plans = [group_outputs(each, order, count) for order in orders]
    outs = [out for plan in plans for out in plan[0]]

    def body(moves, scal, *refs):
        ins, outs_ref, rest = refs[:4], refs[4 : 4 + len(outs)], refs[4 + len(outs) :]
        (fa, fb, ca, cb), buffers = rest[:4], rest[4:]
        waits = [moves.load(src, dst) for src, dst in zip(ins, (fa, fb, ca, cb))]
        for wait in waits:
            wait()
        for j in range(4):
            at = slice(0, D) if j < 3 else slice(MIX, MIX + D)
            cols = slice(HALF * j, HALF * (j + 1))
            value = dot_cols(fa[:, at], ca[:, cols]) + dot_cols(fb[:, at], cb[:, cols])
            put(buffers[j // each], orders[j // each], j % each, value.astype(BF16))
        step = len(outs) // len(orders)
        for i, order in enumerate(orders):
            leave(moves, buffers[i], outs_ref[step * i : step * (i + 1)], scal[1 + order[0]])

    result = call(
        body, "att_grads", scal, [*facts, *cots], outputs(*outs),
        [FACTS_A] * 2 + [COT_ATT] * 2 + [plan[1] for plan in plans],
    )
    step = len(outs) // len(orders)
    return [result[i : i + step] for i in range(0, len(outs), step)]


def finish(scal, ffn_kept, ffn_got, att_kept, att_got):
    width = ffn_kept.shape[2]

    def kernel(scal, ffn_kept, ffn_got, att_kept, att_got, qkv, out, up, down):
        mine = scal[0] == 0
        for half in range(2):

            def group(kept, got, i, j):
                a, b = kept[i, j], got[i, j]
                return jnp.where(mine, a, b) if half == 0 else jnp.where(mine, b, a)

            for j in range(4):
                down[0, width * j : width * (j + 1), HALF * half : HALF * (half + 1)] = group(ffn_kept, ffn_got, 0, j)
                at = HALF_UP * half + HALF * j
                up[0, :, at : at + HALF] = group(ffn_kept, ffn_got, 1, j)
                value = group(att_kept, att_got, j // 2, j % 2)
                if j < 3:
                    at = HALF_QKV * half + HALF * j
                    qkv[0, :, at : at + HALF] = value
                else:
                    out[0, :, HALF * half : HALF * (half + 1)] = value

    return pl.pallas_call(
        kernel,
        in_specs=[SMEM] + [VMEM] * 4,
        out_specs=[VMEM] * 4,
        out_shape=[shape((1, *s), F32) for s in ((width, 3 * D), (width, D), (width, FF), (4 * width, D))],
        cost_estimate=SMALL_COST,
        name="finish",
    )(scal, ffn_kept, ffn_got, att_kept, att_got)


TILE = 512


def lookup_kernel(count, last, hid, *rest):
    tables, rest = rest[:count], rest[count:]
    if last:
        m_in, l_in, a_in, mean_ref, unit_ref, lse_ref, m_ref, l_ref, acc = rest
    else:
        m_ref, l_ref, acc = rest
    step = pl.program_id(0)

    @pl.when(step == 0)
    def _():
        if last:
            m_ref[...] = m_in[...]
            l_ref[...] = l_in[...]
            acc[...] = a_in[...]
        else:
            m_ref[...] = jnp.full((ROWS, 1), MASKED, F32)
            l_ref[...] = jnp.zeros((ROWS, 1), F32)
            acc[...] = jnp.zeros((ROWS, D), F32)

    scores = [dot_rows(hid[...], table[...]) * D**-0.5 for table in tables]
    top = m_ref[...]
    for s in scores:
        top = jnp.maximum(top, jnp.max(s, axis=-1, keepdims=True))
    fade = jnp.exp(m_ref[...] - top)
    m_ref[...] = top
    total_l = l_ref[...] * fade
    total_a = acc[...] * fade
    for s, table in zip(scores, tables):
        p = jnp.exp(s - top)
        total_l = total_l + jnp.sum(p, axis=-1, keepdims=True)
        high = p.astype(BF16)
        low = (p - high.astype(F32)).astype(BF16)
        gained = dot(jnp.concatenate([high, low]), table[...])
        total_a = total_a + (gained[:ROWS] + gained[ROWS:])
    l_ref[...] = total_l
    acc[...] = total_a
    if last:
        @pl.when(step == pl.num_programs(0) - 1)
        def _():
            totals = l_ref[...]
            mean_code = acc[...] / totals
            mean_ref[...] = mean_code
            unit_ref[...] = mean_code * lax.rsqrt(
                jnp.mean(mean_code * mean_code, axis=-1, keepdims=True) + EPS
            )
            lse_ref[...] = m_ref[...] + jnp.log(totals)


def fixed(s):
    return pl.BlockSpec(s, lambda i, *_: (0,) * len(s))


def lookup(hidden, tables, state=None):
    last = state is not None
    rows = tables[0].shape[0]
    tile = min(TILE, rows)
    col, mat = (ROWS, 1), (ROWS, D)
    if last:
        outs = [mat, mat, col]
        scratch = [pltpu.VMEM(col, F32), pltpu.VMEM(col, F32), pltpu.VMEM(mat, F32)]
    else:
        outs, scratch = [col, col, mat], []
    return pl.pallas_call(
        partial(lookup_kernel, len(tables), last),
        grid=(rows // tile,),
        in_specs=[fixed(mat)]
        + [pl.BlockSpec((tile, D), lambda i: (i, 0))] * len(tables)
        + ([fixed(col), fixed(col), fixed(mat)] if last else []),
        out_specs=[fixed(o) for o in outs],
        out_shape=[shape(o, F32) for o in outs],
        scratch_shapes=scratch,
        compiler_params=pltpu.CompilerParams(vmem_limit_bytes=ROOM),
        cost_estimate=SMALL_COST,
        name=f"lookup_{int(last)}",
    )(hidden, *tables, *(state if last else ()))


WIDE = 1024


def over_table(moves, tables, buffer, fold):
    count = len(tables)
    tile = buffer.shape[0] // count
    steps = tables[0].shape[0] // tile
    wide = min(WIDE, buffer.shape[0])
    sems = [moves.sem() for _ in tables]

    def step(i):
        copies = []
        for n, (table, sem) in enumerate(zip(tables, sems)):
            src = table if steps == 1 else table.at[pl.ds(pl.multiple_of(i * tile, tile), tile), :]
            copies.append(pltpu.make_async_copy(src, buffer.at[pl.ds(tile * n, tile), :], sem))
            copies[-1].start()
        for j in range(buffer.shape[0] // wide):
            for copy in copies[wide * j // tile : wide * (j + 1) // tile]:
                copy.wait()
            fold(slice(wide * j, wide * (j + 1)))

    if steps == 1:
        step(0)
    else:
        lax.fori_loop(0, steps, lambda i, carry: (step(i), carry)[1], 0)


def table_buffer(tables):
    return ((len(tables) * min(TILE, tables[0].shape[0]), D), BF16)


def lookup_back(scal, hidden, code, lse, inner, tables):
    count = len(tables)

    def body(moves, scal, *refs):
        ins, tables, refs = refs[:4], refs[4 : 4 + count], refs[4 + count :]
        out_o, keep_o, send_o, rows_ref, lse, inner, buffer, out, low = refs
        places = (rows_ref.at[pl.ds(0, ROWS), :], rows_ref.at[pl.ds(ROWS, ROWS), :], lse, inner)
        for wait in [moves.load(src, dst) for src, dst in zip(ins, places)]:
            wait()
        out[...] = jnp.zeros((ROWS, D), F32)

        def fold(rows):
            both = dot_rows(rows_ref[...], buffer[rows, :])
            p = jnp.exp(both[:ROWS] * D**-0.5 - lse[...])
            ds = (p * (both[ROWS:] - inner[...])).astype(BF16)
            out[...] += dot(ds, buffer[rows, :])

        over_table(moves, tables, buffer, fold)
        value = out[...] * D**-0.5
        out[...] = value
        moves.store(out, out_o)
        low[...] = value.astype(BF16)
        moves.store(low.at[:, half_of(scal, HALF)], keep_o)
        moves.store(low.at[:, half_of(scal, HALF, False)], send_o)

    part = ((ROWS, HALF), BF16)
    return call(
        body, "lookup_back", scal, [hidden, code, lse, inner, *tables], outputs(MAT, part, part),
        [((2 * ROWS, D), BF16), COL, COL, table_buffer(tables), MAT, LOW],
    )


def swapped(value):
    return lax.ppermute(value, "section", [(0, 1), (1, 0)])


def bit_count():
    size = lax.axis_size("dp")
    count = size.bit_length() - 1
    assert size == 1 << count
    return count


def across(value, step):
    size = lax.axis_size("dp")
    return lax.ppermute(value, "dp", [(i, i ^ step) for i in range(size)])


def along(value, bit):
    return across(value, 1 << bit)


def after(value, *others):
    return lax.optimization_barrier((value, *others))[0]


def total(terms):
    summed = terms[0].astype(F32)
    for term in terms[1:]:
        summed = summed + term.astype(F32)
    return summed


class Share:
    def __init__(self, parts, order):
        self.order = order
        if len(parts) == 2:
            self.terms, self.ready = [parts[0]], parts[1]
        else:
            count = len(order)
            value = parts[0].reshape((-1,) + (2,) * count + (D >> count, HALF))
            axes = [count - bit for bit in order]
            self.terms, self.ready = [value.transpose(axes + [0, count + 1, count + 2])], None

    def split(self, stage):
        if stage == 0 and self.ready is not None:
            return self.ready
        mine = (lax.axis_index("dp") >> self.order[stage]) & 1

        def pick(which):
            return [lax.dynamic_index_in_dim(t, which, 0, keepdims=False) for t in self.terms]

        sent = total(pick(1 - mine)).astype(BF16)
        self.terms = pick(mine)
        return sent

    def send(self, stage, *values):
        self.sent = after(self.split(stage), *values)
        self.got = along(self.sent, self.order[stage])

    def receive(self, *values):
        self.terms.append(after(self.got, *values))


class Group:
    def __init__(self, parts, orders, joint):
        self.shares = [Share(part, order) for part, order in zip(parts, orders)]
        self.joint = joint

    def ready(self):
        return [share.terms[0] for share in self.shares]

    def send(self, stage, *values):
        if stage < self.joint:
            for share in self.shares:
                share.send(stage, *values)
            self.sent = [share.sent for share in self.shares]
        else:
            self.sent = [after(jnp.stack([share.split(stage) for share in self.shares]), *values)]
            self.got = along(self.sent[0], self.shares[0].order[stage])

    def receive(self, stage, *values):
        if stage < self.joint:
            for share in self.shares:
                share.receive(*values)
        else:
            got = after(self.got, *values)
            for i, share in enumerate(self.shares):
                share.terms.append(got[i])

    def result(self):
        sums = jnp.concatenate([total(share.terms) for share in self.shares])
        return sums.reshape((2, -1) + sums.shape[-2:])


def pair_orders():
    far = list(range(2, bit_count()))
    return [0, 1] + far, [1, 0] + far


def pair(parts):
    return Group(parts, pair_orders(), 2)


def far_order():
    return [list(range(2, bit_count())) + [0, 1]]


def per_device(
    patches,
    recon_cot,
    lengths,
    codebook,
    w_qkv,
    w_out,
    w_up,
    w_down,
    norm_gain,
    norm_bias,
    bias_out,
    bias_up,
):
    section = lax.axis_index("section")
    on_first = section == 0
    size = lax.axis_size("dp")
    count = bit_count()
    me = lax.axis_index("dp")
    scal = jnp.stack([section, *((me >> bit) & 1 for bit in range(count))]).astype(jnp.int32)
    own_small = pack_small(norm_gain, norm_bias, bias_out, bias_up)
    small = (lengths, own_small, swapped(own_small))
    weights = [(w[0], swapped(w[0])) for w in (w_qkv, w_out)]

    table = codebook
    for bit in range(count - 1, 2, -1):
        got = after(along(table, bit), small[2], weights[0][1], weights[1][1])
        table = jnp.concatenate([table, got])
    weights += [(w[0], swapped(after(w[0], table))) for w in (w_up, w_down)]
    got = along(table, 2)
    from_table = along(table, 1)
    facts_ea, qkv_e, probs_e = att_forward(0, after(scal, table), patches, small, weights)
    got = after(got, facts_ea)
    from_got = along(got, 0)
    left = jnp.concatenate([table, after(from_table, got)])
    late = [along(left, 0)]
    right = jnp.concatenate([got, after(from_got, left)])
    late.append(along(right, 1))
    pieces = [left, right]
    pieces_other = [swapped(piece) for piece in pieces]
    hidden, facts_ef, resid_e, slope_e = ffn_forward(
        0, after(scal, *pieces), patches, small, facts_ea, weights
    )
    state = lookup(hidden, pieces + pieces_other)
    late = after(late, state[0])
    late_other = [swapped(piece) for piece in late]
    tables = pieces + pieces_other + late + late_other
    mean_code, unit, lse = lookup(hidden, late + late_other, state)
    facts_ea = (facts_ea, swapped(after(facts_ea, *late_other)))
    facts_ef = (facts_ef, swapped(after(facts_ef, *late_other)))
    recon, facts_df, facts_da, qkv_d, probs_d, resid_d, slope_d = block_forward(
        1, after(scal, facts_ea[1], facts_ef[1]), unit, small, weights
    )
    facts_df = (facts_df, swapped(facts_df))
    facts_da = (facts_da, swapped(facts_da))
    recon_first = lax.ppermute(recon, "section", [(0, 1)])
    lse_other = swapped(lse)

    keep, send, d_resid, sums_df = ffn_backward(
        1, scal, recon_cot, slope_d, resid_d, small, weights, True
    )
    first_f = pair(ffn_grads(after(scal, keep), facts_df, (keep, swapped(send)), [recon_cot], count, pair_orders(), True))
    first_f.send(0)
    keep, send, sums_da, code, inner = att_backward(
        1, after(scal, facts_da[1], *first_f.sent), d_resid, qkv_d, probs_d, unit, small, weights, mean_code
    )
    got = swapped(send)
    d_hidden, g_keep, g_send = lookup_back(scal, hidden, code, lse, inner, tables)
    g_got = swapped(g_send)
    first_f.receive(0, d_hidden, recon_first, lse_other)
    first_f.send(1)
    first_a = pair(att_grads(after(scal, *first_f.sent), facts_da, (keep, got), count, pair_orders()))
    first_a.send(0)
    keep, send, d_resid, sums_ef = ffn_backward(
        0, after(scal, g_got, *first_a.sent), d_hidden, slope_e, resid_e, small, weights, False
    )
    got = swapped(send)
    first_f.receive(1, keep)
    first_f.send(2)
    second_f = pair(
        ffn_grads(after(scal, keep, *first_f.sent), facts_ef, (keep, got), (g_keep, g_got), count, pair_orders(), False)
    )
    second_f.send(0)
    first_a.receive(0, *second_f.ready())
    first_a.send(1)
    keep, send, sums, sums_send, grad_x = att_backward(
        0, after(scal, *second_f.sent, *first_a.sent), d_resid, qkv_e, probs_e, patches, small, weights,
        sums_before=(sums_ef, sums_df, sums_da),
    )
    got = swapped(send)
    sums_got = swapped(sums_send)
    first_f.receive(2, sums)
    first_f.send(3)
    second_a = pair(att_grads(after(scal, sums_got, *first_f.sent), facts_ea, (keep, got), count, pair_orders()))
    second_f.receive(0, *second_a.ready())
    second_f.send(1)
    first_a.receive(1, *second_f.sent)
    closed = [share.terms[-1] for share in first_a.shares]
    if count == 4:
        first_f.receive(3, *closed)
        closed = [first_f.shares[0].terms[-1]]
    second_a.send(0, *closed)
    first_a.send(2, *second_a.sent)
    second_f.receive(1, *first_a.sent)
    second_f.send(2)
    sums = sums + after(sums_got, *second_f.sent)
    sums_got = along(sums, 2)
    first_a.receive(2, sums)
    first_a.send(3)
    grad_second = lax.ppermute(after(grad_x, sums), "section", [(1, 0)])
    second_a.receive(0, *first_a.sent)
    second_a.send(1)
    first_a.receive(3, grad_second, *second_a.sent)
    second_f.receive(2, first_a.shares[0].terms[-1])
    second_f.send(3)
    sums = sums + after(sums_got, *second_f.sent)
    sums_got = along(sums, 0)
    second_a.receive(1, sums)
    second_a.send(2)
    sums = sums + after(sums_got, *second_a.sent)
    sums_got = along(sums, 1)
    last = second_a.sent
    if count > 4:
        first_a.send(4)
        waiting = [[first_f, 3], [first_a, 4], [second_f, 3]]
        for step in range(count):
            for entry in waiting:
                group, stage = entry
                if stage < count - (1 if group is second_f else 0):
                    group.receive(stage, *last)
                    if stage + 1 < count:
                        group.send(stage + 1)
                        last = group.sent
                    entry[1] += 1
    ends = jnp.where(
        on_first, jnp.concatenate([grad_x, grad_second]), jnp.concatenate([recon_first, recon])
    )[None]
    lse, lse_other = after([lse, lse_other], *last)
    lse, lse_other = lse[:, 0], lse_other[:, 0]
    codes = jnp.where(on_first, jnp.concatenate([lse, lse_other]), jnp.concatenate([lse_other, lse]))
    sums = sums + after(sums_got, *last)
    sums_got = along(sums, 3)
    for bit in range(4, count):
        sums = sums + sums_got
        sums_got = along(sums, bit)
    for stage in range(2, count - 1):
        second_a.receive(stage, sums, codes)
        second_a.send(stage + 1)
    sums = sums + after(sums_got, *second_a.sent)
    width = D // size
    rows = lax.dynamic_slice_in_dim(sums, me * width, width, axis=1)
    grad_gain = jnp.stack([rows[8], rows[0]])[None]
    grad_nbias = jnp.stack([rows[9], rows[1]])[None]
    grad_bout = jnp.stack([rows[3], rows[2]])[None]
    grad_bup = lax.dynamic_slice_in_dim(sums[4:8].reshape(FF), me * width * 4, width * 4)[None]
    second_f.receive(count - 1, grad_gain, grad_nbias, grad_bout, grad_bup, ends)

    def shared_out(encoder, decoder):
        encoder, decoder = encoder.result(), decoder.result()
        return jnp.where(on_first, encoder, decoder), swapped(jnp.where(on_first, decoder, encoder))

    ffn = shared_out(second_f, first_f)
    second_a.receive(count - 1, ffn[0])
    att = shared_out(second_a, first_a)
    grad_qkv, grad_out, grad_up, grad_down = finish(scal, *ffn, *att)
    return (ends, codes, grad_qkv, grad_out, grad_up, grad_down, grad_gain, grad_nbias, grad_bout, grad_bup)


def solution(mesh):
    placed = (
        P("dp", None),
        P("dp", None),
        P("dp", None),
        P(("dp", "section"), None),
        P("section", None, None),
        P("section", None, None),
        P("section", None, None),
        P("section", None, None),
        P("section", None, None),
        P("section", None, None),
        P("section", None, None),
        P("section", None),
    )
    return jax.shard_map(
        per_device,
        mesh=mesh,
        in_specs=placed,
        out_specs=(
            P("section", "dp", None),
            P("dp"),
            P("section", "dp", None),
            P("section", "dp", None),
            P("section", "dp", None),
            P("section", "dp", None),
            P("section", None, "dp"),
            P("section", None, "dp"),
            P("section", None, "dp"),
            P("section", "dp"),
        ),
        check_vma=False,
    )
```

```python
from functools import partial

import jax
import jax.numpy as jnp
from jax import lax
from jax.experimental import pallas as pl
from jax.experimental.layout import Layout, with_layout_constraint
from jax.experimental.pallas import tpu as pltpu
from jax.sharding import PartitionSpec as P

D = 768
HEADS = 12
HD = 64
FF = 3072
ROWS = 256
PAIR = 2 * HD
EPS = 1e-06
MASKED = -1e30
F32 = jnp.float32
BF16 = jnp.bfloat16
N2, FFN_FACTS = FF, FF + D
MIX, ATT_FACTS = D, 2 * D
HALF = D // 2
HALF_UP = FF // 2
HALF_QKV = 3 * D // 2
TAIL_P = 0.35
TAIL = (0.19620077326315646, 0.2185939781557991, 0.05480664657447366, 0.5651487076988272,
        -0.5574354264567037, 0.7060774515721405, -0.18339209581143395)
VMEM = pl.BlockSpec(memory_space=pltpu.VMEM)
SMEM = pl.BlockSpec(memory_space=pltpu.SMEM)
ANY = pl.BlockSpec(memory_space=pl.ANY)
ROOM = 63 * 1024 * 1024


def dot(a, b):
    return jnp.dot(a, b, preferred_element_type=F32)


def dot_rows(a, b):
    return lax.dot_general(a, b, (((1,), (1,)), ((), ())), preferred_element_type=F32)


def dot_cols(a, b):
    return lax.dot_general(a, b, (((0,), (0,)), ((), ())), preferred_element_type=F32)


def unit_rows(values):
    centre = values - jnp.mean(values, axis=-1, keepdims=True)
    inverse = lax.rsqrt(jnp.mean(centre * centre, axis=-1, keepdims=True) + EPS)
    return centre * inverse, inverse


def norm_back(scaled, unit, inverse):
    return inverse * (
        scaled
        - jnp.mean(scaled, axis=-1, keepdims=True)
        - unit * jnp.mean(scaled * unit, axis=-1, keepdims=True)
    )


def gelu_parts(z):
    bell = jnp.exp(-0.5 * z * z)
    t = 1.0 / (1.0 + (TAIL_P * 0.5**0.5) * jnp.abs(z))
    poly = TAIL[6] * t + TAIL[5]
    for c in TAIL[4::-1]:
        poly = poly * t + c
    tail = 0.5 * poly * t * bell
    cdf = jnp.where(z >= 0, 1.0 - tail, tail)
    return z * cdf, cdf + z * bell * 0.3989422804014327


def image_ids(scal, lens, shape, axis):
    position = lax.broadcasted_iota(jnp.int32, shape, axis)
    limit = jnp.int32(0)
    ids = jnp.zeros(shape, jnp.int32)
    for i in range(4):
        limit = limit + lens[scal[0], i]
        ids = ids + (position >= limit).astype(jnp.int32)
    return ids


def shape(s, t):
    return jax.ShapeDtypeStruct(s, t)


class Moves:
    def __init__(self, sems):
        self.sems = sems
        self.used = 0
        self.leaving = []

    def sem(self):
        self.used += 1
        return self.sems.at[self.used - 1]

    def load(self, src, dst):
        copy = pltpu.make_async_copy(src, dst, self.sem())
        copy.start()
        return copy.wait

    def load_either(self, first, src, other, dst):
        sem = self.sem()
        for take, ref in ((first, src), (jnp.logical_not(first), other)):
            @pl.when(take)
            def _():
                pltpu.make_async_copy(ref, dst, sem).start()

        return pltpu.make_async_copy(src, dst, sem).wait

    def load_tiles(self, first, src, other, dst, axis):
        tiles = []
        for j in range(dst.shape[axis] // D):
            at = (pl.ds(D * j, D),) if axis == 0 else (slice(None), pl.ds(D * j, D))
            tiles.append((at, self.sem()))
        for take, ref in ((first, src), (jnp.logical_not(first), other)):
            @pl.when(take)
            def _():
                for at, sem in tiles:
                    pltpu.make_async_copy(ref.at[at], dst.at[at], sem).start()

        return [pltpu.make_async_copy(src.at[at], dst.at[at], sem).wait for at, sem in tiles]

    def store(self, src, dst):
        copy = pltpu.make_async_copy(src, dst, self.sem())
        copy.start()
        self.leaving.append(copy.wait)

    def finish(self):
        for wait in self.leaving:
            wait()


SEMS = 32
SMALL_COST = pl.CostEstimate(flops=1000, bytes_accessed=1000, transcendentals=0)


def call(body, name, scal, inputs, outs, scratch, small=None):
    extra = () if small is None else small[1:]

    def kernel(*refs):
        scal, *refs = refs
        moves = Moves(refs[-1])
        if small is None:
            body(moves, scal, *refs[:-1])
        else:
            lens, own, other, *refs = refs
            chosen = refs[-2]
            chosen[...] = jnp.where(scal[0] == small[0], own[...], other[...])
            body(moves, scal, lens, chosen, *refs[:-2])
        moves.finish()

    return pl.pallas_call(
        kernel,
        in_specs=[SMEM] + [SMEM, VMEM, VMEM][: len(extra)] + [ANY] * len(inputs),
        out_specs=[ANY] * len(outs),
        out_shape=outs,
        scratch_shapes=[
            *(pltpu.VMEM(s, t) for s, t in (*scratch, *([SMALL] if extra else []))),
            pltpu.SemaphoreType.DMA((SEMS,)),
        ],
        compiler_params=pltpu.CompilerParams(vmem_limit_bytes=ROOM),
        cost_estimate=SMALL_COST,
        name=name,
    )(scal, *extra, *inputs)


SMALL = ((10, D), F32)
W_QKV = ((D, 3 * D), BF16)
W_OUT = ((D, D), BF16)
W_UP = ((D, FF), BF16)
W_DOWN = ((FF, D), BF16)
MAT = ((ROWS, D), F32)
LOW = ((ROWS, D), BF16)
COL = ((ROWS, 1), F32)


def rows_of(scal, own=True):
    which = scal[0] if own else 1 - scal[0]
    return pl.ds(pl.multiple_of(which * ROWS, ROWS), ROWS)


def half_of(scal, width, own=True):
    which = scal[0] if own else 1 - scal[0]
    return pl.ds(pl.multiple_of(which * width, 128), width)


def pack_small(gains, shifts, bias_out, bias_up):
    def kernel(gains, shifts, bias_out, bias_up, out):
        for i, ref in enumerate((gains, shifts, bias_out)):
            out[2 * i : 2 * i + 2, :] = ref[0]
        for j in range(FF // D):
            out[6 + j : 7 + j, :] = bias_up[:, D * j : D * (j + 1)]

    return pl.pallas_call(
        kernel, in_specs=[VMEM] * 4, out_specs=VMEM, out_shape=shape(*SMALL), cost_estimate=SMALL_COST, name="pack_small",
    )(gains, shifts, bias_out, bias_up)


def by_head(pair, first):
    zero = jnp.zeros_like(pair)
    return jnp.concatenate([jnp.where(first, pair, zero), jnp.where(first, zero, pair)])


def att_forward_part(moves, scal, lens, x, small, wq, wait, facts, qkv, probs, out):
    facts_hbm, qkv_hbm, probs_hbm = out
    unit, _ = unit_rows(x)
    n1 = (unit * small[0:1, :] + small[2:3, :]).astype(BF16)
    facts[:, :D] = n1
    same = image_ids(scal, lens, (ROWS, ROWS), 0) == image_ids(scal, lens, (ROWS, ROWS), 1)
    bias = jnp.where(same, 0.0, MASKED)
    first = lax.broadcasted_iota(jnp.int32, (1, PAIR), 1) < HD
    for j in range(3):
        wait[j]()
        qkv[:, D * j : D * (j + 1)] = dot(n1, wq[:, D * j : D * (j + 1)]).astype(BF16)
    moves.store(qkv, qkv_hbm)
    both = jnp.concatenate([bias, bias])
    for p in range(HEADS // 2):
        q = by_head(qkv[:, PAIR * p : PAIR * (p + 1)] * jnp.asarray(HD**-0.5, BF16), first)
        k = qkv[:, D + PAIR * p : D + PAIR * (p + 1)]
        v = qkv[:, 2 * D + PAIR * p : 2 * D + PAIR * (p + 1)]
        s = dot_rows(q, k) + both
        s = jnp.exp(s - jnp.max(s, axis=-1, keepdims=True))
        pr = (s * (1.0 / jnp.sum(s, axis=-1, keepdims=True))).astype(BF16)
        probs[2 * p : 2 * p + 2] = pr.reshape(2, ROWS, ROWS)
        out = dot(pr, v)
        facts[:, MIX + PAIR * p : MIX + PAIR * (p + 1)] = jnp.where(first, out[:ROWS], out[ROWS:]).astype(BF16)
    moves.store(probs, probs_hbm)
    moves.store(facts, facts_hbm)


def ffn_forward_part(moves, x, small, mixed, wo, wu, wd, waits, facts, resid_ref, slope, y_ref, out):
    y_hbm, facts_hbm, resid_hbm, slope_hbm = out
    waits[0]()
    resid = x + dot(mixed, wo[...]) + small[4:5, :]
    resid_ref[...] = resid
    moves.store(resid_ref, resid_hbm)
    unit, _ = unit_rows(resid)
    n2 = (unit * small[1:2, :] + small[3:4, :]).astype(BF16)
    facts[:, N2 : N2 + D] = n2
    y = resid + small[5:6, :]
    tiles = FF // D

    def pre_tile(j):
        waits[1][j]()
        return dot(n2, wu[:, D * j : D * (j + 1)]) + small[6 + j : 7 + j, :]

    pre = pre_tile(0)
    for j in range(tiles):
        cols = slice(D * j, D * (j + 1))
        waits[2][j]()
        later = pre_tile(j + 1) if j + 1 < tiles else None
        act, sl = gelu_parts(pre)
        act = act.astype(BF16)
        facts[:, cols] = act
        slope[:, cols] = sl.astype(BF16)
        y = y + dot(act, wd[cols, :])
        pre = later
    moves.store(facts, facts_hbm)
    moves.store(slope, slope_hbm)
    y_ref[...] = y.astype(y_ref.dtype)
    moves.store(y_ref, y_hbm)


FACTS_A = ((ROWS, ATT_FACTS), BF16)
FACTS_F = ((ROWS, FFN_FACTS), BF16)
QKV = ((ROWS, 3 * D), BF16)
PROBS = ((HEADS, ROWS, ROWS), BF16)
SLOPE = ((ROWS, FF), BF16)


def outputs(*kinds):
    return [shape(*kind) for kind in kinds]


def block_forward(block, scal, x, small, weights):
    def body(moves, scal, lens, small, x_in, wq_a, wq_b, wo_a, wo_b, wu_a, wu_b, wd_a, wd_b,
             y_o, facts_fo, facts_ao, qkv_o, probs_o, resid_o, slope_o,
             x, wq, wo, wu, wd, y, facts_f, facts_a, qkv, probs, resid, slope):
        own = scal[0] == block
        wait_x = moves.load(x_in, x)
        wait_q = moves.load_tiles(own, wq_a, wq_b, wq, 1)
        waits = [moves.load_either(own, a, b, w) for a, b, w in ((wo_a, wo_b, wo), (wu_a, wu_b, wu), (wd_a, wd_b, wd))]
        waits = [waits[0]] + [[wait] + [lambda: None] * 3 for wait in waits[1:]]
        wait_x()
        xs = x[...]
        att_forward_part(moves, scal, lens, xs, small, wq, wait_q, facts_a, qkv, probs, (facts_ao, qkv_o, probs_o))
        ffn_forward_part(
            moves, xs, small, facts_a[:, MIX : MIX + D], wo, wu, wd, waits, facts_f, resid, slope, y,
            (y_o, facts_fo, resid_o, slope_o),
        )

    kinds = (MAT, FACTS_F, FACTS_A, QKV, PROBS, MAT, SLOPE)
    return call(
        body, f"forward_{block}", scal, [x, *sum(weights, ())], outputs(*kinds),
        [MAT, W_QKV, W_OUT, W_UP, W_DOWN, *kinds], (block, *small),
    )


def att_forward(block, scal, patches, small, weights):
    def body(moves, scal, lens, small, x_in, wq_a, wq_b, facts_o, qkv_o, probs_o, x, wq, facts, qkv, probs):
        wait_x = moves.load(x_in.at[rows_of(scal), :], x)
        wait_w = moves.load_tiles(scal[0] == block, wq_a, wq_b, wq, 1)
        wait_x()
        att_forward_part(
            moves, scal, lens, x[...].astype(F32), small, wq, wait_w, facts, qkv, probs, (facts_o, qkv_o, probs_o)
        )

    kinds = (FACTS_A, QKV, PROBS)
    return call(
        body, f"att_forward_{block}", scal, [patches, *weights[0]], outputs(*kinds),
        [LOW, W_QKV, *kinds], (block, *small),
    )


def ffn_forward(block, scal, patches, small, facts_a, weights):
    def body(moves, scal, lens, small, x_in, facts_ai, wo_a, wo_b, wu_a, wu_b, wd_a, wd_b,
             y_o, facts_o, resid_o, slope_o, x, mixed, wo, wu, wd, y, facts, resid, slope):
        own = scal[0] == block
        wait_x = moves.load(x_in.at[rows_of(scal), :], x)
        wait_m = moves.load(facts_ai.at[:, pl.ds(MIX, D)], mixed)
        waits = [
            moves.load_either(own, wo_a, wo_b, wo),
            moves.load_tiles(own, wu_a, wu_b, wu, 1),
            moves.load_tiles(own, wd_a, wd_b, wd, 0),
        ]
        wait_x()
        wait_m()
        ffn_forward_part(
            moves, x[...].astype(F32), small, mixed[...], wo, wu, wd, waits, facts, resid, slope, y,
            (y_o, facts_o, resid_o, slope_o),
        )

    kinds = (LOW, FACTS_F, MAT, SLOPE)
    return call(
        body, f"ffn_forward_{block}", scal, [patches, facts_a, *sum(weights[1:], ())], outputs(*kinds),
        [LOW, LOW, W_OUT, W_UP, W_DOWN, *kinds], (block, *small),
    )


COT_UP = ((ROWS, HALF_UP), BF16)
COT_ATT = ((ROWS, HALF_QKV + HALF), BF16)
SUMS = ((8, D), F32)


def ffn_backward(block, scal, g, slope, resid, small, weights, own_rows):
    def body(moves, scal, lens, small, g_in, slope_in, resid_in, wu_a, wu_b, wd_a, wd_b,
             keep_o, send_o, dres_o, sums, g_ref, slope, resid, wu, wd, d_pre_ref, dres):
        own = scal[0] == block
        wait_g = moves.load(g_in.at[rows_of(scal), :] if own_rows else g_in, g_ref)
        wait_d = moves.load_tiles(own, wd_a, wd_b, wd, 0)
        wait_s = moves.load(slope_in, slope)
        wait_u = moves.load_tiles(own, wu_a, wu_b, wu, 1)
        wait_r = moves.load(resid_in, resid)
        wait_g()
        g = g_ref[...].astype(F32)
        gl = g.astype(BF16)
        small_sums = [None] * 4
        small_sums[2] = jnp.sum(g, axis=0, keepdims=True)
        d_n2 = jnp.zeros((ROWS, D), F32)
        up_sums = []
        tiles = FF // D

        def act_tile(j):
            wait_d[j]()
            return dot_rows(gl, wd[D * j : D * (j + 1), :])

        later = act_tile(0)
        wait_s()
        for j in range(tiles):
            cols = slice(D * j, D * (j + 1))
            wait_u[j]()
            d_act = later
            later = act_tile(j + 1) if j + 1 < tiles else None
            d_pre = (d_act * slope[:, cols].astype(F32)).astype(BF16)
            d_pre_ref[:, cols] = d_pre
            up_sums.append(jnp.sum(d_pre.astype(F32), axis=0, keepdims=True))
            d_n2 = d_n2 + dot_rows(d_pre, wu[:, cols])
        moves.store(d_pre_ref.at[:, half_of(scal, HALF_UP)], keep_o)
        moves.store(d_pre_ref.at[:, half_of(scal, HALF_UP, False)], send_o)
        wait_r()
        unit, inverse = unit_rows(resid[...])
        small_sums[0] = jnp.sum(d_n2 * unit, axis=0, keepdims=True)
        small_sums[1] = jnp.sum(d_n2, axis=0, keepdims=True)
        d_resid = g + norm_back(d_n2 * small[1:2, :], unit, inverse)
        dres[...] = d_resid
        moves.store(dres, dres_o)
        small_sums[3] = jnp.sum(d_resid, axis=0, keepdims=True)
        for i, value in enumerate(small_sums + up_sums):
            sums[i : i + 1, :] = value

    def with_sums(moves, *refs):
        *head, sums_buffer = refs
        sums_o = head[13]
        head[13] = sums_buffer
        body(moves, *head)
        moves.store(sums_buffer, sums_o)

    g_kind = (tuple(g.shape), g.dtype) if not own_rows else ((ROWS, D), g.dtype)
    return call(
        with_sums, f"ffn_backward_{block}", scal, [g, slope, resid, *weights[2], *weights[3]],
        outputs(COT_UP, COT_UP, MAT, SUMS),
        [g_kind, SLOPE, MAT, W_UP, W_DOWN, SLOPE, MAT, SUMS], (block, *small),
    )


def att_backward(block, scal, d_resid, qkv, probs, x, small, weights, mean_code=None, sums_before=None):
    final = mean_code is None

    def body(moves, scal, lens, small, dres_in, qkv_in, probs_in, x_in, wq_a, wq_b, wo_a, wo_b, *rest):
        if final:
            (ef_in, df_in, da_in, keep_o, send_o, own_o, other_o, gx_o,
             dres, qkv, probs, x_ref, wq, wo, d_qkv, rl_ref, sums, ef, df, da, packed, gx) = rest
            wait_sums = [moves.load(src, dst) for src, dst in ((ef_in, ef), (df_in, df), (da_in, da))]
        else:
            (mean_in, keep_o, send_o, sums_o, code_o, inner_o,
             dres, qkv, probs, x_ref, wq, wo, d_qkv, rl_ref, sums, mean_ref, code_ref, inner_ref) = rest
        own = scal[0] == block
        wait_g = moves.load(dres_in, dres)
        wait_o = moves.load_either(own, wo_a, wo_b, wo)
        wait_k = moves.load(qkv_in, qkv)
        wait_p = moves.load(probs_in, probs)
        wait_q = moves.load_either(own, wq_a, wq_b, wq)
        wait_x = moves.load(x_in.at[rows_of(scal), :] if final else x_in, x_ref)
        if not final:
            wait_m = moves.load(mean_in, mean_ref)
        wait_g()
        d_resid = dres[...]
        rl = d_resid.astype(BF16)
        rl_ref[...] = rl
        for out, mine in ((keep_o, True), (send_o, False)):
            moves.store(rl_ref.at[:, half_of(scal, HALF, mine)], out.at[:, pl.ds(HALF_QKV, HALF)])
        first = lax.broadcasted_iota(jnp.int32, (1, PAIR), 1) < HD
        wait_o()
        d_mixed = dot_rows(rl, wo[...]).astype(BF16)
        wait_k()
        wait_p()
        scale = jnp.asarray(HD**-0.5, BF16)
        for p in range(HEADS // 2):
            q = qkv[:, PAIR * p : PAIR * (p + 1)] * scale
            k = qkv[:, D + PAIR * p : D + PAIR * (p + 1)]
            v = qkv[:, 2 * D + PAIR * p : 2 * D + PAIR * (p + 1)]
            dm = d_mixed[:, PAIR * p : PAIR * (p + 1)]
            dm = by_head(dm, first)
            pr = probs[2 * p : 2 * p + 2].reshape(2 * ROWS, ROWS)
            dp = dot_rows(dm, v)
            prf = pr.astype(F32)
            ds = (prf * (dp - jnp.sum(dp * prf, axis=-1, keepdims=True))).astype(BF16)
            dq = dot(ds, k)
            dq = jnp.where(first, dq[:ROWS], dq[ROWS:]) * HD**-0.5
            for at, value in ((0, dq), (D, dot_cols(ds, by_head(q, first))), (2 * D, dot_cols(pr, dm))):
                d_qkv[:, at + PAIR * p : at + PAIR * (p + 1)] = value.astype(BF16)
        for out, mine in ((keep_o, True), (send_o, False)):
            moves.store(d_qkv.at[:, half_of(scal, HALF_QKV, mine)], out.at[:, pl.ds(0, HALF_QKV)])
        wait_q()
        d_n1 = dot_rows(d_qkv[...], wq[...])
        wait_x()
        x = x_ref[...].astype(F32)
        unit, inverse = unit_rows(x)
        sums[0:1, :] = jnp.sum(d_n1 * unit, axis=0, keepdims=True)
        sums[1:2, :] = jnp.sum(d_n1, axis=0, keepdims=True)
        if final:
            for wait in wait_sums:
                wait()
            for i, (ffn, att) in enumerate(((ef, sums), (df, da))):
                packed[i, 0:8, :] = ffn[...]
                packed[i, 8:10, :] = att[0:2, :]
            moves.store(packed.at[scal[0]], own_o)
            moves.store(packed.at[1 - scal[0]], other_o)
        else:
            sums[2:8, :] = jnp.zeros((6, D), F32)
            moves.store(sums, sums_o)
        grad_x = d_resid + norm_back(d_n1 * small[0:1, :], unit, inverse)
        if final:
            gx[...] = grad_x
            moves.store(gx, gx_o)
        else:
            wait_m()
            mean_code = mean_ref[...]
            inv = lax.rsqrt(jnp.mean(mean_code * mean_code, axis=-1, keepdims=True) + EPS)
            code = inv * (grad_x - x * jnp.mean(grad_x * x, axis=-1, keepdims=True))
            code = code.astype(BF16)
            code_ref[...] = code
            moves.store(code_ref, code_o)
            inner_ref[...] = jnp.sum(code.astype(F32) * mean_code, axis=-1, keepdims=True)
            moves.store(inner_ref, inner_o)

    if final:
        more_in, more, sums_out = [*sums_before], [MAT], [SMALL, SMALL]
        more_scratch = [SUMS, SUMS, SUMS, ((2, 10, D), F32)]
    else:
        more_in, more, sums_out = [mean_code], [LOW, COL], [SUMS]
        more_scratch = [MAT]
    return call(
        body, f"att_backward_{block}", scal, [d_resid, qkv, probs, x, *weights[0], *weights[1], *more_in],
        outputs(COT_ATT, COT_ATT, *sums_out, *more),
        [MAT, QKV, PROBS, LOW if final else MAT, W_QKV, W_OUT, QKV, LOW, SUMS, *more_scratch, *more],
        (block, *small),
    )


def group_outputs(kinds, order, count):
    width = D >> count
    if width % 16:
        return [((kinds, D, HALF), BF16)], ((kinds, D, HALF), BF16)
    tail = (kinds, width, HALF)
    return [((2,) * (count - 1) + tail, BF16)] * 2, ((2,) * count + tail, BF16)


def put(buffer, order, kind, value, owner=0):
    if len(buffer.shape) == 3:
        width = D >> len(order)
        buffer[kind, width * owner : width * owner + value.shape[0], :] = value
        return
    width = buffer.shape[-2]
    for i in range(value.shape[0] // width):
        place = tuple((owner + i) >> bit & 1 for bit in order)
        buffer[place + (kind,)] = value[width * i : width * (i + 1)]


def leave(moves, buffer, outs, mine):
    if len(outs) == 1:
        moves.store(buffer, outs[0])
    else:
        moves.store(buffer.at[mine], outs[0])
        moves.store(buffer.at[1 - mine], outs[1])


def twice(kind):
    return ((2 * kind[0][0], kind[0][1]), kind[1])


def ffn_grads(scal, facts, cots, outs_g, count, orders, both):
    down, down_buffer = group_outputs(FF // D, orders[0], count)
    up, up_buffer = group_outputs(HALF_UP // HALF, orders[1], count)
    width = D >> count
    given = 4 + len(outs_g)

    def body(moves, scal, *refs):
        ins, outs, (f, c, g, buf_d, buf_u) = refs[:given], refs[given:-5], refs[-5:]
        own, other = (pl.ds(0, ROWS), pl.ds(ROWS, ROWS))
        if both:
            wait_g = [
                moves.load(ins[4].at[rows_of(scal, mine), half_of(scal, HALF)], g.at[rows, :])
                for rows, mine in ((own, True), (other, False))
            ]
        else:
            wait_g = [moves.load(ref, g.at[rows, :]) for ref, rows in zip(ins[4:], (own, other))]
        wait_f = []
        for j in range(FFN_FACTS // D):
            cols = pl.ds(D * j, D)
            wait_f.append([moves.load(src.at[:, cols], f.at[rows, cols]) for src, rows in zip(ins, (own, other))])
        wait_c = [moves.load(ref, c.at[rows, :]) for ref, rows in zip(ins[2:4], (own, other))]
        for wait in wait_g:
            wait()
        for j in range(FF // D):
            cols = slice(D * j, D * (j + 1))
            for wait in wait_f[j]:
                wait()
            value = dot_cols(f[:, cols], g[...])
            value = value.astype(BF16)
            owners = D // (4 * width)
            for i in range(owners):
                for kind in range(4):
                    at = width * (4 * i + kind)
                    put(buf_d, orders[0], kind, value[at : at + width], owners * j + i)
        leave(moves, buf_d, outs[: len(down)], scal[1 + orders[0][0]])
        for wait in wait_f[-1] + wait_c:
            wait()
        n2 = slice(N2, N2 + D)
        for j in range(HALF_UP // HALF):
            cols = slice(HALF * j, HALF * (j + 1))
            value = dot_cols(f[:, n2], c[:, cols])
            put(buf_u, orders[1], j, value.astype(BF16))
        leave(moves, buf_u, outs[len(down) :], scal[1 + orders[1][0]])

    result = call(
        body, "ffn_grads", scal, [*facts, *cots, *outs_g], outputs(*down, *up),
        [twice(FACTS_F), twice(COT_UP), ((2 * ROWS, HALF), BF16), down_buffer, up_buffer],
    )
    return result[: len(down)], result[len(down) :]


def att_grads(scal, facts, cots, count, orders):
    each = 4 // len(orders)
    plans = [group_outputs(each, order, count) for order in orders]
    outs = [out for plan in plans for out in plan[0]]

    def body(moves, scal, *refs):
        ins, outs_ref, rest = refs[:4], refs[4 : 4 + len(outs)], refs[4 + len(outs) :]
        (f, c), buffers = rest[:2], rest[2:]
        waits = [
            moves.load(src, dst.at[pl.ds(ROWS * i, ROWS), :]) for dst, pairs in ((f, ins[:2]), (c, ins[2:]))
            for i, src in enumerate(pairs)
        ]
        for wait in waits:
            wait()
        for j in range(4):
            at = slice(0, D) if j < 3 else slice(MIX, MIX + D)
            cols = slice(HALF * j, HALF * (j + 1))
            value = dot_cols(f[:, at], c[:, cols])
            put(buffers[j // each], orders[j // each], j % each, value.astype(BF16))
        step = len(outs) // len(orders)
        for i, order in enumerate(orders):
            leave(moves, buffers[i], outs_ref[step * i : step * (i + 1)], scal[1 + order[0]])

    result = call(
        body, "att_grads", scal, [*facts, *cots], outputs(*outs),
        [twice(FACTS_A), twice(COT_ATT)] + [plan[1] for plan in plans],
    )
    step = len(outs) // len(orders)
    return [result[i : i + step] for i in range(0, len(outs), step)]


def finish(scal, kept, got, ffn):
    width = kept.shape[2]

    def kernel(scal, kept, got, first, second):
        mine = scal[0] == 0
        for half in range(2):

            def group(i, j):
                a, b = kept[i, j], got[i, j]
                return jnp.where(mine, a, b) if half == 0 else jnp.where(mine, b, a)

            for j in range(4):
                if ffn:
                    second[0, width * j : width * (j + 1), HALF * half : HALF * (half + 1)] = group(0, j)
                    at = HALF_UP * half + HALF * j
                    first[0, :, at : at + HALF] = group(1, j)
                elif j < 3:
                    at = HALF_QKV * half + HALF * j
                    first[0, :, at : at + HALF] = group(j // 2, j % 2)
                else:
                    second[0, :, HALF * half : HALF * (half + 1)] = group(1, 1)

    sizes = ((width, FF), (4 * width, D)) if ffn else ((width, 3 * D), (width, D))
    return pl.pallas_call(
        kernel,
        in_specs=[SMEM, VMEM, VMEM],
        out_specs=[VMEM] * 2,
        out_shape=[shape((1, *s), F32) for s in sizes],
        cost_estimate=SMALL_COST,
        name="finish_ffn" if ffn else "finish_att",
    )(scal, kept, got)


TILE = 512


def lookup_kernel(count, last, hid, *rest):
    tables, rest = rest[:count], rest[count:]
    if last:
        m_in, l_in, a_in, mean_ref, unit_ref, lse_ref, m_ref, l_ref, acc = rest
    else:
        m_ref, l_ref, acc = rest
    step = pl.program_id(0)

    @pl.when(step == 0)
    def _():
        if last:
            m_ref[...] = m_in[...]
            l_ref[...] = l_in[...]
            acc[...] = a_in[...]
        else:
            m_ref[...] = jnp.full((ROWS, 1), MASKED, F32)
            l_ref[...] = jnp.zeros((ROWS, 1), F32)
            acc[...] = jnp.zeros((ROWS, D), F32)

    scores = [dot_rows(hid[...], table[...]) * D**-0.5 for table in tables]
    top = m_ref[...]
    for s in scores:
        top = jnp.maximum(top, jnp.max(s, axis=-1, keepdims=True))
    fade = jnp.exp(m_ref[...] - top)
    m_ref[...] = top
    total_l = l_ref[...] * fade
    total_a = acc[...] * fade
    for s, table in zip(scores, tables):
        p = jnp.exp(s - top)
        total_l = total_l + jnp.sum(p, axis=-1, keepdims=True)
        high = p.astype(BF16)
        low = (p - high.astype(F32)).astype(BF16)
        gained = dot(jnp.concatenate([high, low]), table[...])
        total_a = total_a + (gained[:ROWS] + gained[ROWS:])
    l_ref[...] = total_l
    acc[...] = total_a
    if last:
        @pl.when(step == pl.num_programs(0) - 1)
        def _():
            totals = l_ref[...]
            mean_code = acc[...] / totals
            mean_ref[...] = mean_code
            unit_ref[...] = mean_code * lax.rsqrt(
                jnp.mean(mean_code * mean_code, axis=-1, keepdims=True) + EPS
            )
            lse_ref[...] = m_ref[...] + jnp.log(totals)


def fixed(s):
    return pl.BlockSpec(s, lambda i, *_: (0,) * len(s))


def lookup(hidden, tables, state=None):
    last = state is not None
    rows = tables[0].shape[0]
    tile = min(TILE, rows)
    col, mat = (ROWS, 1), (ROWS, D)
    if last:
        outs = [mat, mat, col]
        scratch = [pltpu.VMEM(col, F32), pltpu.VMEM(col, F32), pltpu.VMEM(mat, F32)]
    else:
        outs, scratch = [col, col, mat], []
    return pl.pallas_call(
        partial(lookup_kernel, len(tables), last),
        grid=(rows // tile,),
        in_specs=[fixed(mat)]
        + [pl.BlockSpec((tile, D), lambda i: (i, 0))] * len(tables)
        + ([fixed(col), fixed(col), fixed(mat)] if last else []),
        out_specs=[fixed(o) for o in outs],
        out_shape=[shape(o, F32) for o in outs],
        scratch_shapes=scratch,
        compiler_params=pltpu.CompilerParams(vmem_limit_bytes=ROOM),
        cost_estimate=SMALL_COST,
        name=f"lookup_{int(last)}",
    )(hidden, *tables, *(state if last else ()))


WIDE = 1024


def over_table(moves, tables, buffer, fold):
    count = len(tables)
    tile = buffer.shape[0] // count
    steps = tables[0].shape[0] // tile
    wide = min(WIDE, buffer.shape[0])
    sems = [moves.sem() for _ in tables]

    def step(i):
        copies = []
        for n, (table, sem) in enumerate(zip(tables, sems)):
            src = table if steps == 1 else table.at[pl.ds(pl.multiple_of(i * tile, tile), tile), :]
            copies.append(pltpu.make_async_copy(src, buffer.at[pl.ds(tile * n, tile), :], sem))
            copies[-1].start()
        for j in range(buffer.shape[0] // wide):
            for copy in copies[wide * j // tile : wide * (j + 1) // tile]:
                copy.wait()
            fold(slice(wide * j, wide * (j + 1)))

    if steps == 1:
        step(0)
    else:
        lax.fori_loop(0, steps, lambda i, carry: (step(i), carry)[1], 0)


def table_buffer(tables):
    return ((len(tables) * min(TILE, tables[0].shape[0]), D), BF16)


def lookup_back(scal, hidden, code, lse, inner, tables):
    count = len(tables)

    def body(moves, scal, *refs):
        ins, tables, refs = refs[:4], refs[4 : 4 + count], refs[4 + count :]
        out_o, keep_o, send_o, rows_ref, lse, inner, buffer, out, low = refs
        places = (rows_ref.at[pl.ds(0, ROWS), :], rows_ref.at[pl.ds(ROWS, ROWS), :], lse, inner)
        for wait in [moves.load(src, dst) for src, dst in zip(ins, places)]:
            wait()
        out[...] = jnp.zeros((ROWS, D), F32)

        def fold(rows):
            both = dot_rows(rows_ref[...], buffer[rows, :])
            p = jnp.exp(both[:ROWS] * D**-0.5 - lse[...])
            ds = (p * (both[ROWS:] - inner[...])).astype(BF16)
            out[...] += dot(ds, buffer[rows, :])

        over_table(moves, tables, buffer, fold)
        value = out[...] * D**-0.5
        out[...] = value
        moves.store(out, out_o)
        low[...] = value.astype(BF16)
        moves.store(low.at[:, half_of(scal, HALF)], keep_o)
        moves.store(low.at[:, half_of(scal, HALF, False)], send_o)

    part = ((ROWS, HALF), BF16)
    return call(
        body, "lookup_back", scal, [hidden, code, lse, inner, *tables], outputs(MAT, part, part),
        [((2 * ROWS, D), BF16), COL, COL, table_buffer(tables), MAT, LOW],
    )


def swapped(value):
    return lax.ppermute(value, "section", [(0, 1), (1, 0)])


def bit_count():
    size = lax.axis_size("dp")
    count = size.bit_length() - 1
    assert size == 1 << count
    return count


def across(value, step):
    size = lax.axis_size("dp")
    return lax.ppermute(value, "dp", [(i, i ^ step) for i in range(size)])


def along(value, bit):
    return across(value, 1 << bit)


def after(value, *others):
    return lax.optimization_barrier((value, *others))[0]


def total(terms):
    summed = terms[0].astype(F32)
    for term in terms[1:]:
        summed = summed + term.astype(F32)
    return summed


class Share:
    def __init__(self, parts, order):
        self.order = order
        if len(parts) == 2:
            self.terms, self.ready = [parts[0]], parts[1]
        else:
            count = len(order)
            value = parts[0].reshape((-1,) + (2,) * count + (D >> count, HALF))
            axes = [count - bit for bit in order]
            self.terms, self.ready = [value.transpose(axes + [0, count + 1, count + 2])], None

    def split(self, stage):
        if stage == 0 and self.ready is not None:
            return self.ready
        mine = (lax.axis_index("dp") >> self.order[stage]) & 1

        def pick(which):
            return [lax.dynamic_index_in_dim(t, which, 0, keepdims=False) for t in self.terms]

        sent = total(pick(1 - mine)).astype(BF16)
        self.terms = pick(mine)
        return sent

    def send(self, stage, *values):
        self.sent = after(self.split(stage), *values)
        self.got = along(self.sent, self.order[stage])

    def receive(self, *values):
        self.terms.append(after(self.got, *values))


class Group:
    def __init__(self, parts, orders, joint):
        self.shares = [Share(part, order) for part, order in zip(parts, orders)]
        self.joint = joint

    def ready(self):
        return [share.terms[0] for share in self.shares]

    def send(self, stage, *values):
        if stage < self.joint:
            for share in self.shares:
                share.send(stage, *values)
            self.sent = [share.sent for share in self.shares]
        else:
            self.sent = [after(jnp.stack([share.split(stage) for share in self.shares]), *values)]
            self.got = along(self.sent[0], self.shares[0].order[stage])

    def receive(self, stage, *values):
        if stage < self.joint:
            for share in self.shares:
                share.receive(*values)
        else:
            got = after(self.got, *values)
            for i, share in enumerate(self.shares):
                share.terms.append(got[i])

    def result(self):
        sums = jnp.concatenate([total(share.terms) for share in self.shares])
        return sums.reshape((2, -1) + sums.shape[-2:])


def pair_orders():
    far = list(range(2, bit_count()))
    return [0, 1] + far, [1, 0] + far


def pair(parts):
    return Group(parts, pair_orders(), 2)


def far_order():
    return [list(range(2, bit_count())) + [0, 1]]


def per_device(
    patches,
    recon_cot,
    lengths,
    codebook,
    w_qkv,
    w_out,
    w_up,
    w_down,
    norm_gain,
    norm_bias,
    bias_out,
    bias_up,
):
    section = lax.axis_index("section")
    on_first = section == 0
    size = lax.axis_size("dp")
    count = bit_count()
    me = lax.axis_index("dp")
    scal = jnp.stack([section, *((me >> bit) & 1 for bit in range(count))]).astype(jnp.int32)
    own_small = pack_small(norm_gain, norm_bias, bias_out, bias_up)
    small = (lengths, own_small, swapped(own_small))
    weights = [(w[0], swapped(w[0])) for w in (w_qkv, w_out)]

    table = codebook
    for bit in range(count - 1, 2, -1):
        got = after(along(table, bit), small[2], weights[0][1], weights[1][1])
        table = jnp.concatenate([table, got])
    weights += [(w[0], swapped(after(w[0], table))) for w in (w_up, w_down)]
    got = along(table, 2)
    from_table = along(table, 1)
    facts_ea, qkv_e, probs_e = att_forward(0, after(scal, table), patches, small, weights)
    got = after(got, facts_ea)
    from_got = along(got, 0)
    left = jnp.concatenate([table, after(from_table, got)])
    late = [along(left, 0)]
    right = jnp.concatenate([got, after(from_got, left)])
    late.append(along(right, 1))
    pieces = [left, right]
    pieces_other = [swapped(piece) for piece in pieces]
    hidden, facts_ef, resid_e, slope_e = ffn_forward(
        0, after(scal, *pieces), patches, small, facts_ea, weights
    )
    state = lookup(hidden, pieces + pieces_other)
    late = after(late, state[0])
    late_other = [swapped(piece) for piece in late]
    tables = pieces + pieces_other + late + late_other
    mean_code, unit, lse = lookup(hidden, late + late_other, state)
    facts_ea = (facts_ea, swapped(after(facts_ea, *late_other)))
    facts_ef = (facts_ef, swapped(after(facts_ef, *late_other)))
    recon, facts_df, facts_da, qkv_d, probs_d, resid_d, slope_d = block_forward(
        1, after(scal, facts_ea[1], facts_ef[1]), unit, small, weights
    )
    facts_df = (facts_df, swapped(facts_df))
    facts_da = (facts_da, swapped(facts_da))
    recon_first = lax.ppermute(recon, "section", [(0, 1)])
    lse_other = swapped(lse)

    keep, send, d_resid, sums_df = ffn_backward(
        1, scal, recon_cot, slope_d, resid_d, small, weights, True
    )
    first_f = pair(ffn_grads(after(scal, keep), facts_df, (keep, swapped(send)), [recon_cot], count, pair_orders(), True))
    first_f.send(0)
    keep, send, sums_da, code, inner = att_backward(
        1, after(scal, facts_da[1], *first_f.sent), d_resid, qkv_d, probs_d, unit, small, weights, mean_code
    )
    got = swapped(send)
    d_hidden, g_keep, g_send = lookup_back(scal, hidden, code, lse, inner, tables)
    g_got = swapped(g_send)
    first_f.receive(0, d_hidden, recon_first, lse_other)
    first_f.send(1)
    first_a = pair(att_grads(after(scal, *first_f.sent), facts_da, (keep, got), count, pair_orders()))
    first_a.send(0)
    keep, send, d_resid, sums_ef = ffn_backward(
        0, after(scal, g_got, *first_a.sent), d_hidden, slope_e, resid_e, small, weights, False
    )
    got = swapped(send)
    first_f.receive(1, keep)
    first_f.send(2)
    second_f = pair(
        ffn_grads(after(scal, keep, *first_f.sent), facts_ef, (keep, got), (g_keep, g_got), count, pair_orders(), False)
    )
    second_f.send(0)
    first_a.receive(0, *second_f.ready())
    first_a.send(1)
    keep, send, sums, sums_send, grad_x = att_backward(
        0, after(scal, *second_f.sent, *first_a.sent), d_resid, qkv_e, probs_e, patches, small, weights,
        sums_before=(sums_ef, sums_df, sums_da),
    )
    got = swapped(send)
    sums_got = swapped(sums_send)
    first_f.receive(2, sums)
    first_f.send(3)
    second_a = pair(att_grads(after(scal, sums_got, *first_f.sent), facts_ea, (keep, got), count, pair_orders()))
    second_f.receive(0, *second_a.ready())
    second_f.send(1)
    first_a.receive(1, *second_f.sent)
    closed = [share.terms[-1] for share in first_a.shares]
    if count == 4:
        first_f.receive(3, *closed)
        closed = [first_f.shares[0].terms[-1]]
    second_a.send(0, *closed)
    first_a.send(2, *second_a.sent)
    second_f.receive(1, *first_a.sent)
    second_f.send(2)
    sums = sums + after(sums_got, *second_f.sent)
    sums_got = along(sums, 2)
    first_a.receive(2, sums)
    first_a.send(3)
    grad_second = lax.ppermute(after(grad_x, sums), "section", [(1, 0)])
    second_a.receive(0, *first_a.sent)
    second_a.send(1)
    first_a.receive(3, grad_second, *second_a.sent)
    second_f.receive(2, first_a.shares[0].terms[-1])
    second_f.send(3)
    sums = sums + after(sums_got, *second_f.sent)
    sums_got = along(sums, 0)
    second_a.receive(1, sums)
    second_a.send(2)
    sums = sums + after(sums_got, *second_a.sent)
    sums_got = along(sums, 1)
    last = second_a.sent
    if count > 4:
        first_a.send(4)
        waiting = [[first_f, 3], [first_a, 4], [second_f, 3]]
        for step in range(count):
            for entry in waiting:
                group, stage = entry
                if stage < count - (1 if group is second_f else 0):
                    group.receive(stage, *last)
                    if stage + 1 < count:
                        group.send(stage + 1)
                        last = group.sent
                    entry[1] += 1
    ends = jnp.where(
        on_first, jnp.concatenate([grad_x, grad_second]), jnp.concatenate([recon_first, recon])
    )[None]
    lse, lse_other = after([lse, lse_other], *last)
    lse, lse_other = lse[:, 0], lse_other[:, 0]
    codes = jnp.where(on_first, jnp.concatenate([lse, lse_other]), jnp.concatenate([lse_other, lse]))
    sums = sums + after(sums_got, *last)
    sums_got = along(sums, 3)
    for bit in range(4, count):
        sums = sums + sums_got
        sums_got = along(sums, bit)
    for stage in range(2, count - 1):
        second_a.receive(stage, sums, codes)
        second_a.send(stage + 1)
    sums = sums + after(sums_got, *second_a.sent)
    width = D // size
    rows = lax.dynamic_slice_in_dim(sums, me * width, width, axis=1)
    grad_gain = jnp.stack([rows[8], rows[0]])[None]
    grad_nbias = jnp.stack([rows[9], rows[1]])[None]
    grad_bout = jnp.stack([rows[3], rows[2]])[None]
    grad_bup = lax.dynamic_slice_in_dim(sums[4:8].reshape(FF), me * width * 4, width * 4)[None]
    second_f.receive(count - 1, grad_gain, grad_nbias, grad_bout, grad_bup, ends)

    def shared_out(encoder, decoder):
        encoder, decoder = encoder.result(), decoder.result()
        return jnp.where(on_first, encoder, decoder), swapped(jnp.where(on_first, decoder, encoder))

    ffn = shared_out(second_f, first_f)
    grad_up, grad_down = finish(scal, *ffn, True)
    second_a.receive(count - 1, grad_up)
    grad_qkv, grad_out = finish(scal, *shared_out(second_a, first_a), False)
    return (ends, codes, grad_qkv, grad_out, grad_up, grad_down, grad_gain, grad_nbias, grad_bout, grad_bup)


def solution(mesh):
    placed = (
        P("dp", None),
        P("dp", None),
        P("dp", None),
        P(("dp", "section"), None),
        P("section", None, None),
        P("section", None, None),
        P("section", None, None),
        P("section", None, None),
        P("section", None, None),
        P("section", None, None),
        P("section", None, None),
        P("section", None),
    )
    return jax.shard_map(
        per_device,
        mesh=mesh,
        in_specs=placed,
        out_specs=(
            P("section", "dp", None),
            P("dp"),
            P("section", "dp", None),
            P("section", "dp", None),
            P("section", "dp", None),
            P("section", "dp", None),
            P("section", None, "dp"),
            P("section", None, "dp"),
            P("section", None, "dp"),
            P("section", "dp"),
        ),
        check_vma=False,
    )
```
